32 devices in a mesh: dp: 16 (over z, y, core), tensor: 2 (over x).
Axes of the slice: x: 2, y: 2, z: 4, core: 2. Of those that a mesh axis runs over, the one named last changes fastest.
Arguments:
- inputs: bfloat16 [16, 512, 1024], P('dp', 'tensor'), may hold values from -6 to 6
- segments: int32 [16, 512], P('dp'), may hold values from 0 to 2, as said below
- w_query: bfloat16 [1024, 1024], P('dp', 'tensor'), may hold values from -0.1875 to 0.1875
- w_key: bfloat16 [1024, 1024], P('dp', 'tensor'), may hold values from -0.1875 to 0.1875
- w_value: bfloat16 [1024, 1024], P('dp', 'tensor'), may hold values from -0.1875 to 0.1875
- w_output: bfloat16 [1024, 1024], P('tensor', 'dp'), may hold values from -3 to 3
- w_expand: bfloat16 [1024, 4096], P('dp', 'tensor'), may hold values from -0.1875 to 0.1875
- w_reduce: bfloat16 [4096, 1024], P('tensor', 'dp'), may hold values from -0.09375 to 0.09375
- query_bias_vector: float32 [1024], P('tensor'), may hold values from -3 to 3
- b_value: float32 [1024], P('tensor'), may hold values from -3 to 3
- b_output: float32 [1024], replicated, may hold values from -3 to 3
- b_expand: float32 [4096], P('tensor'), may hold values from -3 to 3
- b_reduce: float32 [1024], replicated, may hold values from -3 to 3
- gain_first: float32 [1024], replicated, may hold values from 0.5 to 1.5
- shift_first: float32 [1024], replicated, may hold values from -3 to 3
- gain_second: float32 [1024], replicated, may hold values from 0.5 to 1.5
- shift_second: float32 [1024], replicated, may hold values from -3 to 3
- cotangent: bfloat16 [16, 512, 1024], P('dp', 'tensor'), may hold values from -6 to 6
Outputs:
- result: bfloat16 [16, 512, 1024], P('dp', 'tensor')
- grad_inputs: float32 [16, 512, 1024], P('dp', 'tensor')
- grad_w_query: float32 [1024, 1024], P('dp', 'tensor')
- key_weight_gradient: float32 [1024, 1024], P('dp', 'tensor')
- grad_w_value: float32 [1024, 1024], P('dp', 'tensor')
- grad_w_output: float32 [1024, 1024], P('tensor', 'dp')
- grad_w_expand: float32 [1024, 4096], P('dp', 'tensor')
- grad_w_reduce: float32 [4096, 1024], P('tensor', 'dp')
- grad_b_query: float32 [1024], P('tensor')
- grad_b_value: float32 [1024], P('tensor')
- grad_b_output: float32 [1024], replicated
- grad_b_expand: float32 [4096], P('tensor')
- grad_b_reduce: float32 [1024], replicated
- grad_gain_first: float32 [1024], replicated
- grad_shift_first: float32 [1024], replicated
- grad_gain_second: float32 [1024], replicated
- grad_shift_second: float32 [1024], replicated
The draws below stay inside these ranges and needn't reach their ends.
Inputs may be any that keep to these rules, and one draw needn't show every extreme that they name: `segments`: segment numbers never fall along a sequence; equal numbers mark tokens of one document. Of the 1 sequence of each index of dp, one holds a single document.
All inputs are finite; a program needn't handle non-finite values.
Results may differ from the reference program's by a relative error of at most 0.018.
Values may be sent and summed in bfloat16 or wider, within the bound.
No kernel may reach another device: no remote copies, remote signals or barrier semaphores. Data moves between devices by JAX's collectives and lax.ppermute only.
A program may use at most 128 MiB of HBM per device.

```python
import math
import jax
import jax.numpy as jnp
from jax import lax

D = 1024
H = 16
HD = 64
FF = 4096
LEN = 512
SEQS = 1
NSEQ = 16


def draw_segments(key, part):
    key = jax.random.fold_in(key, 11)
    key_open, key_mid, key_pick = jax.random.split(key, 3)
    opening = jax.random.randint(key_open, (NSEQ, 1), 1, LEN // 4 + 1)
    middle = jax.random.randint(key_mid, (NSEQ, 1), LEN * 25 // 64, LEN * 5 // 8)
    column = jnp.arange(LEN)[None, :]
    labels = (column >= opening).astype(jnp.int32) + (column >= opening + middle).astype(jnp.int32)
    chosen = jax.random.randint(key_pick, (NSEQ // SEQS, 1), 0, SEQS)
    single = (jnp.arange(NSEQ).reshape(NSEQ // SEQS, SEQS) == chosen).reshape(NSEQ, 1)
    return jnp.where(single, 0, labels).astype(jnp.int32)


def spiked(array, stream_key, source, target, blocks, factor):
    owner, partner = [(jnp.arange(array.shape[axis_at]) // (array.shape[axis_at] // blocks)).reshape([-1 if axis == axis_at else 1 for axis in range(array.ndim)]) for axis_at in (source, target)]
    chosen = jax.random.permutation(stream_key, blocks)[partner]
    strong = (owner == chosen) | (owner == (partner + blocks // 2) % blocks)
    return jnp.where(strong, factor * array, array)


def shard_levels(own_key, extent, cuts, least, top_value):
    loudness, own = 1.0, jax.random.fold_in(own_key, 6)
    for position, shards_of in cuts:
        steps = jnp.exp(jax.random.uniform(jax.random.fold_in(own, position), (shards_of,), jnp.float32, least / len(cuts), top_value / len(cuts)))
        loudness = loudness * jnp.repeat(steps, extent[position] // shards_of).reshape([-1 if axis == position else 1 for axis in range(len(extent))])
    return loudness


def noise(own_key, extent, deviation, reach, cuts=(), kind=jnp.bfloat16):
    drawn = jax.random.normal(own_key, extent, jnp.float32) * deviation
    if len(cuts) > 0:
        drawn = shard_levels(own_key, extent, cuts, -0.22, 0.18) * drawn
    return jnp.clip(drawn, min=-reach, max=reach).astype(kind)


def gaussian_with(rng, dims, scale, most, cuts, heavy, kind=jnp.bfloat16):
    entries = scale * jax.random.normal(rng, dims, jnp.float32)
    if cuts:
        entries = entries * shard_levels(rng, dims, cuts, -0.22, 0.18)
    return jnp.clip(spiked(entries, jax.random.fold_in(rng, 3), *heavy), -most, most).astype(kind)


def setup_inputs(seed: int = 0) -> dict:
    splits = jax.random.split(jax.random.key(seed), 19)
    inputs = noise(splits[0], (NSEQ, LEN, D), 1.0, 6.0, ((0, 16), (1, 2)))
    segments = draw_segments(jax.random.fold_in(splits[18], 71), 0)
    w_query = noise(splits[2], (D, D), D ** -0.5, 0.1875, ((0, 16), (1, 2)))
    w_key = noise(splits[3], (D, D), D ** -0.5, 0.1875, ((0, 16), (1, 2)))
    w_value = noise(splits[4], (D, D), D ** -0.5, 0.1875, ((0, 16), (1, 2)))
    w_output = noise(splits[5], (D, D), 4 ** -0.5, 3.0, ((0, 2), (1, 16)))
    w_expand = noise(splits[6], (D, FF), D ** -0.5, 0.1875, ((0, 16), (1, 2)))
    w_reduce = noise(splits[7], (FF, D), FF ** -0.5, 0.09375, ((0, 2), (1, 16)))
    query_bias_vector = noise(splits[8], (D,), 0.5, 3.0, ((0, 2),), jnp.float32)
    b_value = noise(splits[9], (D,), 0.5, 3.0, ((0, 2),), jnp.float32)
    b_output = noise(splits[10], (D,), 0.5, 3.0, (), jnp.float32)
    b_expand = noise(splits[11], (FF,), 0.5, 3.0, ((0, 2),), jnp.float32)
    b_reduce = noise(splits[12], (D,), 0.5, 3.0, (), jnp.float32)
    gain_first = jnp.clip(1.0 + 0.1 * jax.random.normal(splits[13], (D,), jnp.float32), 0.5, 1.5)
    shift_first = noise(splits[14], (D,), 0.5, 3.0, (), jnp.float32)
    gain_second = jnp.clip(1.0 + 0.1 * jax.random.normal(splits[15], (D,), jnp.float32), 0.5, 1.5)
    shift_second = noise(splits[16], (D,), 0.5, 3.0, (), jnp.float32)
    cotangent = gaussian_with(splits[17], (NSEQ, LEN, D), 1.0, 6.0, ((0, 16), (1, 2)), (0, 2, 16, 2.0))
    return {"inputs": inputs, "segments": segments, "w_query": w_query, "w_key": w_key, "w_value": w_value, "w_output": w_output, "w_expand": w_expand, "w_reduce": w_reduce, "query_bias_vector": query_bias_vector, "b_value": b_value, "b_output": b_output, "b_expand": b_expand, "b_reduce": b_reduce, "gain_first": gain_first, "shift_first": shift_first, "gain_second": gain_second, "shift_second": shift_second, "cotangent": cotangent}


@jax.custom_vjp
def low(v):
    return lax.optimization_barrier(v.astype(jnp.bfloat16)).astype(jnp.float32)

@jax.custom_vjp
def low_back(v):
    return v

def low_keep(v):
    return (low(v), None)

def low_pass(kept, grad):
    return (grad,)

def back_keep(v):
    return (v, None)

def back_low(kept, grad):
    return (low(grad),)
low.defvjp(low_keep, low_pass)
low_back.defvjp(back_keep, back_low)
norm_eps = 1e-05
masked_score = -1e+30
highest = lax.Precision.HIGHEST

def layer_norm(weight_matrix, gain_vec, shift_vec):
    centre = weight_matrix - lax.optimization_barrier(jnp.mean(weight_matrix, axis=-1, keepdims=True))
    spread = lax.optimization_barrier(jnp.mean(centre * centre, axis=-1, keepdims=True))
    return centre * lax.rsqrt(spread + norm_eps) * gain_vec + shift_vec

def linear(source_tensor, weight_matrix):
    return jnp.einsum('...i,ij->...j', source_tensor, weight_matrix, precision=highest)

def attend(pieces):
    query_blk, key_blk, value_blk, labels = pieces
    scores = jnp.einsum('qhd,khd->hqk', query_blk, key_blk, precision=highest) * HD ** (-0.5)
    scores = low_back(scores)
    same_doc = labels[:, None] == labels[None, :]
    scores = jnp.where(same_doc[None], scores, masked_score)
    softmax_out = low(jax.nn.softmax(scores, axis=-1))
    return jnp.einsum('hqk,khd->qhd', softmax_out, value_blk, precision=highest)

def layer(tokens, labels, w_query, w_key, w_value, w_output, w_expand, w_reduce, query_bias_vector, b_value, b_output, b_expand, b_reduce, gain_first, shift_first, gain_second, shift_second):
    seq_count, seq_len, width = tokens.shape
    divided_shape = (seq_count, seq_len, H, HD)
    query_all = low_back(low(linear(tokens, w_query) + query_bias_vector)).reshape(divided_shape)
    key_rows_gathered = low_back(low(linear(tokens, w_key))).reshape(divided_shape)
    value_all = low_back(low(linear(tokens, w_value) + b_value)).reshape(divided_shape)
    context = lax.map(jax.checkpoint(attend), (query_all, key_rows_gathered, value_all, labels))
    context = low_back(low(context.reshape(seq_count, seq_len, width)))
    attended = tokens + low_back(linear(context, w_output)) + b_output
    normed = layer_norm(attended, gain_first, shift_first)
    expanded = low_back(linear(low(normed), w_expand) + b_expand)
    activated = low(jax.nn.gelu(expanded, approximate=False))
    mixed = normed + low_back(linear(activated, w_reduce)) + b_reduce
    return layer_norm(mixed, gain_second, shift_second)

def reference(inputs, segments, w_query, w_key, w_value, w_output, w_expand, w_reduce, query_bias_vector, b_value, b_output, b_expand, b_reduce, gain_first, shift_first, gain_second, shift_second, cotangent):
    params = tuple((element.astype(jnp.float32) for element in (w_query, w_key, w_value, w_output, w_expand, w_reduce, query_bias_vector, b_value, b_output, b_expand, b_reduce, gain_first, shift_first, gain_second, shift_second)))
    batch_size = math.gcd(NSEQ, max(1, 4096 // LEN))
    blocks = NSEQ // batch_size
    tokens_in = inputs.astype(jnp.float32).reshape(blocks, batch_size, LEN, D)
    labels_in = segments.reshape(blocks, batch_size, LEN)
    grads_in = cotangent.astype(jnp.float32).reshape(blocks, batch_size, LEN, D)

    def scan_step(totals, block_data):
        tokens, labels, grad_out = block_data

        def forward(tokens_f, *weights):
            return layer(tokens_f, labels, *weights)
        output, pullback = jax.vjp(forward, tokens, *params)
        gradients = pullback(grad_out)
        totals = tuple((total + extra for total, extra in zip(totals, gradients[1:])))
        return (totals, (output.astype(jnp.bfloat16), gradients[0]))
    zeros_init = tuple((jnp.zeros_like(element) for element in params))
    totals, (outputs, grad_tokens) = lax.scan(scan_step, zeros_init, (tokens_in, labels_in, grads_in))
    return (outputs.reshape(NSEQ, LEN, D), grad_tokens.reshape(NSEQ, LEN, D), totals[0], totals[1], totals[2], totals[3], totals[4], totals[5], totals[6], totals[7], totals[8], totals[9], totals[10], totals[11], totals[12], totals[13], totals[14])
```

```python
import functools

import jax
import jax.numpy as jnp
from jax import lax
from jax.experimental import pallas as pl
from jax.experimental.pallas import tpu as pltpu
from jax.sharding import PartitionSpec as P

HD = 64
NORM_EPS = 1e-05
MASKED = -1e30
BF = jnp.bfloat16
F32 = jnp.float32


def dot(a, b):
    return lax.dot_general(a, b, (((1,), (0,)), ((), ())), preferred_element_type=F32)


def dot_nt(a, b):
    return lax.dot_general(a, b, (((1,), (1,)), ((), ())), preferred_element_type=F32)


def dot_tn(a, b):
    return lax.dot_general(a, b, (((0,), (0,)), ((), ())), preferred_element_type=F32)


def ln_forward(values, gain, shift):
    centre = values - jnp.mean(values, axis=-1, keepdims=True)
    scale = lax.rsqrt(jnp.mean(centre * centre, axis=-1, keepdims=True) + NORM_EPS)
    unit = centre * scale
    return unit * gain + shift, unit, scale


def ln_backward(grad, unit, scale, gain):
    grad_unit = grad * gain
    along = jnp.mean(grad_unit * unit, axis=-1, keepdims=True)
    return scale * (grad_unit - jnp.mean(grad_unit, axis=-1, keepdims=True) - unit * along)


def local_scores(query, key, labels):
    same = labels[:, None] == labels[None, :]
    scores = jnp.einsum("qhd,khd->hqk", query, key, preferred_element_type=F32) * HD ** (-0.5)
    return jnp.where(same[None], scores, MASKED)


def attend_forward(pieces):
    query, key, value, labels = pieces
    scores = local_scores(query, key, labels)
    top = jnp.max(scores, axis=-1, keepdims=True)
    weights = jnp.exp(scores - top)
    totals = jnp.sum(weights, axis=-1, keepdims=True)
    probs = (weights / totals).astype(BF)
    context = jnp.einsum("hqk,khd->qhd", probs, value, preferred_element_type=F32)
    return context.astype(BF), (top + jnp.log(totals))[..., 0]


def attend_backward(pieces):
    query, key, value, labels, log_total, grad_ctx = pieces
    scores = local_scores(query, key, labels)
    probs = jnp.exp(scores - log_total[..., None])
    grad_probs = jnp.einsum("qhd,khd->hqk", grad_ctx, value, preferred_element_type=F32)
    grad_value = jnp.einsum(
        "hqk,qhd->khd", probs.astype(BF), grad_ctx, preferred_element_type=F32
    )
    inner = jnp.sum(probs * grad_probs, axis=-1, keepdims=True)
    grad_scores = (probs * (grad_probs - inner)).astype(BF)
    grad_query = jnp.einsum("hqk,khd->qhd", grad_scores, key, preferred_element_type=F32)
    grad_key = jnp.einsum("hqk,qhd->khd", grad_scores, query, preferred_element_type=F32)
    factor = HD ** (-0.5)
    return (
        (grad_query * factor).astype(BF),
        (grad_key * factor).astype(BF),
        grad_value.astype(BF),
    )


def assemble_kernel(count, cols, places, *refs):
    out = refs[count]
    for i in range(count):
        rows, wide = refs[i].shape
        row = pl.multiple_of(places[i], 16)
        out[pl.ds(row, rows), cols[i] : cols[i] + wide] = refs[i][...]


def assemble(pieces, rows, cols):
    count = len(pieces)
    places = jnp.stack([jnp.asarray(piece[1], jnp.int32) for piece in pieces])
    return pl.pallas_call(
        functools.partial(assemble_kernel, count, [piece[2] for piece in pieces]),
        out_shape=jax.ShapeDtypeStruct((rows, cols), pieces[0][0].dtype),
        in_specs=[pl.BlockSpec(memory_space=pltpu.SMEM)]
        + [pl.BlockSpec(memory_space=pltpu.VMEM)] * count,
        out_specs=pl.BlockSpec(memory_space=pltpu.VMEM),
        compiler_params=pltpu.CompilerParams(vmem_limit_bytes=40 << 20),
        cost_estimate=pl.CostEstimate(
            flops=0, bytes_accessed=4 * rows * cols, transcendentals=0
        ),
    )(places, *[piece[0] for piece in pieces])


class Links:
    def __init__(self):
        self.dp = lax.axis_size("dp")
        self.tensor = lax.axis_size("tensor")
        self.chips = self.dp // 2
        self.half_way = self.chips // 2
        self.order = list(range(0, self.chips, 2)) + list(range(1, self.chips, 2))[::-1]
        place = [0] * self.chips
        for i, chip in enumerate(self.order):
            place[chip] = i
        me = lax.axis_index("dp")
        self.core = me % 2
        self.ring_place = jnp.asarray(place, jnp.int32)[me // 2]
        self.order_array = jnp.asarray(self.order, jnp.int32)

    def chip_at(self, distance):
        return self.order_array[(self.ring_place + distance + self.chips) % self.chips]

    def swap_core(self, array):
        return lax.ppermute(array, "dp", [(i, i ^ 1) for i in range(self.dp)])

    def swap_dp(self, array, bit):
        return lax.ppermute(array, "dp", [(i, i ^ bit) for i in range(self.dp)])

    def swap_tensor(self, array, bit):
        return lax.ppermute(array, "tensor", [(i, i ^ bit) for i in range(self.tensor)])

    def along_ring(self, array, step):
        pairs = [
            (2 * self.order[i] + c, 2 * self.order[(i + step) % self.chips] + c)
            for i in range(self.chips)
            for c in range(2)
        ]
        return lax.ppermute(array, "dp", pairs)

    def bits(self, size):
        return [1 << b for b in range((size - 1).bit_length())]

    def gather_blocks(self, block):
        blocks = [block]
        for bit in self.bits(self.tensor):
            blocks = blocks + [self.swap_tensor(b, bit) for b in blocks]
        return blocks

    def sum_blocks(self, blocks):
        for bit in self.bits(self.tensor):
            low = [b.astype(BF) for b in blocks]
            got = [self.swap_tensor(low[j ^ bit], bit) for j in range(len(low))]
            blocks = [a.astype(F32) + b.astype(F32) for a, b in zip(low, got)]
        return blocks

    def scatter_blocks(self, blocks):
        for bit in self.bits(self.tensor)[::-1]:
            got = [self.swap_tensor(blocks[j + bit].astype(BF), bit) for j in range(bit)]
            blocks = [blocks[j].astype(F32) + got[j].astype(F32) for j in range(bit)]
        return blocks[0]

    def sum_small(self, vector, axis):
        rows = vector.reshape(-1, 128)
        swap, size = (
            (self.swap_tensor, self.tensor) if axis == "tensor" else (self.swap_dp, self.dp)
        )
        for bit in self.bits(size):
            rows = rows + swap(rows, bit)
        return rows.reshape(vector.shape)

    def gather_weights(self, shard):
        rows, cols = shard.shape
        half = cols // 256 * 128
        arrived = [(shard, 0, 0)]
        up, down = shard, shard
        for step in range(1, self.half_way):
            up, down = self.along_ring(up, 1), self.along_ring(down, -1)
            arrived += [(up, -step, 0), (down, step, 0)]
        up = self.along_ring(up[:, :half], 1)
        down = self.along_ring(down[:, half:], -1)
        arrived += [(up, -self.half_way, 0), (down, self.half_way, half)]
        pieces = []
        for block, distance, col in arrived:
            row = 2 * rows * self.chip_at(distance)
            pieces.append((block, row + rows * self.core, col))
            pieces.append((self.swap_core(block), row + rows * (1 - self.core), col))
        return assemble(pieces, rows * self.dp, cols)

    def scatter_grads(self, grad):
        block_rows = grad.shape[0] // self.chips
        half = grad.shape[1] // 2

        def block(distance):
            return lax.dynamic_slice_in_dim(
                grad, block_rows * self.chip_at(distance), block_rows, 0
            )

        far = block(self.half_way)
        up = self.along_ring(far[:, :half], 1)
        down = self.along_ring(far[:, half:], -1)
        for step in range(self.half_way - 1, 0, -1):
            ahead, behind = block(step), block(-step)
            if step == self.half_way - 1:
                ahead = jnp.concatenate([add(ahead[:, :half], up), ahead[:, half:]], 1)
                behind = jnp.concatenate([behind[:, :half], add(behind[:, half:], down)], 1)
            else:
                ahead, behind = add(ahead, up), add(behind, down)
            up = self.along_ring(ahead, 1)
            down = self.along_ring(behind, -1)
        return block(0).astype(F32) + up.astype(F32) + down.astype(F32)

    def swap_halves(self, total):
        rows = total.shape[0] // 2
        mine = lax.dynamic_slice_in_dim(total, rows * self.core, rows, 0)
        other = lax.dynamic_slice_in_dim(total, rows * (1 - self.core), rows, 0)
        got = self.swap_core(other.astype(BF)).astype(F32)
        return jnp.where(
            self.core == 0,
            jnp.concatenate([mine, got], 1),
            jnp.concatenate([got, mine], 1),
        )

    def pair_grad(self, wide, narrow):
        half = narrow.shape[1] // 2
        keep = lax.dynamic_slice_in_dim(narrow, half * self.core, half, 1)
        give = lax.dynamic_slice_in_dim(narrow, half * (1 - self.core), half, 1)
        total = dot_tn(wide, keep) + dot_tn(self.swap_core(wide), self.swap_core(give))
        return total.astype(BF)


def add(a, b):
    return (a.astype(F32) + b.astype(F32)).astype(BF)


def gelu_pair(u):
    cdf = 0.5 * (1.0 + lax.erf(u * (0.5**0.5)))
    slope = cdf + u * jnp.exp(-0.5 * u * u) * 0.3989422804014327
    return u * cdf, slope


def shards(
    inputs,
    segments,
    w_query,
    w_key,
    w_value,
    w_output,
    w_expand,
    w_reduce,
    query_bias_vector,
    b_value,
    b_output,
    b_expand,
    b_reduce,
    gain_first,
    shift_first,
    gain_second,
    shift_second,
    cotangent,
):
    links = Links()
    parts = links.tensor
    rank = lax.axis_index("tensor")
    seqs, span, width = inputs.shape
    local = w_query.shape[1]
    hidden = w_expand.shape[1]

    full_qkv = links.gather_weights(jnp.concatenate([w_query, w_key, w_value], 1))
    full_out_expand = links.gather_weights(jnp.concatenate([w_output.T, w_expand], 1))
    full_out, full_expand = full_out_expand[:, :local], full_out_expand[:, local:]
    full_reduce = links.gather_weights(w_reduce.T)

    def flat(block):
        return block.reshape(seqs * span, block.shape[-1])

    def joined(blocks):
        return jnp.concatenate(
            [b.reshape(seqs, span, b.shape[-1]) for b in blocks], axis=1
        )

    def split(array):
        return [flat(array[:, j * span : (j + 1) * span]) for j in range(parts)]

    token_blocks = [flat(b) for b in links.gather_blocks(inputs)]
    cotangent_blocks = [flat(b) for b in links.gather_blocks(cotangent)]
    labels = jnp.concatenate(
        [
            lax.dynamic_slice_in_dim(segments, span * (rank ^ j), span, 1)
            for j in range(parts)
        ],
        axis=1,
    )
    tokens = joined(token_blocks).reshape(seqs * span * parts, width)

    qkv_bias = jnp.concatenate([query_bias_vector, jnp.zeros_like(b_value), b_value])
    qkv = (dot(tokens, full_qkv) + qkv_bias).astype(BF)
    heads = (seqs, span * parts, local // HD, HD)
    query, key, value = (
        qkv[:, i * local : (i + 1) * local].reshape(heads) for i in range(3)
    )
    context, log_total = lax.map(attend_forward, (query, key, value, labels))
    context = context.reshape(seqs, span * parts, local)

    sums = links.sum_blocks([dot_nt(c, full_out) for c in split(context)])
    normed, unit_first, scale_first, normed_low, activated, slopes, partial = (
        [], [], [], [], [], [], [],
    )
    for tok, s in zip(token_blocks, sums):
        out, unit, scale = ln_forward(
            tok.astype(F32) + s + b_output, gain_first, shift_first
        )
        normed.append(out)
        unit_first.append(unit)
        scale_first.append(scale)
        low = out.astype(BF)
        normed_low.append(low)
        act, slope = gelu_pair(dot(low, full_expand) + b_expand)
        activated.append(act.astype(BF))
        slopes.append(slope.astype(BF))
        partial.append(dot_nt(activated[-1], full_reduce))

    sums = links.sum_blocks(partial)
    result = None
    grad_mixed, reduce_in, expand_low, partial, small = [], [], [], [], {}
    for j in range(parts):
        out, unit, scale = ln_forward(
            normed[j] + sums[j] + b_reduce, gain_second, shift_second
        )
        cot = cotangent_blocks[j].astype(F32)
        grad = ln_backward(cot, unit, scale, gain_second)
        if j == 0:
            result = out.astype(BF).reshape(seqs, span, width)
            small["gain_second"] = jnp.sum(cot * unit, axis=0)
            small["shift_second"] = jnp.sum(cot, axis=0)
            small["b_reduce"] = jnp.sum(grad, axis=0)
        grad_mixed.append(grad)
        reduce_in.append(grad.astype(BF))
        expand_low.append((dot(reduce_in[j], full_reduce) * slopes[j].astype(F32)).astype(BF))
        partial.append(dot_nt(expand_low[j], full_expand))

    sums = links.sum_blocks(partial)
    grad_attended, attn_low, grad_context = [], [], []
    for j in range(parts):
        grad_normed = grad_mixed[j] + sums[j]
        grad = ln_backward(grad_normed, unit_first[j], scale_first[j], gain_first)
        if j == 0:
            small["gain_first"] = jnp.sum(grad_normed * unit_first[0], axis=0)
            small["shift_first"] = jnp.sum(grad_normed, axis=0)
            small["b_output"] = jnp.sum(grad, axis=0)
        grad_attended.append(grad)
        attn_low.append(grad.astype(BF))
        grad_context.append(dot(attn_low[j], full_out).astype(BF))

    half_hidden, half_local = hidden // 2, local // 2
    grad_ffn = links.scatter_grads(
        jnp.concatenate(
            [
                links.pair_grad(jnp.concatenate(reduce_in), jnp.concatenate(activated)),
                links.pair_grad(jnp.concatenate(normed_low), jnp.concatenate(expand_low)),
            ],
            axis=1,
        )
    )
    grad_reduce = links.swap_halves(grad_ffn[:, :half_hidden])
    grad_expand = links.swap_halves(grad_ffn[:, half_hidden:])
    grad_b_expand = sum(jnp.sum(e.astype(F32), axis=0) for e in expand_low)

    grad_query, grad_key, grad_value = lax.map(
        attend_backward,
        (query, key, value, labels, log_total, joined(grad_context).reshape(heads)),
    )
    flat_shape = (seqs * span * parts, local)
    grad_qkv = jnp.concatenate(
        [g.reshape(flat_shape) for g in (grad_query, grad_key, grad_value)], axis=1
    )
    grad_attn = links.scatter_grads(
        jnp.concatenate(
            [
                links.pair_grad(tokens, grad_qkv),
                links.pair_grad(jnp.concatenate(attn_low), jnp.concatenate(split(context))),
            ],
            axis=1,
        )
    )
    grad_qkv_weights = links.swap_halves(grad_attn[:, : 3 * half_local])
    grad_output = links.swap_halves(grad_attn[:, 3 * half_local :])
    inputs_back = dot_nt(grad_qkv, full_qkv).reshape(seqs, span * parts, width)
    grad_inputs = grad_attended[0] + links.scatter_blocks(split(inputs_back))
    bias_sums = jnp.sum(grad_qkv.astype(F32), axis=0)

    names = ("b_output", "b_reduce", "gain_first", "shift_first", "gain_second", "shift_second")
    early = links.sum_small(jnp.stack([small[k] for k in names]), "tensor")
    late = links.sum_small(
        jnp.concatenate([early.reshape(-1), grad_b_expand, bias_sums]), "dp"
    )
    early = late[: 6 * width].reshape(6, width)
    middle = late[6 * width : 6 * width + hidden]
    late = late[6 * width + hidden :]
    return (
        result,
        grad_inputs.reshape(seqs, span, width),
        grad_qkv_weights[:, :local],
        grad_qkv_weights[:, local : 2 * local],
        grad_qkv_weights[:, 2 * local :],
        grad_output.T,
        grad_expand,
        grad_reduce.T,
        late[:local],
        late[2 * local :],
        early[0],
        middle,
        early[1],
        early[2],
        early[3],
        early[4],
        early[5],
    )


def solution(mesh):
    return jax.shard_map(
        shards,
        mesh=mesh,
        in_specs=(
            P("dp", "tensor", None),
            P("dp", None),
            P("dp", "tensor"),
            P("dp", "tensor"),
            P("dp", "tensor"),
            P("tensor", "dp"),
            P("dp", "tensor"),
            P("tensor", "dp"),
            P("tensor"),
            P("tensor"),
            P(),
            P("tensor"),
            P(),
            P(),
            P(),
            P(),
            P(),
            P("dp", "tensor", None),
        ),
        out_specs=(
            P("dp", "tensor", None),
            P("dp", "tensor", None),
            P("dp", "tensor"),
            P("dp", "tensor"),
            P("dp", "tensor"),
            P("tensor", "dp"),
            P("dp", "tensor"),
            P("tensor", "dp"),
            P("tensor"),
            P("tensor"),
            P(),
            P("tensor"),
            P(),
            P(),
            P(),
            P(),
            P(),
        ),
        check_vma=False,
    )
```

```python
import functools

import jax
import jax.numpy as jnp
from jax import lax
from jax.experimental import pallas as pl
from jax.experimental.pallas import tpu as pltpu
from jax.sharding import PartitionSpec as P

HD = 64
NORM_EPS = 1e-05
MASKED = -1e30
BF = jnp.bfloat16
F32 = jnp.float32
PARAMS = pltpu.CompilerParams(vmem_limit_bytes=60 << 20)
VMEM = pl.BlockSpec(memory_space=pltpu.VMEM)
SMEM = pl.BlockSpec(memory_space=pltpu.SMEM)
ANY = pl.BlockSpec(memory_space=pltpu.HBM)


def dot(a, b):
    return lax.dot_general(a, b, (((1,), (0,)), ((), ())), preferred_element_type=F32)


def dot_nt(a, b):
    return lax.dot_general(a, b, (((1,), (1,)), ((), ())), preferred_element_type=F32)


def dot_tn(a, b):
    return lax.dot_general(a, b, (((0,), (0,)), ((), ())), preferred_element_type=F32)


def cost(flops, nbytes):
    return pl.CostEstimate(flops=flops // 1024, bytes_accessed=nbytes // 1024, transcendentals=0)


def lane_half(array, head):
    lanes = lax.broadcasted_iota(jnp.int32, array.shape, 1)
    return jnp.where((lanes < HD) == (head == 0), array, jnp.zeros_like(array))


def column_of(row):
    return jnp.broadcast_to(row, (128, row.shape[1])).T[:, :1]


def attend_forward_kernel(parts, qkv_ref, row_ref, out_w_ref, *refs):
    ctx_ref, lse_ref, part_refs, scratch = refs[0], refs[1], refs[2 : 2 + parts], refs[-1]
    query, key, value = (qkv_ref[:, i * 128 : (i + 1) * 128] for i in range(3))
    same = column_of(row_ref[0]) == row_ref[0]
    query = query * jnp.asarray(HD**-0.5, BF)
    value_t = value.T
    out = []
    for head in range(2):
        scores = dot_nt(key, lane_half(query, head))
        scores = jnp.where(same, scores, MASKED)
        top = jnp.max(scores, axis=0, keepdims=True)
        weights = jnp.exp(scores - top)
        total = jnp.sum(weights, axis=0, keepdims=True)
        probs = (weights * (1.0 / total)).astype(BF)
        lse_ref[0, head : head + 1, :] = top + jnp.log(total)
        out.append(dot(value_t[head * HD : (head + 1) * HD], probs))
    context = jnp.concatenate(out, axis=0).T.astype(BF)
    ctx_ref[...] = context
    pair, pairs = pl.program_id(1), pl.num_programs(1)
    scratch[pair] = context

    @pl.when(pair == pairs - 1)
    def _():
        span = part_refs[0].shape[0]
        whole = jnp.concatenate([scratch[i] for i in range(scratch.shape[0])], axis=1)
        for j, part_ref in enumerate(part_refs):
            part_ref[...] = dot_nt(whole[j * span : (j + 1) * span], out_w_ref[...]).astype(BF)


def attend_forward(qkv, labels, full_attn, parts):
    seqs, length = labels.shape
    pairs = qkv.shape[1] // 384
    local, width, span = 128 * pairs, full_attn.shape[0], length // parts
    out = pl.pallas_call(
        functools.partial(attend_forward_kernel, parts),
        grid=(seqs, pairs),
        in_specs=[
            pl.BlockSpec((length, 384), lambda s, p: (s, p)),
            pl.BlockSpec((1, 1, length), lambda s, p: (s, 0, 0)),
            pl.BlockSpec((width, local), lambda s, p: (0, 3)),
        ],
        out_specs=[
            pl.BlockSpec((length, 128), lambda s, p: (s, p)),
            pl.BlockSpec((1, 2, length), lambda s, p: (s * pairs + p, 0, 0)),
        ]
        + [pl.BlockSpec((span, width), lambda s, p: (s, 0))] * parts,
        out_shape=[
            jax.ShapeDtypeStruct((seqs * length, local), BF),
            jax.ShapeDtypeStruct((seqs * pairs, 2, length), F32),
        ]
        + [jax.ShapeDtypeStruct((seqs * span, width), BF)] * parts,
        scratch_shapes=[pltpu.VMEM((pairs, length, 128), BF)],
        compiler_params=PARAMS,
        cost_estimate=cost(seqs * pairs * 24 * 128 * length * length, 8 << 20),
    )(qkv, labels[:, None, :], full_attn)
    return out[0], out[1], out[2:]


def attend_backward_kernel(qkv_ref, row_ref, lse_ref, *refs):
    out_ref, sum_ref = refs[-2:]
    query, key, value = (qkv_ref[:, i * 128 : (i + 1) * 128] for i in range(3))
    grad_ctx = jnp.concatenate([ref[...] for ref in refs[:-2]], axis=0)
    same = column_of(row_ref[0]) == row_ref[0]
    small_query = query * jnp.asarray(HD**-0.5, BF)
    key_t = key.T
    grad_q, grad_k, grad_v = [], [], []
    for head in range(2):
        scores = dot_nt(key, lane_half(small_query, head))
        probs = jnp.exp(jnp.where(same, scores, MASKED) - lse_ref[0, head : head + 1, :])
        grad_probs = dot_nt(value, lane_half(grad_ctx, head))
        inner = jnp.sum(probs * grad_probs, axis=0, keepdims=True)
        grad_scores = (probs * (grad_probs - inner)).astype(BF)
        grad_q.append(dot(key_t[head * HD : (head + 1) * HD], grad_scores))
        grad_k.append(dot(grad_scores, query))
        grad_v.append(dot(probs.astype(BF), grad_ctx))
    lanes = lax.broadcasted_iota(jnp.int32, grad_k[0].shape, 1) < HD
    factor = HD**-0.5
    outs = (
        jnp.concatenate(grad_q, axis=0).T * factor,
        jnp.where(lanes, grad_k[0], grad_k[1]) * factor,
        jnp.where(lanes, grad_v[0], grad_v[1]),
    )
    for i, value in enumerate(outs):
        low = value.astype(BF)
        out_ref[:, i * 128 : (i + 1) * 128] = low
        sum_ref[0, :, i * 128 : (i + 1) * 128] = jnp.sum(
            low.astype(F32), axis=0, keepdims=True
        )


def attend_backward(qkv, labels, lse, grad_ctx):
    seqs, length = labels.shape
    pairs = qkv.shape[1] // 384
    grad, sums = pl.pallas_call(
        attend_backward_kernel,
        grid=(seqs, pairs),
        in_specs=[
            pl.BlockSpec((length, 384), lambda s, p: (s, p)),
            pl.BlockSpec((1, 1, length), lambda s, p: (s, 0, 0)),
            pl.BlockSpec((1, 2, length), lambda s, p: (s * pairs + p, 0, 0)),
        ]
        + [
            pl.BlockSpec((length // len(grad_ctx), 128), lambda s, p: (s, p))
            for _ in grad_ctx
        ],
        out_specs=[
            pl.BlockSpec((length, 384), lambda s, p: (s, p)),
            pl.BlockSpec((1, 1, 384), lambda s, p: (s, 0, p)),
        ],
        out_shape=[
            jax.ShapeDtypeStruct(qkv.shape, BF),
            jax.ShapeDtypeStruct((seqs, 1, qkv.shape[1]), F32),
        ],
        compiler_params=PARAMS,
        cost_estimate=cost(seqs * pairs * 40 * 128 * length * length, 8 << 20),
    )(qkv, labels[:, None, :], lse, *grad_ctx)
    return grad, jnp.sum(sums, axis=(0, 1))


def ring_chip(place, chips):
    return jnp.where(place < chips // 2, 2 * place, 2 * (chips - 1 - place) + 1)


def ring_place(chip, chips):
    return jnp.where(chip % 2 == 0, chip // 2, chips - 1 - chip // 2)


def chip_at(me, distance, chips):
    return ring_chip((ring_place(me // 2, chips) + distance + chips) % chips, chips)


def gathered_rows(me, plan, rows, chips):
    out = []
    for distance, other, row in plan:
        core = me % 2
        owner = 2 * chip_at(me, distance, chips) + (1 - core if other else core)
        out.append(pl.multiple_of(owner * rows + row, 16))
    return out


def place_pieces(me, plan, rows, chips, pieces, out, sem):
    copies = [
        pltpu.make_async_copy(piece, out.at[pl.ds(row, piece.shape[0]), :], sem.at[i])
        for i, (piece, row) in enumerate(
            zip(pieces, gathered_rows(me, plan, rows, chips))
        )
    ]
    for copy in copies:
        copy.start()
    for copy in copies:
        copy.wait()


def assemble_kernel(plan, rows, chips, me_ref, *refs):
    pieces, out, sem = refs[: len(plan)], refs[-2], refs[-1]
    place_pieces(me_ref[0], plan, rows, chips, pieces, out, sem)


def assemble(me, plan, pieces, rows, chips):
    cols = pieces[0].shape[1]
    return pl.pallas_call(
        functools.partial(assemble_kernel, plan, rows, chips),
        out_shape=jax.ShapeDtypeStruct((2 * chips * rows, cols), BF),
        in_specs=[SMEM] + [ANY] * len(plan),
        out_specs=VMEM,
        scratch_shapes=[pltpu.SemaphoreType.DMA((len(plan),))],
        compiler_params=PARAMS,
        cost_estimate=cost(0, 8 * chips * rows * cols),
    )(me, *pieces)


def project_kernel(plan, rows, chips, parts, me_ref, bias_ref, *refs):
    blocks, pieces = refs[:parts], refs[parts : parts + len(plan)]
    full, out, sem = refs[-3], refs[-2], refs[-1]
    place_pieces(me_ref[0], plan, rows, chips, pieces, full, sem)
    cols = out.shape[1]
    count = blocks[0].shape[0]
    for i, block in enumerate(blocks):
        for start in range(0, cols, 384):
            out[i * count : (i + 1) * count, start : start + 384] = (
                dot(block[...], full[:, start : start + 384])
                + bias_ref[:, start : start + 384]
            ).astype(BF)


def project(me, plan, pieces, rows, chips, blocks, bias):
    cols, wide = pieces[0].shape[1], bias.shape[1]
    count, width = blocks[0].shape
    tokens = count * len(blocks)
    return pl.pallas_call(
        functools.partial(project_kernel, plan, rows, chips, len(blocks)),
        out_shape=[
            jax.ShapeDtypeStruct((width, cols), BF),
            jax.ShapeDtypeStruct((tokens, wide), BF),
        ],
        in_specs=[SMEM, VMEM] + [VMEM] * len(blocks) + [ANY] * len(plan),
        out_specs=[VMEM, VMEM],
        scratch_shapes=[pltpu.SemaphoreType.DMA((len(plan),))],
        compiler_params=PARAMS,
        cost_estimate=cost(2 * tokens * width * wide, 8 * width * cols),
    )(me, bias, *blocks, *pieces)


def grad_kernel(chips, sources, terms, me_ref, *refs):
    scratch, out = refs[-1], refs[-2]
    d = 2 * pl.program_id(0)
    rows = out.shape[1]
    k = 0
    for col, term in zip(terms, sources):
        total = None
        for _ in range(term):
            pair = jnp.concatenate([refs[k][...], refs[k + 1][...]], axis=1)
            product = dot_tn(pair, refs[k + 2][...])
            total = product if total is None else total + product
            k += 3
        cols = slice(col, col + total.shape[1])
        if total.shape[0] == 2 * rows:
            out[0, :, cols] = total[:rows].astype(BF)
            out[1, :, cols] = total[rows:].astype(BF)
        else:
            lanes = total.shape[0] // 2
            scratch[:, cols] = total
            for i in range(2):
                off = lanes * i + (chip_at(me_ref[0], d + i, chips) * rows) % lanes
                out[i, :, cols] = scratch[pl.ds(pl.multiple_of(off, 32), rows), cols].astype(BF)


def pair_grads(me, chips, terms):
    width = terms[0][0][0].shape[1]
    rows = width // chips
    lanes = max(rows, 128)
    specs, arrays, cols, sources, start, flops = [], [], [], [], 0, 0
    for term in terms:
        cols.append(start)
        sources.append(len(term))
        for wide, narrow, both, row in term:
            count, most = wide.shape[0], narrow.shape[1]
            half = most // 2 if both else most
            if both and half % 128:
                narrow = lax.dynamic_slice_in_dim(narrow, half * (me[0] % 2), half, 1)
                both = False
            specs += [
                pl.BlockSpec(
                    (count, lanes),
                    lambda d, m, i=i: (0, chip_at(m[0], 2 * d + i, chips) * rows // lanes),
                )
                for i in range(2)
            ] + [
                pl.BlockSpec(
                    (count, half),
                    lambda d, m, both=both, row=row: (row, m[0] % 2 if both else 0),
                ),
            ]
            arrays += [wide, wide, narrow]
            flops += 2 * count * width * half
        start += half
    return pl.pallas_call(
        functools.partial(grad_kernel, chips, sources, cols),
        grid_spec=pltpu.PrefetchScalarGridSpec(
            num_scalar_prefetch=1,
            grid=(chips // 2,),
            in_specs=specs,
            out_specs=pl.BlockSpec((2, rows, start), lambda d, m: (d, 0, 0)),
            scratch_shapes=[pltpu.VMEM((2 * lanes, start if lanes > rows else 128), F32)],
        ),
        out_shape=jax.ShapeDtypeStruct((chips, rows, start), BF),
        compiler_params=PARAMS,
        cost_estimate=cost(flops, 8 << 20),
    )(me, *arrays)


def start_all(pairs, sem):
    copies = [
        pltpu.make_async_copy(source, target, sem.at[i])
        for i, (source, target) in enumerate(pairs)
    ]
    for copy in copies:
        copy.start()
    return copies


def wait_all(copies):
    for copy in copies:
        copy.wait()


def start_weights(me, plan, rows, chips, pieces, first, wide, out, sem):
    return start_all(
        [
            (piece.at[:, first : first + wide], out.at[pl.ds(row, piece.shape[0]), :])
            for piece, row in zip(pieces, gathered_rows(me, plan, rows, chips))
        ],
        sem,
    )


def halves(me, kept, own, give):
    wide = own.shape[1]
    core = me % 2
    return [
        (kept.at[:, pl.ds(pl.multiple_of(wide * core, 128), wide)], own),
        (kept.at[:, pl.ds(pl.multiple_of(wide * (1 - core), 128), wide)], give),
    ]


def ffn_forward_kernel(plan, rows, chips, me_ref, bias_o, gain, shift, bias_e, *refs):
    count = len(plan)
    ins, pieces = refs[:3], refs[3 : 3 + count]
    unit_out, low_out, own_out, give_out, slope_out, scale_out, part_out = refs[3 + count : 10 + count]
    (
        tok, own, got, expand, reduce, unit_keep, low_keep, act_keep, slope_keep,
        sem, expand_sem, reduce_sem, out_sem,
    ) = refs[10 + count :]
    me = me_ref[0]
    hidden = act_keep.shape[1]
    loads = start_all(zip(ins, (tok, own, got)), sem)
    expand_loads = start_weights(me, plan, rows, chips, pieces, 0, hidden, expand, expand_sem)
    reduce_loads = start_weights(me, plan, rows, chips, pieces, hidden, hidden, reduce, reduce_sem)
    wait_all(loads)
    normed, unit, scale = ln_forward(
        tok[...].astype(F32) + (own[...].astype(F32) + got[...].astype(F32)) + bias_o[...],
        gain[...],
        shift[...],
    )
    scale_out[...] = scale
    unit_keep[...] = unit
    low_keep[...] = normed.astype(BF)
    copies = start_all([(unit_keep, unit_out), (low_keep, low_out)], out_sem)
    wait_all(expand_loads)
    step = min(512, hidden)
    for start in range(0, hidden, step):
        cols = slice(start, start + step)
        act, slope = gelu_pair(dot(low_keep[...], expand[:, cols]) + bias_e[:, cols])
        act_keep[:, cols] = act.astype(BF)
        slope_keep[:, cols] = slope.astype(BF)
    copies += start_all(
        halves(me, act_keep, own_out, give_out) + [(slope_keep, slope_out)],
        out_sem.at[pl.ds(2, 3)],
    )
    wait_all(reduce_loads)
    part_out[...] = dot_nt(act_keep[...], reduce[...]).astype(BF)
    wait_all(copies)


def ffn_scratch(ring, width, hidden):
    pieces = len(ring.plan)
    return [pltpu.VMEM((width, hidden), BF)] * 2, [
        pltpu.SemaphoreType.DMA((pieces,)),
        pltpu.SemaphoreType.DMA((pieces,)),
    ]


def ffn_forward(me, ring, chips, tok, own, got, bias_o, gain, shift, bias_e):
    count, width = tok.shape
    hidden = bias_e.shape[0]
    weights, sems = ffn_scratch(ring, width, hidden)
    return pl.pallas_call(
        functools.partial(ffn_forward_kernel, ring.plan, ring.rows, chips),
        out_shape=[
            jax.ShapeDtypeStruct((count, width), F32),
            jax.ShapeDtypeStruct((count, width), BF),
            jax.ShapeDtypeStruct((count, hidden // 2), BF),
            jax.ShapeDtypeStruct((count, hidden // 2), BF),
            jax.ShapeDtypeStruct((count, hidden), BF),
            jax.ShapeDtypeStruct((count, 1), F32),
            jax.ShapeDtypeStruct((count, width), BF),
        ],
        in_specs=[SMEM] + [VMEM] * 4 + [ANY] * (3 + len(ring.plan)),
        out_specs=[ANY] * 5 + [VMEM] * 2,
        scratch_shapes=[pltpu.VMEM((count, width), BF)] * 3
        + weights
        + [
            pltpu.VMEM((count, width), F32),
            pltpu.VMEM((count, width), BF),
            pltpu.VMEM((count, hidden), BF),
            pltpu.VMEM((count, hidden), BF),
            pltpu.SemaphoreType.DMA((3,)),
        ]
        + sems
        + [pltpu.SemaphoreType.DMA((5,))],
        compiler_params=PARAMS,
        cost_estimate=cost(8 * count * width * hidden, 16 << 20),
    )(me, bias_o[None], gain[None], shift[None], bias_e[None], tok, own, got, *ring.pieces)


def ffn_backward_kernel(plan, rows, chips, me_ref, vec_ref, *refs):
    count = len(plan)
    ins, pieces = refs[:5], refs[5 : 5 + count]
    result_out, grad_out, low_out, own_out, give_out, part_out, sum_out, wide_out = refs[
        5 + count : 13 + count
    ]
    (
        unit_ref, own, got, cot_ref, slope, expand, reduce,
        result_keep, grad_keep, low_keep, wide_keep,
        sem, expand_sem, reduce_sem, out_sem,
    ) = refs[13 + count :]
    me = me_ref[0]
    hidden = wide_keep.shape[1]
    loads = start_all(zip(ins, (unit_ref, own, got, cot_ref, slope)), sem)
    reduce_loads = start_weights(me, plan, rows, chips, pieces, hidden, hidden, reduce, reduce_sem)
    expand_loads = start_weights(me, plan, rows, chips, pieces, 0, hidden, expand, expand_sem)
    gain_first, shift_first, bias_r, gain, shift = (vec_ref[i : i + 1, :] for i in range(5))
    wait_all(loads)
    mixed = (
        unit_ref[...] * gain_first
        + shift_first
        + (own[...].astype(F32) + got[...].astype(F32))
        + bias_r
    )
    out, unit, scale = ln_forward(mixed, gain, shift)
    cot = cot_ref[...].astype(F32)
    grad = ln_backward(cot, unit, scale, gain)
    result_keep[...] = out.astype(BF)
    grad_keep[...] = grad
    low_keep[...] = grad.astype(BF)
    copies = start_all(
        [(result_keep, result_out), (grad_keep, grad_out), (low_keep, low_out)], out_sem
    )
    for i, value in enumerate((cot * unit, cot, grad)):
        sum_out[i : i + 1, :] = jnp.sum(value, axis=0, keepdims=True)
    wait_all(reduce_loads)
    step = min(512, hidden)
    for start in range(0, hidden, step):
        cols = slice(start, start + step)
        low = (dot(low_keep[...], reduce[:, cols]) * slope[:, cols].astype(F32)).astype(BF)
        wide_keep[:, cols] = low
        wide_out[:, cols] = jnp.sum(low.astype(F32), axis=0, keepdims=True)
    copies += start_all(halves(me, wide_keep, own_out, give_out), out_sem.at[pl.ds(3, 2)])
    wait_all(expand_loads)
    part_out[...] = dot_nt(wide_keep[...], expand[...]).astype(BF)
    wait_all(copies)


def ffn_backward(me, ring, chips, unit, own, got, cot, slope, vectors):
    count, width = unit.shape
    hidden = slope.shape[1]
    weights, sems = ffn_scratch(ring, width, hidden)
    block = pltpu.VMEM((count, width), BF)
    wide = pltpu.VMEM((count, hidden), BF)
    return pl.pallas_call(
        functools.partial(ffn_backward_kernel, ring.plan, ring.rows, chips),
        out_shape=[
            jax.ShapeDtypeStruct((count, width), BF),
            jax.ShapeDtypeStruct((count, width), F32),
            jax.ShapeDtypeStruct((count, width), BF),
            jax.ShapeDtypeStruct((count, hidden // 2), BF),
            jax.ShapeDtypeStruct((count, hidden // 2), BF),
            jax.ShapeDtypeStruct((count, width), BF),
            jax.ShapeDtypeStruct((3, width), F32),
            jax.ShapeDtypeStruct((1, hidden), F32),
        ],
        in_specs=[SMEM, VMEM] + [ANY] * (5 + len(ring.plan)),
        out_specs=[ANY] * 5 + [VMEM] * 3,
        scratch_shapes=[pltpu.VMEM((count, width), F32), block, block, block, wide]
        + weights
        + [
            block,
            pltpu.VMEM((count, width), F32),
            block,
            wide,
            pltpu.SemaphoreType.DMA((5,)),
        ]
        + sems
        + [pltpu.SemaphoreType.DMA((5,))],
        compiler_params=PARAMS,
        cost_estimate=cost(8 * count * width * hidden, 16 << 20),
    )(me, vectors, unit, own, got, cot, slope, *ring.pieces)


def first_backward_kernel(
    mixed_ref, own_ref, got_ref, unit_ref, scale_ref, gain_ref, out_w_ref, *refs
):
    grad_out, low_out, ctx_out, sum_out = refs
    grad_normed = mixed_ref[...] + (own_ref[...].astype(F32) + got_ref[...].astype(F32))
    unit = unit_ref[...]
    grad = ln_backward(grad_normed, unit, scale_ref[...], gain_ref[...])
    low = grad.astype(BF)
    grad_out[...] = grad
    low_out[...] = low
    ctx_out[...] = dot(low, out_w_ref[...]).astype(BF)
    for i, value in enumerate((grad_normed * unit, grad_normed, grad)):
        sum_out[i : i + 1, :] = jnp.sum(value, axis=0, keepdims=True)


def first_backward(mixed, own, got, unit, scale, gain, full_attn):
    count, width = unit.shape
    local = full_attn.shape[1] // 4

    def whole(*shape):
        return pl.BlockSpec(shape, lambda i: (0, 0))

    return pl.pallas_call(
        first_backward_kernel,
        grid=(1,),
        out_shape=[
            jax.ShapeDtypeStruct((count, width), F32),
            jax.ShapeDtypeStruct((count, width), BF),
            jax.ShapeDtypeStruct((count, local), BF),
            jax.ShapeDtypeStruct((3, width), F32),
        ],
        in_specs=[whole(count, width)] * 4
        + [whole(count, 1), whole(1, width), pl.BlockSpec((width, local), lambda i: (0, 3))],
        out_specs=[whole(count, width)] * 2 + [whole(count, local), whole(3, width)],
        compiler_params=PARAMS,
        cost_estimate=cost(2 * count * width * local, 6 << 20),
    )(mixed, own, got, unit, scale, gain[None], full_attn)


def pack_kernel(q_ref, k_ref, v_ref, o_ref, out_ref):
    local = q_ref.shape[1]
    for pair in range(local // 128):
        for i, ref in enumerate((q_ref, k_ref, v_ref)):
            col = 384 * pair + 128 * i
            out_ref[:, col : col + 128] = ref[:, 128 * pair : 128 * (pair + 1)]
    out_ref[:, 3 * local :] = o_ref[...]


def pack(w_query, w_key, w_value, w_output):
    rows, local = w_query.shape
    return pl.pallas_call(
        pack_kernel,
        out_shape=jax.ShapeDtypeStruct((rows, 4 * local), BF),
        in_specs=[VMEM] * 4,
        out_specs=VMEM,
        compiler_params=PARAMS,
    )(w_query, w_key, w_value, w_output)


def pair_major(parts):
    lead = parts[0].shape[:-1]
    stacked = jnp.stack([p.reshape(*lead, -1, 128) for p in parts], axis=-2)
    return stacked.reshape(*lead, -1)


def from_pair_major(array):
    lead = array.shape[:-1]
    stacked = array.reshape(*lead, -1, 3, 128)
    return [stacked[..., i, :].reshape(*lead, -1) for i in range(3)]


def tie(*arrays):
    return lax.optimization_barrier(arrays)


def ln_forward(values, gain, shift):
    centre = values - jnp.mean(values, axis=-1, keepdims=True)
    scale = lax.rsqrt(jnp.mean(centre * centre, axis=-1, keepdims=True) + NORM_EPS)
    unit = centre * scale
    return unit * gain + shift, unit, scale


def ln_backward(grad, unit, scale, gain):
    grad_unit = grad * gain
    along = jnp.mean(grad_unit * unit, axis=-1, keepdims=True)
    return scale * (grad_unit - jnp.mean(grad_unit, axis=-1, keepdims=True) - unit * along)


class Links:
    def __init__(self):
        self.dp = lax.axis_size("dp")
        self.tensor = lax.axis_size("tensor")
        self.chips = self.dp // 2
        self.half_way = self.chips // 2
        self.order = list(range(0, self.chips, 2)) + list(range(1, self.chips, 2))[::-1]
        self.place = lax.axis_index("dp").astype(jnp.int32)
        self.core = self.place % 2
        self.me = self.place.reshape(1)

    def swap_core(self, array):
        return self.swap_dp(array, 1)

    def swap_dp(self, array, bit):
        return lax.ppermute(array, "dp", [(i, i ^ bit) for i in range(self.dp)])

    def swap_tensor(self, array, bit):
        return lax.ppermute(array, "tensor", [(i, i ^ bit) for i in range(self.tensor)])

    def along_ring(self, array, step):
        pairs = [
            (2 * self.order[i] + c, 2 * self.order[(i + step) % self.chips] + c)
            for i in range(self.chips)
            for c in range(2)
        ]
        return lax.ppermute(array, "dp", pairs)

    def bits(self, size):
        return [1 << b for b in range((size - 1).bit_length())]

    def gather_blocks(self, block):
        blocks = [block]
        for bit in self.bits(self.tensor):
            blocks = blocks + [self.swap_tensor(b, bit) for b in blocks]
        return blocks

    def sum_blocks(self, blocks, order, tied=True):
        if self.tensor == 2:
            blocks, got = list(blocks), [None, None]
            first, second = order
            got[second] = self.swap_tensor(blocks[first], 1)
            if tied:
                blocks[second], got[second] = tie(blocks[second], got[second])
            got[first] = self.swap_tensor(blocks[second], 1)
            return list(zip(blocks, got))
        for bit in self.bits(self.tensor):
            low = [b.astype(BF) for b in blocks]
            got = [self.swap_tensor(low[j ^ bit], bit) for j in range(len(low))]
            blocks = [a.astype(F32) + b.astype(F32) for a, b in zip(low, got)]
        return list(zip(low, got))

    def scatter_blocks(self, blocks):
        for bit in self.bits(self.tensor)[::-1]:
            got = [self.swap_tensor(blocks[j + bit].astype(BF), bit) for j in range(bit)]
            blocks = [blocks[j].astype(F32) + got[j].astype(F32) for j in range(bit)]
        return blocks[0]

    def sum_small(self, vector, axis):
        rows = vector.reshape(-1, 128)
        swap, size = (
            (self.swap_tensor, self.tensor) if axis == "tensor" else (self.swap_dp, self.dp)
        )
        for bit in self.bits(size):
            rows = rows + swap(rows, bit)
        return rows.reshape(vector.shape)

    def own_half(self, array):
        half = array.shape[1] // 2
        return lax.dynamic_slice_in_dim(array, half * self.core, half, 1)

    def give_half(self, array):
        half = array.shape[1] // 2
        return self.swap_core(
            lax.dynamic_slice_in_dim(array, half * (1 - self.core), half, 1)
        )

    def swap_halves(self, total):
        rows = total.shape[0] // 2
        mine = lax.dynamic_slice_in_dim(total, rows * self.core, rows, 0)
        other = lax.dynamic_slice_in_dim(total, rows * (1 - self.core), rows, 0)
        got = self.swap_core(other.astype(BF)).astype(F32)
        return mine, got

    def in_order(self, mine, got):
        first = self.core == 0
        return jnp.concatenate(
            [jnp.where(first, mine, got), jnp.where(first, got, mine)], axis=1
        )


class Gather:
    def __init__(self, links, shard):
        self.links = links
        self.rows = shard.shape[0]
        self.up = self.down = shard
        self.plan, self.pieces, self.step = [], [], 0
        self.arrive(shard, 0, 0)

    def arrive(self, block, distance, row):
        self.plan += [(distance, 0, row), (distance, 1, row)]
        self.pieces += [block, self.links.swap_core(block)]

    def hops(self):
        for _ in range(max(1, self.links.half_way // 4)):
            self.hop()

    def finish(self):
        while self.step < self.links.half_way:
            self.hop()

    def hop(self):
        if self.step == self.links.half_way:
            return
        self.step += 1
        half, last = self.rows // 2, self.step == self.links.half_way
        up, down = (self.up[:half], self.down[half:]) if last else (self.up, self.down)
        self.up = self.links.along_ring(up, 1)
        self.down = self.links.along_ring(down, -1)
        self.arrive(self.up, -self.step, 0)
        self.arrive(self.down, self.step, half if last else 0)

    def land(self, *arrays):
        out = tie(self.up, self.down, *arrays)
        self.up, self.down = out[:2]
        if self.step:
            self.pieces[-2], self.pieces[-4] = self.down, self.up
        return out[2:] if len(arrays) > 1 else out[2]

    def full(self):
        return assemble(self.links.me, self.plan, self.pieces, self.rows, self.links.chips)


class Scatter:
    def __init__(self, links, blocks):
        self.links, self.blocks, self.step = links, blocks, links.half_way
        self.rows = blocks.shape[1]
        far = blocks[self.step]
        self.up, self.down = far[: self.rows // 2], far[self.rows // 2 :]

    def hops(self):
        for _ in range(max(1, self.links.half_way // 4)):
            self.hop()

    def finish(self):
        while self.step:
            self.hop()

    def hop(self):
        if not self.step:
            return
        links, half = self.links, self.rows // 2
        up, down = links.along_ring(self.up, 1), links.along_ring(self.down, -1)
        if self.step == links.half_way:
            up = jnp.pad(up, ((0, half), (0, 0)))
            down = jnp.pad(down, ((half, 0), (0, 0)))
        self.step -= 1
        if self.step:
            self.up = add(self.blocks[self.step], up)
            self.down = add(self.blocks[links.chips - self.step], down)
        else:
            self.up, self.down = up, down

    def land(self, *arrays):
        out = tie(self.up, self.down, *arrays)
        self.up, self.down = out[:2]
        return out[2:] if len(arrays) > 1 else out[2]

    def total(self):
        self.finish()
        return self.blocks[0].astype(F32) + self.up.astype(F32) + self.down.astype(F32)


def add(a, b):
    return (a.astype(F32) + b.astype(F32)).astype(BF)


def gelu_pair(u):
    cdf = 0.5 * (1.0 + lax.erf(u * (0.5**0.5)))
    slope = cdf + u * jnp.exp(-0.5 * u * u) * 0.3989422804014327
    return u * cdf, slope


def shards(
    inputs,
    segments,
    w_query,
    w_key,
    w_value,
    w_output,
    w_expand,
    w_reduce,
    query_bias_vector,
    b_value,
    b_output,
    b_expand,
    b_reduce,
    gain_first,
    shift_first,
    gain_second,
    shift_second,
    cotangent,
):
    links = Links()
    parts = links.tensor
    rank = lax.axis_index("tensor")
    seqs, span, width = inputs.shape
    local = w_query.shape[1]
    hidden = w_expand.shape[1]
    length = span * parts
    chips = links.chips

    def flat(block):
        return block.reshape(seqs * span, block.shape[-1])

    def joined(blocks):
        return jnp.concatenate(
            [b.reshape(seqs, span, b.shape[-1]) for b in blocks], axis=1
        ).reshape(seqs * length, -1)

    def split(array):
        array = array.reshape(seqs, length, -1)
        return [flat(array[:, j * span : (j + 1) * span]) for j in range(parts)]

    attn = Gather(links, pack(w_query, w_key, w_value, w_output.T))
    attn.hops()
    token_blocks = [flat(b) for b in links.gather_blocks(inputs)]
    attn.hops()
    ffn_shard, cotangent = attn.land(
        jnp.concatenate([w_expand, w_reduce.T], axis=1), cotangent
    )
    attn.hops()
    ffn = Gather(links, attn.land(ffn_shard))
    attn.finish()
    ffn.hops()
    cotangent_blocks = [flat(b) for b in links.gather_blocks(cotangent)]

    labels = jnp.concatenate(
        [
            lax.dynamic_slice_in_dim(segments, span * (rank ^ j), span, 1)
            for j in range(parts)
        ],
        axis=1,
    )
    tokens = token_blocks if seqs == 1 else [joined(token_blocks)]
    tokens_pair = [links.swap_core(t) for t in tokens]

    qkv_bias = pair_major([query_bias_vector, jnp.zeros_like(b_value), b_value])
    full_attn, qkv = project(
        links.me, attn.plan, attn.pieces, attn.rows, chips, tokens, qkv_bias[None]
    )
    ffn.hops()
    context, lse, partial = attend_forward(qkv, labels, full_attn, parts)
    partial = list(partial)
    cotangent_blocks[-1], partial[-1] = tie(cotangent_blocks[-1], partial[-1])
    partial[0] = ffn.land(partial[0])
    sums = links.sum_blocks(partial, range(parts)[::-1], tied=False)
    ffn.hops()
    sums[0] = (sums[0][0], ffn.land(sums[0][1]))
    ffn.finish()

    units, scales, normed_low, activated, slopes, partial = [], [], [], [], [], []
    for tok, (own, got) in zip(token_blocks, sums):
        unit, low, act, act_give, slope, scale, part = ffn_forward(
            links.me, ffn, chips, tok, own, got, b_output, gain_first, shift_first, b_expand
        )
        units.append(unit)
        scales.append(scale)
        normed_low.append(low)
        activated.append((act, act_give))
        slopes.append(slope)
        partial.append(part)

    sums = links.sum_blocks(partial, range(parts))
    vectors = jnp.stack([gain_first, shift_first, b_reduce, gain_second, shift_second])
    grad_mixed, reduce_in, expand_low, partial = ([None] * parts for _ in range(4))
    grad_b_expand, small = 0.0, {}
    for j in range(parts)[::-1]:
        own, got = sums[j]
        out, grad, low, wide, wide_give, part, sums_mixed, sums_wide = ffn_backward(
            links.me, ffn, chips, units[j], own, got, cotangent_blocks[j], slopes[j], vectors
        )
        if j == 0:
            result = out.reshape(seqs, span, width)
            small["gain_second"], small["shift_second"], small["b_reduce"] = sums_mixed
        grad_b_expand = grad_b_expand + sums_wide[0]
        grad_mixed[j], reduce_in[j], expand_low[j], partial[j] = (
            grad, low, (wide, wide_give), part,
        )

    def cut_cores(wide, narrow):
        return [(w, n, False, 0) for w, (n, _) in zip(wide, narrow)] + [
            (links.swap_core(w), links.swap_core(n), False, 0)
            for w, (_, n) in zip(wide, narrow)
        ]

    def both_cores(wide, narrow):
        return [(w, n, True, 0) for w, n in zip(wide, narrow)] + [
            (links.swap_core(w), links.give_half(n), False, 0) for w, n in zip(wide, narrow)
        ]

    def rows_of(wide, narrow):
        pair = links.give_half(narrow)
        return [(w, narrow, True, j) for j, w in enumerate(wide)] + [
            (w, pair, False, j) for j, w in enumerate([links.swap_core(w) for w in wide])
        ]

    sums = links.sum_blocks(partial, range(parts)[::-1])
    blocks = pair_grads(
        links.me,
        chips,
        [cut_cores(reduce_in, activated), cut_cores(normed_low, expand_low)],
    )
    last = sums[parts - 1]
    blocks, got = tie(blocks, last[1])
    sums[parts - 1] = (last[0], got)
    ffn_sum = Scatter(links, blocks)
    ffn_sum.hops()
    grad_attended, attn_low, grad_context = [], [], []
    for j in range(parts):
        grad, low, grad_ctx, sums_first = first_backward(
            grad_mixed[j], *sums[j], units[j], scales[j], gain_first, full_attn
        )
        if j == 0:
            small["gain_first"], small["shift_first"], small["b_output"] = sums_first
        grad_attended.append(grad)
        attn_low.append(low)
        grad_context.append(grad_ctx)
    grad_context[0] = ffn_sum.land(grad_context[0])
    ffn_sum.hops()
    grad_qkv, bias_sums = attend_backward(qkv, labels, lse, grad_context)
    grad_qkv = ffn_sum.land(grad_qkv)
    ffn_sum.hops()
    if seqs == 1:
        context_terms = rows_of(attn_low, context)
        pair = links.give_half(grad_qkv)
        qkv_terms = [(t, grad_qkv, True, j) for j, t in enumerate(tokens)] + [
            (t, pair, False, j) for j, t in enumerate(tokens_pair)
        ]
    else:
        context_terms = both_cores(attn_low, split(context))
        qkv_terms = [
            (tokens[0], grad_qkv, True, 0),
            (tokens_pair[0], links.give_half(grad_qkv), False, 0),
        ]
    blocks, back = tie(pair_grads(links.me, chips, [qkv_terms, context_terms]), grad_qkv)
    attn_sum = Scatter(links, blocks)
    attn_sum.hops()
    inputs_back = dot_nt(back, full_attn[:, : 3 * local])
    grad_inputs = grad_attended[0] + links.scatter_blocks(split(inputs_back))
    ffn_sum.finish()
    grad_inputs, bias_sums = attn_sum.land(grad_inputs, bias_sums)
    attn_sum.finish()
    mine, got = links.swap_halves(ffn_sum.total())
    half_hidden, half_local = hidden // 2, local // 2
    grad_reduce = links.in_order(mine[:, :half_hidden], got[:, :half_hidden])
    grad_expand = links.in_order(mine[:, half_hidden:], got[:, half_hidden:])
    mine, got = links.swap_halves(attn_sum.total())
    grad_wq, grad_wk, grad_wv = from_pair_major(
        links.in_order(mine[:, : 3 * half_local], got[:, : 3 * half_local])
    )
    grad_output = links.in_order(mine[:, 3 * half_local :], got[:, 3 * half_local :])

    names = ("b_output", "b_reduce", "gain_first", "shift_first", "gain_second", "shift_second")
    early = links.sum_small(jnp.stack([small[k] for k in names]), "tensor")
    late = links.sum_small(
        jnp.concatenate([early.reshape(-1), grad_b_expand, bias_sums]), "dp"
    )
    early = late[: 6 * width].reshape(6, width)
    middle = late[6 * width : 6 * width + hidden]
    grad_bq, _, grad_bv = from_pair_major(late[6 * width + hidden :])
    return (
        result,
        grad_inputs.reshape(seqs, span, width),
        grad_wq,
        grad_wk,
        grad_wv,
        grad_output.T,
        grad_expand,
        grad_reduce.T,
        grad_bq,
        grad_bv,
        early[0],
        middle,
        early[1],
        early[2],
        early[3],
        early[4],
        early[5],
    )


def solution(mesh):
    return jax.shard_map(
        shards,
        mesh=mesh,
        in_specs=(
            P("dp", "tensor", None),
            P("dp", None),
            P("dp", "tensor"),
            P("dp", "tensor"),
            P("dp", "tensor"),
            P("tensor", "dp"),
            P("dp", "tensor"),
            P("tensor", "dp"),
            P("tensor"),
            P("tensor"),
            P(),
            P("tensor"),
            P(),
            P(),
            P(),
            P(),
            P(),
            P("dp", "tensor", None),
        ),
        out_specs=(
            P("dp", "tensor", None),
            P("dp", "tensor", None),
            P("dp", "tensor"),
            P("dp", "tensor"),
            P("dp", "tensor"),
            P("tensor", "dp"),
            P("dp", "tensor"),
            P("tensor", "dp"),
            P("tensor"),
            P("tensor"),
            P(),
            P("tensor"),
            P(),
            P(),
            P(),
            P(),
            P(),
        ),
        check_vma=False,
    )
```

```python
import functools

import jax
import jax.numpy as jnp
from jax import lax
from jax.experimental import pallas as pl
from jax.experimental.pallas import tpu as pltpu
from jax.sharding import PartitionSpec as P

HD = 64
NORM_EPS = 1e-05
MASKED = -1e30
BF = jnp.bfloat16
F32 = jnp.float32
PARAMS = pltpu.CompilerParams(vmem_limit_bytes=60 << 20)
VMEM = pl.BlockSpec(memory_space=pltpu.VMEM)
SMEM = pl.BlockSpec(memory_space=pltpu.SMEM)
ANY = pl.BlockSpec(memory_space=pltpu.HBM)


def dot(a, b):
    return lax.dot_general(a, b, (((1,), (0,)), ((), ())), preferred_element_type=F32)


def dot_nt(a, b):
    return lax.dot_general(a, b, (((1,), (1,)), ((), ())), preferred_element_type=F32)


def dot_tn(a, b):
    return lax.dot_general(a, b, (((0,), (0,)), ((), ())), preferred_element_type=F32)


def cost(flops, nbytes):
    return pl.CostEstimate(flops=flops // 1024, bytes_accessed=nbytes // 1024, transcendentals=0)


def lane_half(array, head):
    lanes = lax.broadcasted_iota(jnp.int32, array.shape, 1)
    return jnp.where((lanes < HD) == (head == 0), array, jnp.zeros_like(array))


def column_of(row):
    return jnp.broadcast_to(row, (128, row.shape[1])).T[:, :1]


def attend_forward_kernel(parts, qkv_ref, row_ref, out_w_ref, *refs):
    ctx_ref, lse_ref, part_refs, scratch = refs[0], refs[1], refs[2 : 2 + parts], refs[-1]
    query, key, value = (qkv_ref[:, i * 128 : (i + 1) * 128] for i in range(3))
    same = column_of(row_ref[0]) == row_ref[0]
    query = query * jnp.asarray(HD**-0.5, BF)
    value_t = value.T
    out = []
    for head in range(2):
        scores = dot_nt(key, lane_half(query, head))
        scores = jnp.where(same, scores, MASKED)
        top = jnp.max(scores, axis=0, keepdims=True)
        weights = jnp.exp(scores - top)
        total = jnp.sum(weights, axis=0, keepdims=True)
        probs = (weights * (1.0 / total)).astype(BF)
        lse_ref[0, head : head + 1, :] = top + jnp.log(total)
        out.append(dot(value_t[head * HD : (head + 1) * HD], probs))
    context = jnp.concatenate(out, axis=0).T.astype(BF)
    ctx_ref[...] = context
    pair, pairs = pl.program_id(1), pl.num_programs(1)
    scratch[pair] = context

    @pl.when(pair == pairs - 1)
    def _():
        span = part_refs[0].shape[0]
        whole = jnp.concatenate([scratch[i] for i in range(scratch.shape[0])], axis=1)
        for j, part_ref in enumerate(part_refs):
            part_ref[...] = dot_nt(whole[j * span : (j + 1) * span], out_w_ref[...]).astype(BF)


def attend_forward(qkv, labels, full_attn, parts):
    seqs, length = labels.shape
    pairs = qkv.shape[1] // 384
    local, width, span = 128 * pairs, full_attn.shape[0], length // parts
    out = pl.pallas_call(
        functools.partial(attend_forward_kernel, parts),
        grid=(seqs, pairs),
        in_specs=[
            pl.BlockSpec((length, 384), lambda s, p: (s, p)),
            pl.BlockSpec((1, 1, length), lambda s, p: (s, 0, 0)),
            pl.BlockSpec((width, local), lambda s, p: (0, 3)),
        ],
        out_specs=[
            pl.BlockSpec((length, 128), lambda s, p: (s, p)),
            pl.BlockSpec((1, 2, length), lambda s, p: (s * pairs + p, 0, 0)),
        ]
        + [pl.BlockSpec((span, width), lambda s, p: (s, 0))] * parts,
        out_shape=[
            jax.ShapeDtypeStruct((seqs * length, local), BF),
            jax.ShapeDtypeStruct((seqs * pairs, 2, length), F32),
        ]
        + [jax.ShapeDtypeStruct((seqs * span, width), BF)] * parts,
        scratch_shapes=[pltpu.VMEM((pairs, length, 128), BF)],
        compiler_params=PARAMS,
        cost_estimate=cost(seqs * pairs * 24 * 128 * length * length, 8 << 20),
    )(qkv, labels[:, None, :], full_attn)
    return out[0], out[1], out[2:]


def attend_backward_body(qkv_ref, row_ref, lse_ref, w_ref, parts, *refs):
    out_ref, sum_ref = refs[parts : parts + 2]
    query, key, value = (qkv_ref[:, i * 128 : (i + 1) * 128] for i in range(3))
    grad_ctx = jnp.concatenate([ref[...] for ref in refs[:parts]], axis=0)
    same = column_of(row_ref[0]) == row_ref[0]
    small_query = query * jnp.asarray(HD**-0.5, BF)
    key_t = key.T
    grad_q, grad_k, grad_v = [], [], []
    for head in range(2):
        scores = dot_nt(key, lane_half(small_query, head))
        probs = jnp.exp(jnp.where(same, scores, MASKED) - lse_ref[0, head : head + 1, :])
        grad_probs = dot_nt(value, lane_half(grad_ctx, head))
        inner = jnp.sum(probs * grad_probs, axis=0, keepdims=True)
        grad_scores = (probs * (grad_probs - inner)).astype(BF)
        grad_q.append(dot(key_t[head * HD : (head + 1) * HD], grad_scores))
        grad_k.append(dot(grad_scores, query))
        grad_v.append(dot(probs.astype(BF), grad_ctx))
    lanes = lax.broadcasted_iota(jnp.int32, grad_k[0].shape, 1) < HD
    factor = HD**-0.5
    outs = (
        jnp.concatenate(grad_q, axis=0).T * factor,
        jnp.where(lanes, grad_k[0], grad_k[1]) * factor,
        jnp.where(lanes, grad_v[0], grad_v[1]),
    )
    for i, value in enumerate(outs):
        low = value.astype(BF)
        out_ref[:, i * 128 : (i + 1) * 128] = low
        sum_ref[0, :, i * 128 : (i + 1) * 128] = jnp.sum(
            low.astype(F32), axis=0, keepdims=True
        )


def attend_backward_kernel(parts, halved, me_ref, qkv_ref, row_ref, lse_ref, w_ref, *refs):
    attend_backward_body(qkv_ref, row_ref, lse_ref, w_ref, parts, *refs)
    out_ref, back_refs, total = refs[parts], refs[parts + 2 : 2 * parts + 2], refs[-1]
    pair, pairs = pl.program_id(1), pl.num_programs(1)
    part = dot_nt(out_ref[...], w_ref[...])

    @pl.when(pair == 0)
    def _():
        total[...] = part

    @pl.when(pair != 0)
    def _():
        total[...] += part

    @pl.when(pair == pairs - 1)
    def _():
        span = back_refs[0].shape[0]
        for j, ref in enumerate(back_refs):
            ref[...] = total[j * span : (j + 1) * span, :].astype(ref.dtype)

    if halved:
        give_ref = refs[2 * parts + 2]

        @pl.when(pair // (pairs // 2) == 1 - me_ref[0] % 2)
        def _():
            give_ref[...] = out_ref[...]


def attend_backward(me, qkv, labels, lse, full_attn, grad_ctx):
    seqs, length = labels.shape
    pairs = qkv.shape[1] // 384
    half = pairs // 2
    parts = len(grad_ctx)
    span, width = length // parts, full_attn.shape[0]
    kernel = functools.partial(attend_backward_kernel, parts, half > 0)

    def give_place(s, p, m):
        return s, jnp.clip(p - half * (1 - m[0] % 2), 0, max(half - 1, 0))

    out = pl.pallas_call(
        kernel,
        grid_spec=pltpu.PrefetchScalarGridSpec(
            num_scalar_prefetch=1,
            grid=(seqs, pairs),
            in_specs=[
                pl.BlockSpec((length, 384), lambda s, p, m: (s, p)),
                pl.BlockSpec((1, 1, length), lambda s, p, m: (s, 0, 0)),
                pl.BlockSpec((1, 2, length), lambda s, p, m: (s * pairs + p, 0, 0)),
                pl.BlockSpec((width, 384), lambda s, p, m: (0, p)),
            ]
            + [
                pl.BlockSpec((length // len(grad_ctx), 128), lambda s, p, m: (s, p))
                for _ in grad_ctx
            ],
            out_specs=[
                pl.BlockSpec((length, 384), lambda s, p, m: (s, p)),
                pl.BlockSpec((1, 1, 384), lambda s, p, m: (s, 0, p)),
            ]
            + [pl.BlockSpec((span, width), lambda s, p, m: (s, 0))] * parts
            + ([pl.BlockSpec((length, 384), give_place)] if half else []),
            scratch_shapes=[pltpu.VMEM((length, width), F32)],
        ),
        out_shape=[
            jax.ShapeDtypeStruct(qkv.shape, BF),
            jax.ShapeDtypeStruct((seqs, 1, qkv.shape[1]), F32),
        ]
        + [jax.ShapeDtypeStruct((seqs * span, width), BF if j else F32) for j in range(parts)]
        + ([jax.ShapeDtypeStruct((qkv.shape[0], 384 * half), BF)] if half else []),
        compiler_params=PARAMS,
        cost_estimate=cost(seqs * pairs * 40 * 128 * length * length, 8 << 20),
    )(me, qkv, labels[:, None, :], lse, full_attn, *grad_ctx)
    bias = jnp.sum(out[1], axis=(0, 1))
    return out[0], bias, out[-1] if half else None, list(out[2 : 2 + parts])


def ring_chip(place, chips):
    return jnp.where(place < chips // 2, 2 * place, 2 * (chips - 1 - place) + 1)


def ring_place(chip, chips):
    return jnp.where(chip % 2 == 0, chip // 2, chips - 1 - chip // 2)


def chip_at(me, distance, chips):
    return ring_chip((ring_place(me // 2, chips) + distance + chips) % chips, chips)


def gathered_rows(me, plan, rows, chips):
    out = []
    for distance, other, row in plan:
        core = me % 2
        owner = 2 * chip_at(me, distance, chips) + (1 - core if other else core)
        out.append(pl.multiple_of(owner * rows + row, 16))
    return out


def place_pieces(me, plan, rows, chips, pieces, out, sem):
    copies = [
        pltpu.make_async_copy(piece, out.at[pl.ds(row, piece.shape[0]), :], sem.at[i])
        for i, (piece, row) in enumerate(
            zip(pieces, gathered_rows(me, plan, rows, chips))
        )
    ]
    for copy in copies:
        copy.start()
    for copy in copies:
        copy.wait()


def assemble_kernel(plan, rows, chips, me_ref, *refs):
    pieces, out, sem = refs[: len(plan)], refs[-2], refs[-1]
    place_pieces(me_ref[0], plan, rows, chips, pieces, out, sem)


def assemble(me, plan, pieces, rows, chips):
    cols = pieces[0].shape[1]
    return pl.pallas_call(
        functools.partial(assemble_kernel, plan, rows, chips),
        out_shape=jax.ShapeDtypeStruct((2 * chips * rows, cols), BF),
        in_specs=[SMEM] + [ANY] * len(plan),
        out_specs=VMEM,
        scratch_shapes=[pltpu.SemaphoreType.DMA((len(plan),))],
        compiler_params=PARAMS,
        cost_estimate=cost(0, 8 * chips * rows * cols),
    )(me, *pieces)


def project_kernel(plan, rows, chips, parts, me_ref, bias_ref, *refs):
    blocks, pieces = refs[:parts], refs[parts : parts + len(plan)]
    full_out, out, full, sem, out_sem = refs[parts + len(plan) :]
    place_pieces(me_ref[0], plan, rows, chips, pieces, full, sem)
    copy = pltpu.make_async_copy(full, full_out, out_sem)
    copy.start()
    cols = out.shape[1]
    count = blocks[0].shape[0]
    for i, block in enumerate(blocks):
        for start in range(0, cols, 384):
            out[i * count : (i + 1) * count, start : start + 384] = (
                dot(block[...], full[:, start : start + 384])
                + bias_ref[:, start : start + 384]
            ).astype(BF)
    copy.wait()


def project(me, plan, pieces, rows, chips, blocks, bias):
    cols, wide = pieces[0].shape[1], bias.shape[1]
    count, width = blocks[0].shape
    tokens = count * len(blocks)
    return pl.pallas_call(
        functools.partial(project_kernel, plan, rows, chips, len(blocks)),
        out_shape=[
            jax.ShapeDtypeStruct((width, cols), BF),
            jax.ShapeDtypeStruct((tokens, wide), BF),
        ],
        in_specs=[SMEM, VMEM] + [VMEM] * len(blocks) + [ANY] * len(plan),
        out_specs=[ANY, VMEM],
        scratch_shapes=[
            pltpu.VMEM((width, cols), BF),
            pltpu.SemaphoreType.DMA((len(plan),)),
            pltpu.SemaphoreType.DMA,
        ],
        compiler_params=PARAMS,
        cost_estimate=cost(2 * tokens * width * wide, 8 * width * cols),
    )(me, bias, *blocks, *pieces)


def grad_kernel(chips, sources, terms, me_ref, *refs):
    scratch, out = refs[-1], refs[-2]
    d = 2 * pl.program_id(0)
    rows = out.shape[1]
    k = 0
    for col, term in zip(terms, sources):
        total = None
        for _ in range(term):
            pair = jnp.concatenate([refs[k][...], refs[k + 1][...]], axis=1)
            product = dot_tn(pair, refs[k + 2][...])
            total = product if total is None else total + product
            k += 3
        cols = slice(col, col + total.shape[1])
        if total.shape[0] == 2 * rows:
            out[0, :, cols] = total[:rows].astype(BF)
            out[1, :, cols] = total[rows:].astype(BF)
        else:
            lanes = total.shape[0] // 2
            scratch[:, cols] = total
            for i in range(2):
                off = lanes * i + (chip_at(me_ref[0], d + i, chips) * rows) % lanes
                out[i, :, cols] = scratch[pl.ds(pl.multiple_of(off, 32), rows), cols].astype(BF)


def pair_grads(me, chips, terms):
    width = terms[0][0][0].shape[1]
    rows = width // chips
    lanes = max(rows, 128)
    specs, arrays, cols, sources, start, flops = [], [], [], [], 0, 0
    for term in terms:
        cols.append(start)
        sources.append(len(term))
        for wide, narrow, both, row in term:
            count, most = wide.shape[0], narrow.shape[1]
            half = most // 2 if both else most
            if both and half % 128:
                narrow = lax.dynamic_slice_in_dim(narrow, half * (me[0] % 2), half, 1)
                both = False
            specs += [
                pl.BlockSpec(
                    (count, lanes),
                    lambda d, m, i=i: (0, chip_at(m[0], 2 * d + i, chips) * rows // lanes),
                )
                for i in range(2)
            ] + [
                pl.BlockSpec(
                    (count, half),
                    lambda d, m, both=both, row=row: (row, m[0] % 2 if both else 0),
                ),
            ]
            arrays += [wide, wide, narrow]
            flops += 2 * count * width * half
        start += half
    return pl.pallas_call(
        functools.partial(grad_kernel, chips, sources, cols),
        grid_spec=pltpu.PrefetchScalarGridSpec(
            num_scalar_prefetch=1,
            grid=(chips // 2,),
            in_specs=specs,
            out_specs=pl.BlockSpec((2, rows, start), lambda d, m: (d, 0, 0)),
            scratch_shapes=[pltpu.VMEM((2 * lanes, start if lanes > rows else 128), F32)],
        ),
        out_shape=jax.ShapeDtypeStruct((chips, rows, start), BF),
        compiler_params=PARAMS,
        cost_estimate=cost(flops, 8 << 20),
    )(me, *arrays)


def start_all(pairs, sem):
    copies = [
        pltpu.make_async_copy(source, target, sem.at[i])
        for i, (source, target) in enumerate(pairs)
    ]
    for copy in copies:
        copy.start()
    return copies


def wait_all(copies):
    for copy in copies:
        copy.wait()


def start_weights(me, plan, rows, chips, sources, which, out, sem):
    wide = out.shape[1]
    if plan is None:
        half = wide // 2
        return [
            start_all(
                [(sources[which].at[:, k : k + half], out.at[:, k : k + half])],
                sem.at[pl.ds(k // half, 1)],
            )
            for k in (0, half)
        ]
    return [
        start_all(
            [
                (
                    piece.at[:, which * wide : (which + 1) * wide],
                    out.at[pl.ds(row, piece.shape[0]), :],
                )
                for piece, row in zip(sources, gathered_rows(me, plan, rows, chips))
            ],
            sem,
        )
    ]


def halves(me, kept, own, give):
    wide = own.shape[1]
    core = me % 2
    return [
        (kept.at[:, pl.ds(pl.multiple_of(wide * core, 128), wide)], own),
        (kept.at[:, pl.ds(pl.multiple_of(wide * (1 - core), 128), wide)], give),
    ]


def ffn_forward_kernel(plan, rows, chips, me_ref, bias_o, gain, shift, bias_e, *refs):
    count = 2 if plan is None else len(plan)
    ins, pieces, refs = refs[:3], refs[3 : 3 + count], refs[3 + count :]
    unit_out, low_out, own_out, give_out, slope_out = refs[:5]
    kept_out, refs = ((), refs) if plan is None else (refs[5:7], refs[2:])
    scale_out, part_out, refs = refs[5], refs[6], refs[7:]
    (
        tok, own, got, expand, reduce, unit_keep, low_keep, act_keep, slope_keep,
        sem, expand_sem, reduce_sem, out_sem,
    ) = refs
    me = me_ref[0]
    hidden = act_keep.shape[1]
    loads = start_all(zip(ins, (tok, own, got)), sem)
    expand_loads = start_weights(me, plan, rows, chips, pieces, 0, expand, expand_sem)
    reduce_loads = start_weights(me, plan, rows, chips, pieces, 1, reduce, reduce_sem)
    wait_all(loads)
    normed, unit, scale = ln_forward(
        tok[...].astype(F32) + (own[...].astype(F32) + got[...].astype(F32)) + bias_o[...],
        gain[...],
        shift[...],
    )
    scale_out[...] = scale
    unit_keep[...] = unit
    low_keep[...] = normed.astype(BF)
    copies = start_all([(unit_keep, unit_out), (low_keep, low_out)], out_sem)
    parts = len(expand_loads)
    step = min(512, hidden // parts)
    for start in range(0, hidden, step):
        if start % (hidden // parts) == 0:
            wait_all(expand_loads[start * parts // hidden])
        cols = slice(start, start + step)
        act, slope = gelu_pair(dot(low_keep[...], expand[:, cols]) + bias_e[:, cols])
        act_keep[:, cols] = act.astype(BF)
        slope_keep[:, cols] = slope.astype(BF)
    copies += start_all(
        halves(me, act_keep, own_out, give_out) + [(slope_keep, slope_out)],
        out_sem.at[pl.ds(2, 3)],
    )
    for load in reduce_loads:
        wait_all(load)
    if kept_out:
        copies += start_all(
            zip((expand, reduce), kept_out), out_sem.at[pl.ds(5, 2)]
        )
    part_out[...] = dot_nt(act_keep[...], reduce[...]).astype(BF)
    wait_all(copies)


def ffn_weights(ring, weights):
    if weights is None:
        return ring.plan, ring.pieces
    return None, weights


def ffn_scratch(sources, width, hidden):
    pieces = len(sources)
    return [pltpu.VMEM((width, hidden), BF)] * 2, [
        pltpu.SemaphoreType.DMA((pieces,)),
        pltpu.SemaphoreType.DMA((pieces,)),
    ]


def ffn_forward(me, ring, weights, chips, tok, own, got, bias_o, gain, shift, bias_e):
    count, width = tok.shape
    hidden = bias_e.shape[0]
    plan, sources = ffn_weights(ring, weights)
    scratch, sems = ffn_scratch(sources, width, hidden)
    kept = [] if weights else [jax.ShapeDtypeStruct((width, hidden), BF)] * 2
    out = pl.pallas_call(
        functools.partial(ffn_forward_kernel, plan, ring.rows, chips),
        out_shape=[
            jax.ShapeDtypeStruct((count, width), F32),
            jax.ShapeDtypeStruct((count, width), BF),
            jax.ShapeDtypeStruct((count, hidden // 2), BF),
            jax.ShapeDtypeStruct((count, hidden // 2), BF),
            jax.ShapeDtypeStruct((count, hidden), BF),
        ]
        + kept
        + [
            jax.ShapeDtypeStruct((count, 1), F32),
            jax.ShapeDtypeStruct((count, width), BF),
        ],
        in_specs=[SMEM] + [VMEM] * 4 + [ANY] * (3 + len(sources)),
        out_specs=[ANY] * (5 + len(kept)) + [VMEM] * 2,
        scratch_shapes=[pltpu.VMEM((count, width), BF)] * 3
        + scratch
        + [
            pltpu.VMEM((count, width), F32),
            pltpu.VMEM((count, width), BF),
            pltpu.VMEM((count, hidden), BF),
            pltpu.VMEM((count, hidden), BF),
            pltpu.SemaphoreType.DMA((3,)),
        ]
        + sems
        + [pltpu.SemaphoreType.DMA((5 + len(kept),))],
        compiler_params=PARAMS,
        cost_estimate=cost(8 * count * width * hidden, 16 << 20),
    )(me, bias_o[None], gain[None], shift[None], bias_e[None], tok, own, got, *sources)
    return weights or out[5:7], (*out[:5], *out[5 + len(kept) :])


def ffn_backward_kernel(plan, rows, chips, me_ref, vec_ref, *refs):
    count = 2 if plan is None else len(plan)
    ins, pieces = refs[:5], refs[5 : 5 + count]
    result_out, grad_out, low_out, own_out, give_out, part_out, sum_out, wide_out = refs[
        5 + count : 13 + count
    ]
    (
        unit_ref, own, got, cot_ref, slope, expand, reduce,
        result_keep, grad_keep, low_keep, wide_keep,
        sem, expand_sem, reduce_sem, out_sem,
    ) = refs[13 + count :]
    me = me_ref[0]
    hidden = wide_keep.shape[1]
    loads = start_all(zip(ins, (unit_ref, own, got, cot_ref, slope)), sem)
    reduce_loads = start_weights(me, plan, rows, chips, pieces, 1, reduce, reduce_sem)
    expand_loads = start_weights(me, plan, rows, chips, pieces, 0, expand, expand_sem)
    gain_first, shift_first, bias_r, gain, shift = (vec_ref[i : i + 1, :] for i in range(5))
    wait_all(loads)
    mixed = (
        unit_ref[...] * gain_first
        + shift_first
        + (own[...].astype(F32) + got[...].astype(F32))
        + bias_r
    )
    out, unit, scale = ln_forward(mixed, gain, shift)
    cot = cot_ref[...].astype(F32)
    grad = ln_backward(cot, unit, scale, gain)
    result_keep[...] = out.astype(BF)
    grad_keep[...] = grad
    low_keep[...] = grad.astype(BF)
    copies = start_all(
        [(result_keep, result_out), (grad_keep, grad_out), (low_keep, low_out)], out_sem
    )
    for i, value in enumerate((cot * unit, cot, grad)):
        sum_out[i : i + 1, :] = jnp.sum(value, axis=0, keepdims=True)
    parts = len(reduce_loads)
    step = min(512, hidden // parts)
    for start in range(0, hidden, step):
        if start % (hidden // parts) == 0:
            wait_all(reduce_loads[start * parts // hidden])
        cols = slice(start, start + step)
        low = (dot(low_keep[...], reduce[:, cols]) * slope[:, cols].astype(F32)).astype(BF)
        wide_keep[:, cols] = low
        wide_out[:, cols] = jnp.sum(low.astype(F32), axis=0, keepdims=True)
    copies += start_all(halves(me, wide_keep, own_out, give_out), out_sem.at[pl.ds(3, 2)])
    for load in expand_loads:
        wait_all(load)
    part_out[...] = dot_nt(wide_keep[...], expand[...]).astype(BF)
    wait_all(copies)


def ffn_backward(me, ring, weights, chips, unit, own, got, cot, slope, vectors):
    count, width = unit.shape
    hidden = slope.shape[1]
    plan, sources = ffn_weights(ring, weights)
    scratch, sems = ffn_scratch(sources, width, hidden)
    block = pltpu.VMEM((count, width), BF)
    wide = pltpu.VMEM((count, hidden), BF)
    return pl.pallas_call(
        functools.partial(ffn_backward_kernel, plan, ring.rows, chips),
        out_shape=[
            jax.ShapeDtypeStruct((count, width), BF),
            jax.ShapeDtypeStruct((count, width), F32),
            jax.ShapeDtypeStruct((count, width), BF),
            jax.ShapeDtypeStruct((count, hidden // 2), BF),
            jax.ShapeDtypeStruct((count, hidden // 2), BF),
            jax.ShapeDtypeStruct((count, width), BF),
            jax.ShapeDtypeStruct((3, width), F32),
            jax.ShapeDtypeStruct((1, hidden), F32),
        ],
        in_specs=[SMEM, VMEM] + [ANY] * (5 + len(sources)),
        out_specs=[ANY] * 5 + [VMEM] * 3,
        scratch_shapes=[pltpu.VMEM((count, width), F32), block, block, block, wide]
        + scratch
        + [
            block,
            pltpu.VMEM((count, width), F32),
            block,
            wide,
            pltpu.SemaphoreType.DMA((5,)),
        ]
        + sems
        + [pltpu.SemaphoreType.DMA((5,))],
        compiler_params=PARAMS,
        cost_estimate=cost(8 * count * width * hidden, 16 << 20),
    )(me, vectors, unit, own, got, cot, slope, *sources)


def first_backward_kernel(
    mixed_ref, own_ref, got_ref, unit_ref, scale_ref, gain_ref, out_w_ref, *refs
):
    grad_out, low_out, ctx_out, sum_out = refs
    grad_normed = mixed_ref[...] + (own_ref[...].astype(F32) + got_ref[...].astype(F32))
    unit = unit_ref[...]
    grad = ln_backward(grad_normed, unit, scale_ref[...], gain_ref[...])
    low = grad.astype(BF)
    grad_out[...] = grad
    low_out[...] = low
    ctx_out[...] = dot(low, out_w_ref[...]).astype(BF)
    for i, value in enumerate((grad_normed * unit, grad_normed, grad)):
        sum_out[i : i + 1, :] = jnp.sum(value, axis=0, keepdims=True)


def first_backward(mixed, own, got, unit, scale, gain, full_attn):
    count, width = unit.shape
    local = full_attn.shape[1] // 4

    def whole(*shape):
        return pl.BlockSpec(shape, lambda i: (0, 0))

    return pl.pallas_call(
        first_backward_kernel,
        grid=(1,),
        out_shape=[
            jax.ShapeDtypeStruct((count, width), F32),
            jax.ShapeDtypeStruct((count, width), BF),
            jax.ShapeDtypeStruct((count, local), BF),
            jax.ShapeDtypeStruct((3, width), F32),
        ],
        in_specs=[whole(count, width)] * 4
        + [whole(count, 1), whole(1, width), pl.BlockSpec((width, local), lambda i: (0, 3))],
        out_specs=[whole(count, width)] * 2 + [whole(count, local), whole(3, width)],
        compiler_params=PARAMS,
        cost_estimate=cost(2 * count * width * local, 6 << 20),
    )(mixed, own, got, unit, scale, gain[None], full_attn)


def pack_kernel(q_ref, k_ref, v_ref, o_ref, out_ref):
    local = q_ref.shape[1]
    for pair in range(local // 128):
        for i, ref in enumerate((q_ref, k_ref, v_ref)):
            col = 384 * pair + 128 * i
            out_ref[:, col : col + 128] = ref[:, 128 * pair : 128 * (pair + 1)]
    out_ref[:, 3 * local :] = o_ref[...]


def pack(w_query, w_key, w_value, w_output):
    rows, local = w_query.shape
    return pl.pallas_call(
        pack_kernel,
        out_shape=jax.ShapeDtypeStruct((rows, 4 * local), BF),
        in_specs=[VMEM] * 4,
        out_specs=VMEM,
        compiler_params=PARAMS,
    )(w_query, w_key, w_value, w_output)


def pair_major(parts):
    lead = parts[0].shape[:-1]
    stacked = jnp.stack([p.reshape(*lead, -1, 128) for p in parts], axis=-2)
    return stacked.reshape(*lead, -1)


def from_pair_major(array):
    lead = array.shape[:-1]
    stacked = array.reshape(*lead, -1, 3, 128)
    return [stacked[..., i, :].reshape(*lead, -1) for i in range(3)]


def tie(*arrays):
    return lax.optimization_barrier(arrays)


def ln_forward(values, gain, shift):
    centre = values - jnp.mean(values, axis=-1, keepdims=True)
    scale = lax.rsqrt(jnp.mean(centre * centre, axis=-1, keepdims=True) + NORM_EPS)
    unit = centre * scale
    return unit * gain + shift, unit, scale


def ln_backward(grad, unit, scale, gain):
    grad_unit = grad * gain
    along = jnp.mean(grad_unit * unit, axis=-1, keepdims=True)
    return scale * (grad_unit - jnp.mean(grad_unit, axis=-1, keepdims=True) - unit * along)


def ring_add_kernel(ahead_ref, behind_ref, up_ref, down_ref, up_out, down_out):
    rows = up_ref.shape[0]
    start = ahead_ref.shape[1] - rows
    for own, got, out, first in (
        (ahead_ref, up_ref, up_out, 0),
        (behind_ref, down_ref, down_out, start),
    ):
        total = own[0, first : first + rows].astype(F32) + got[...].astype(F32)
        out[first : first + rows, :] = total.astype(BF)
        if start:
            rest = slice(rows, None) if first == 0 else slice(0, start)
            out[rest, :] = own[0, rest]


def ring_add(blocks, step, up, down):
    chips, rows, cols = blocks.shape

    def whole(shape):
        return pl.BlockSpec(shape, lambda i: (0, 0))

    return pl.pallas_call(
        ring_add_kernel,
        grid=(1,),
        in_specs=[
            pl.BlockSpec((1, rows, cols), lambda i: (step, 0, 0)),
            pl.BlockSpec((1, rows, cols), lambda i: (chips - step, 0, 0)),
            whole(up.shape),
            whole(down.shape),
        ],
        out_specs=[whole((rows, cols))] * 2,
        out_shape=[jax.ShapeDtypeStruct((rows, cols), BF)] * 2,
        compiler_params=PARAMS,
        cost_estimate=cost(0, 10 * rows * cols),
    )(blocks, blocks, up, down)


class Links:
    def __init__(self):
        self.dp = lax.axis_size("dp")
        self.tensor = lax.axis_size("tensor")
        self.chips = self.dp // 2
        self.half_way = self.chips // 2
        self.order = list(range(0, self.chips, 2)) + list(range(1, self.chips, 2))[::-1]
        self.place = lax.axis_index("dp").astype(jnp.int32)
        self.core = self.place % 2
        self.me = self.place.reshape(1)

    def swap_core(self, array):
        return self.swap_dp(array, 1)

    def swap_dp(self, array, bit):
        return lax.ppermute(array, "dp", [(i, i ^ bit) for i in range(self.dp)])

    def swap_tensor(self, array, bit):
        return lax.ppermute(array, "tensor", [(i, i ^ bit) for i in range(self.tensor)])

    def along_ring(self, array, step):
        pairs = [
            (2 * self.order[i] + c, 2 * self.order[(i + step) % self.chips] + c)
            for i in range(self.chips)
            for c in range(2)
        ]
        return lax.ppermute(array, "dp", pairs)

    def bits(self, size):
        return [1 << b for b in range((size - 1).bit_length())]

    def gather_blocks(self, block):
        blocks = [block]
        for bit in self.bits(self.tensor):
            blocks = blocks + [self.swap_tensor(b, bit) for b in blocks]
        return blocks

    def sum_blocks(self, blocks, order, tied=True):
        if self.tensor == 2:
            blocks, got = list(blocks), [None, None]
            first, second = order
            got[second] = self.swap_tensor(blocks[first], 1)
            if tied:
                blocks[second], got[second] = tie(blocks[second], got[second])
            got[first] = self.swap_tensor(blocks[second], 1)
            return list(zip(blocks, got))
        for bit in self.bits(self.tensor):
            low = [b.astype(BF) for b in blocks]
            got = [self.swap_tensor(low[j ^ bit], bit) for j in range(len(low))]
            blocks = [a.astype(F32) + b.astype(F32) for a, b in zip(low, got)]
        return list(zip(low, got))

    def scatter_blocks(self, blocks):
        for bit in self.bits(self.tensor)[::-1]:
            got = [self.swap_tensor(blocks[j + bit].astype(BF), bit) for j in range(bit)]
            blocks = [blocks[j].astype(F32) + got[j].astype(F32) for j in range(bit)]
        return blocks[0]

    def sum_small(self, vector, axis):
        rows = vector.reshape(-1, 128)
        swap, size = (
            (self.swap_tensor, self.tensor) if axis == "tensor" else (self.swap_dp, self.dp)
        )
        for bit in self.bits(size):
            rows = rows + swap(rows, bit)
        return rows.reshape(vector.shape)

    def sum_near(self, rows):
        for bit in self.bits(self.dp)[:2]:
            rows = rows + self.swap_dp(rows, bit)
        return rows

    def sum_far(self, rows):
        far = [rows] + [self.swap_dp(rows, bit) for bit in range(4, self.dp, 4)]
        while len(far) > 1:
            far = [a + b for a, b in zip(far[::2], far[1::2])]
        return far[0]

    def own_half(self, array):
        half = array.shape[1] // 2
        return lax.dynamic_slice_in_dim(array, half * self.core, half, 1)

    def give_half(self, array):
        half = array.shape[1] // 2
        return self.swap_core(
            lax.dynamic_slice_in_dim(array, half * (1 - self.core), half, 1)
        )

    def swap_halves(self, total):
        rows = total.shape[0] // 2
        mine = lax.dynamic_slice_in_dim(total, rows * self.core, rows, 0)
        other = lax.dynamic_slice_in_dim(total, rows * (1 - self.core), rows, 0)
        got = self.swap_core(other.astype(BF)).astype(F32)
        return mine, got

    def in_order(self, mine, got):
        first = self.core == 0
        return jnp.concatenate(
            [jnp.where(first, mine, got), jnp.where(first, got, mine)], axis=1
        )


class Gather:
    def __init__(self, links, shard):
        self.links = links
        self.rows = shard.shape[0]
        self.up = self.down = shard
        self.plan, self.pieces, self.step = [], [], 0
        self.arrive(shard, 0, 0)

    def arrive(self, block, distance, row):
        self.plan += [(distance, 0, row), (distance, 1, row)]
        self.pieces += [block, self.links.swap_core(block)]

    def hops(self):
        for _ in range(max(1, self.links.half_way // 4)):
            self.hop()

    def finish(self):
        while self.step < self.links.half_way:
            self.hop()

    def hop(self):
        if self.step == self.links.half_way:
            return
        self.step += 1
        half, last = self.rows // 2, self.step == self.links.half_way
        up, down = (self.up[:half], self.down[half:]) if last else (self.up, self.down)
        self.up = self.links.along_ring(up, 1)
        self.down = self.links.along_ring(down, -1)
        self.arrive(self.up, -self.step, 0)
        self.arrive(self.down, self.step, half if last else 0)

    def land(self, *arrays):
        out = tie(self.up, self.down, *arrays)
        self.up, self.down = out[:2]
        if self.step:
            self.pieces[-2], self.pieces[-4] = self.down, self.up
        return out[2:] if len(arrays) > 1 else out[2]

    def full(self):
        return assemble(self.links.me, self.plan, self.pieces, self.rows, self.links.chips)


class Scatter:
    def __init__(self, links, blocks):
        self.links, self.blocks, self.step = links, blocks, links.half_way
        self.arrived = None
        self.rows = blocks.shape[1]
        far = blocks[self.step]
        self.up, self.down = far[: self.rows // 2], far[self.rows // 2 :]

    def hops(self):
        for _ in range(max(1, self.links.half_way // 4)):
            self.hop()

    def finish(self):
        while self.step:
            self.hop()

    def hop(self):
        if not self.step:
            return
        links = self.links
        self.ready()
        up, down = links.along_ring(self.up, 1), links.along_ring(self.down, -1)
        self.step -= 1
        if self.step:
            self.arrived, self.up, self.down = (up, down), None, None
        else:
            self.up, self.down = up, down

    def ready(self):
        if self.up is None:
            self.up, self.down = ring_add(self.blocks, self.step, *self.arrived)

    def land(self, *arrays):
        moving = self.arrived if self.up is None else (self.up, self.down)
        out = tie(*moving, *arrays)
        if self.up is None:
            self.arrived = out[:2]
        else:
            self.up, self.down = out[:2]
        return out[2:] if len(arrays) > 1 else out[2]

    def total(self):
        self.finish()
        return self.blocks[0].astype(F32) + self.up.astype(F32) + self.down.astype(F32)


def add(a, b):
    return (a.astype(F32) + b.astype(F32)).astype(BF)


def gelu_pair(u):
    cdf = 0.5 * (1.0 + lax.erf(u * (0.5**0.5)))
    slope = cdf + u * jnp.exp(-0.5 * u * u) * 0.3989422804014327
    return u * cdf, slope


def shards(
    inputs,
    segments,
    w_query,
    w_key,
    w_value,
    w_output,
    w_expand,
    w_reduce,
    query_bias_vector,
    b_value,
    b_output,
    b_expand,
    b_reduce,
    gain_first,
    shift_first,
    gain_second,
    shift_second,
    cotangent,
):
    links = Links()
    parts = links.tensor
    rank = lax.axis_index("tensor")
    seqs, span, width = inputs.shape
    local = w_query.shape[1]
    hidden = w_expand.shape[1]
    length = span * parts
    chips = links.chips

    def flat(block):
        return block.reshape(seqs * span, block.shape[-1])

    def joined(blocks):
        return jnp.concatenate(
            [b.reshape(seqs, span, b.shape[-1]) for b in blocks], axis=1
        ).reshape(seqs * length, -1)

    def split(array):
        array = array.reshape(seqs, length, -1)
        return [flat(array[:, j * span : (j + 1) * span]) for j in range(parts)]

    attn = Gather(links, pack(w_query, w_key, w_value, w_output.T))
    attn.hops()
    token_blocks = [flat(b) for b in links.gather_blocks(inputs)]
    token_blocks[-1] = attn.land(token_blocks[-1])
    attn.hops()
    ffn_shard, cotangent, token_blocks[-1] = attn.land(
        jnp.concatenate([w_expand, w_reduce.T], axis=1), cotangent, token_blocks[-1]
    )
    attn.hops()
    cotangent_blocks = [flat(b) for b in links.gather_blocks(cotangent)]
    ffn_shard = attn.land(ffn_shard)
    attn.finish()
    ffn = Gather(links, ffn_shard)
    ffn.hops()

    labels = jnp.concatenate(
        [
            lax.dynamic_slice_in_dim(segments, span * (rank ^ j), span, 1)
            for j in range(parts)
        ],
        axis=1,
    )
    tokens = token_blocks if seqs == 1 else [joined(token_blocks)]
    tokens_pair = [links.swap_core(t) for t in tokens]

    qkv_bias = pair_major([query_bias_vector, jnp.zeros_like(b_value), b_value])
    full_attn, qkv = project(
        links.me, attn.plan, attn.pieces, attn.rows, chips, tokens, qkv_bias[None]
    )
    ffn.hops()
    context, lse, partial = attend_forward(qkv, labels, full_attn, parts)
    partial = list(partial)
    cotangent_blocks[-1], partial[-1] = tie(cotangent_blocks[-1], partial[-1])
    partial[0] = ffn.land(partial[0])
    sums = links.sum_blocks(partial, range(parts)[::-1], tied=False)
    ffn.hops()
    sums[0] = (sums[0][0], ffn.land(sums[0][1]))
    ffn.finish()

    weights = None
    units, scales, normed_low, activated, slopes, partial = [], [], [], [], [], []
    for tok, (own, got) in zip(token_blocks, sums):
        weights, (unit, low, act, act_give, slope, scale, part) = ffn_forward(
            links.me, ffn, weights, chips, tok, own, got, b_output, gain_first, shift_first, b_expand
        )
        units.append(unit)
        scales.append(scale)
        normed_low.append(low)
        activated.append((act, act_give))
        slopes.append(slope)
        partial.append(part)

    sums = links.sum_blocks(partial, range(parts), tied=False)
    vectors = jnp.stack([gain_first, shift_first, b_reduce, gain_second, shift_second])
    grad_mixed, reduce_in, expand_low, partial = ([None] * parts for _ in range(4))
    grad_b_expand, small = 0.0, {}
    for j in range(parts)[::-1]:
        own, got = sums[j]
        out, grad, low, wide, wide_give, part, sums_mixed, sums_wide = ffn_backward(
            links.me, ffn, weights, chips, units[j], own, got, cotangent_blocks[j], slopes[j], vectors
        )
        if j == 0:
            result = out.reshape(seqs, span, width)
            small["gain_second"], small["shift_second"], small["b_reduce"] = sums_mixed
        grad_b_expand = grad_b_expand + sums_wide[0]
        grad_mixed[j], reduce_in[j], expand_low[j], partial[j] = (
            grad, low, (wide, wide_give), part,
        )

    def cut_cores(wide, narrow):
        return [(w, n, False, 0) for w, (n, _) in zip(wide, narrow)] + [
            (links.swap_core(w), links.swap_core(n), False, 0)
            for w, (_, n) in zip(wide, narrow)
        ]

    def both_cores(wide, narrow):
        return [(w, n, True, 0) for w, n in zip(wide, narrow)] + [
            (links.swap_core(w), links.give_half(n), False, 0) for w, n in zip(wide, narrow)
        ]

    def rows_of(wide, narrow):
        pair = links.give_half(narrow)
        return [(w, narrow, True, j) for j, w in enumerate(wide)] + [
            (w, pair, False, j) for j, w in enumerate([links.swap_core(w) for w in wide])
        ]

    sums = links.sum_blocks(partial, range(parts)[::-1])
    grad_attended, attn_low, grad_context = [], [], []

    def first(j):
        grad, low, grad_ctx, sums_first = first_backward(
            grad_mixed[j], *sums[j], units[j], scales[j], gain_first, full_attn
        )
        if j == 0:
            small["gain_first"], small["shift_first"], small["b_output"] = sums_first
        grad_attended.append(grad)
        attn_low.append(low)
        grad_context.append(grad_ctx)

    first(0)
    names = ("b_output", "b_reduce", "gain_first", "shift_first", "gain_second", "shift_second")
    early = links.sum_small(jnp.stack([small[k] for k in names]), "tensor")
    terms = [cut_cores(reduce_in, activated), cut_cores(normed_low, expand_low)]
    wide, grad_context[0] = tie(terms[0][0][0], grad_context[0])
    terms[0][0] = (wide, *terms[0][0][1:])
    blocks = pair_grads(links.me, chips, terms)
    last = sums[parts - 1]
    blocks, early, got = tie(blocks, early, last[1])
    sums[parts - 1] = (last[0], got)
    ffn_sum = Scatter(links, blocks)
    ffn_sum.hops()
    for j in range(1, parts):
        first(j)
    grad_context[-1] = ffn_sum.land(grad_context[-1])
    ffn_sum.hops()
    grad_qkv, bias_sums, give, back_low = attend_backward(
        links.me, qkv, labels, lse, full_attn, grad_context
    )
    grad_qkv, bias_sums = ffn_sum.land(grad_qkv, bias_sums)
    vector = jnp.concatenate([early.reshape(-1), grad_b_expand, bias_sums]).reshape(-1, 128)
    vector = links.sum_near(vector)
    ffn_sum.hops()
    pair = links.give_half(grad_qkv) if give is None else links.swap_core(give)
    if seqs == 1:
        context_terms = rows_of(attn_low, context)
        qkv_terms = [(t, grad_qkv, True, j) for j, t in enumerate(tokens)] + [
            (t, pair, False, j) for j, t in enumerate(tokens_pair)
        ]
    else:
        context_terms = both_cores(attn_low, split(context))
        qkv_terms = [
            (tokens[0], grad_qkv, True, 0),
            (tokens_pair[0], pair, False, 0),
        ]
    blocks = pair_grads(links.me, chips, [qkv_terms, context_terms])
    blocks, vector = ffn_sum.land(blocks, vector)
    attn_sum = Scatter(links, blocks)
    attn_sum.hops()
    ffn_sum.finish()
    vector = links.sum_far(vector)
    back_low[-1] = attn_sum.land(back_low[-1])
    attn_sum.hops()
    grad_inputs = grad_attended[0] + links.scatter_blocks(back_low)
    vector = attn_sum.land(vector)
    attn_sum.hops()
    grad_inputs = attn_sum.land(grad_inputs)
    attn_sum.finish()
    vector = vector.reshape(-1)
    mine, got = links.swap_halves(ffn_sum.total())
    half_hidden, half_local = hidden // 2, local // 2
    grad_reduce = links.in_order(mine[:, :half_hidden], got[:, :half_hidden])
    grad_expand = links.in_order(mine[:, half_hidden:], got[:, half_hidden:])
    mine, got = links.swap_halves(attn_sum.total())
    grad_wq, grad_wk, grad_wv = from_pair_major(
        links.in_order(mine[:, : 3 * half_local], got[:, : 3 * half_local])
    )
    grad_output = links.in_order(mine[:, 3 * half_local :], got[:, 3 * half_local :])

    early = vector[: 6 * width].reshape(6, width)
    middle = vector[6 * width : 6 * width + hidden]
    grad_bq, _, grad_bv = from_pair_major(vector[6 * width + hidden :])
    return (
        result,
        grad_inputs.reshape(seqs, span, width),
        grad_wq,
        grad_wk,
        grad_wv,
        grad_output.T,
        grad_expand,
        grad_reduce.T,
        grad_bq,
        grad_bv,
        early[0],
        middle,
        early[1],
        early[2],
        early[3],
        early[4],
        early[5],
    )


def solution(mesh):
    return jax.shard_map(
        shards,
        mesh=mesh,
        in_specs=(
            P("dp", "tensor", None),
            P("dp", None),
            P("dp", "tensor"),
            P("dp", "tensor"),
            P("dp", "tensor"),
            P("tensor", "dp"),
            P("dp", "tensor"),
            P("tensor", "dp"),
            P("tensor"),
            P("tensor"),
            P(),
            P("tensor"),
            P(),
            P(),
            P(),
            P(),
            P(),
            P("dp", "tensor", None),
        ),
        out_specs=(
            P("dp", "tensor", None),
            P("dp", "tensor", None),
            P("dp", "tensor"),
            P("dp", "tensor"),
            P("dp", "tensor"),
            P("tensor", "dp"),
            P("dp", "tensor"),
            P("tensor", "dp"),
            P("tensor"),
            P("tensor"),
            P(),
            P("tensor"),
            P(),
            P(),
            P(),
            P(),
            P(),
        ),
        check_vma=False,
    )
```

```python
import functools

import jax
import jax.numpy as jnp
from jax import lax
from jax.experimental import pallas as pl
from jax.experimental.pallas import tpu as pltpu
from jax.sharding import PartitionSpec as P

HD = 64
NORM_EPS = 1e-05
MASKED = -1e30
BF = jnp.bfloat16
F32 = jnp.float32
PARAMS = pltpu.CompilerParams(vmem_limit_bytes=60 << 20)
VMEM = pl.BlockSpec(memory_space=pltpu.VMEM)
SMEM = pl.BlockSpec(memory_space=pltpu.SMEM)
ANY = pl.BlockSpec(memory_space=pltpu.HBM)


def dot(a, b):
    return lax.dot_general(a, b, (((1,), (0,)), ((), ())), preferred_element_type=F32)


def dot_nt(a, b):
    return lax.dot_general(a, b, (((1,), (1,)), ((), ())), preferred_element_type=F32)


def dot_tn(a, b):
    return lax.dot_general(a, b, (((0,), (0,)), ((), ())), preferred_element_type=F32)


def cost(flops, nbytes):
    return pl.CostEstimate(flops=flops // 1024, bytes_accessed=nbytes // 1024, transcendentals=0)


def lane_half(array, head):
    lanes = lax.broadcasted_iota(jnp.int32, array.shape, 1)
    return jnp.where((lanes < HD) == (head == 0), array, jnp.zeros_like(array))


def column_of(row):
    return jnp.broadcast_to(row, (128, row.shape[1])).T[:, :1]


def attend_forward_kernel(parts, qkv_ref, row_ref, out_w_ref, *refs):
    ctx_ref, lse_ref, part_refs, scratch = refs[0], refs[1], refs[2 : 2 + parts], refs[-1]
    query, key, value = (qkv_ref[:, i * 128 : (i + 1) * 128] for i in range(3))
    same = column_of(row_ref[0]) == row_ref[0]
    query = query * jnp.asarray(HD**-0.5, BF)
    value_t = value.T
    out = []
    for head in range(2):
        scores = dot_nt(key, lane_half(query, head))
        scores = jnp.where(same, scores, MASKED)
        top = jnp.max(scores, axis=0, keepdims=True)
        weights = jnp.exp(scores - top)
        total = jnp.sum(weights, axis=0, keepdims=True)
        probs = (weights * (1.0 / total)).astype(BF)
        lse_ref[0, head : head + 1, :] = top + jnp.log(total)
        out.append(dot(value_t[head * HD : (head + 1) * HD], probs))
    context = jnp.concatenate(out, axis=0).T.astype(BF)
    ctx_ref[...] = context
    pair, pairs = pl.program_id(1), pl.num_programs(1)
    scratch[pair] = context

    @pl.when(pair == pairs - 1)
    def _():
        span = part_refs[0].shape[0]
        whole = jnp.concatenate([scratch[i] for i in range(scratch.shape[0])], axis=1)
        for j, part_ref in enumerate(part_refs):
            part_ref[...] = dot_nt(whole[j * span : (j + 1) * span], out_w_ref[...]).astype(BF)


def attend_forward(qkv, rows, full_attn, parts):
    seqs, _, length = rows.shape
    pairs = qkv.shape[1] // 384
    local, width, span = 128 * pairs, full_attn.shape[0], length // parts
    out = pl.pallas_call(
        functools.partial(attend_forward_kernel, parts),
        grid=(seqs, pairs),
        in_specs=[
            pl.BlockSpec((length, 384), lambda s, p: (s, p)),
            pl.BlockSpec((1, 1, length), lambda s, p: (s, 0, 0)),
            pl.BlockSpec((width, local), lambda s, p: (0, 3)),
        ],
        out_specs=[
            pl.BlockSpec((length, 128), lambda s, p: (s, p)),
            pl.BlockSpec((1, 2, length), lambda s, p: (s * pairs + p, 0, 0)),
        ]
        + [pl.BlockSpec((span, width), lambda s, p: (s, 0))] * parts,
        out_shape=[
            jax.ShapeDtypeStruct((seqs * length, local), BF),
            jax.ShapeDtypeStruct((seqs * pairs, 2, length), F32),
        ]
        + [jax.ShapeDtypeStruct((seqs * span, width), BF)] * parts,
        scratch_shapes=[pltpu.VMEM((pairs, length, 128), BF)],
        compiler_params=PARAMS,
        cost_estimate=cost(seqs * pairs * 24 * 128 * length * length, 8 << 20),
    )(qkv, rows, full_attn)
    return out[0], out[1], out[2:]


def attend_backward_body(qkv_ref, row_ref, lse_ref, w_ref, parts, *refs):
    out_ref, sum_ref = refs[parts : parts + 2]
    query, key, value = (qkv_ref[:, i * 128 : (i + 1) * 128] for i in range(3))
    grad_ctx = jnp.concatenate([ref[...] for ref in refs[:parts]], axis=0)
    same = column_of(row_ref[0]) == row_ref[0]
    small_query = query * jnp.asarray(HD**-0.5, BF)
    key_t = key.T
    grad_q, grad_k, grad_v = [], [], []
    for head in range(2):
        scores = dot_nt(key, lane_half(small_query, head))
        probs = jnp.exp(jnp.where(same, scores, MASKED) - lse_ref[0, head : head + 1, :])
        grad_probs = dot_nt(value, lane_half(grad_ctx, head))
        inner = jnp.sum(probs * grad_probs, axis=0, keepdims=True)
        grad_scores = (probs * (grad_probs - inner)).astype(BF)
        grad_q.append(dot(key_t[head * HD : (head + 1) * HD], grad_scores))
        grad_k.append(dot(grad_scores, query))
        grad_v.append(dot(probs.astype(BF), grad_ctx))
    lanes = lax.broadcasted_iota(jnp.int32, grad_k[0].shape, 1) < HD
    factor = HD**-0.5
    outs = (
        jnp.concatenate(grad_q, axis=0).T * factor,
        jnp.where(lanes, grad_k[0], grad_k[1]) * factor,
        jnp.where(lanes, grad_v[0], grad_v[1]),
    )
    for i, value in enumerate(outs):
        low = value.astype(BF)
        out_ref[:, i * 128 : (i + 1) * 128] = low
        sum_ref[0, :, i * 128 : (i + 1) * 128] = jnp.sum(
            low.astype(F32), axis=0, keepdims=True
        )


def attend_backward_kernel(parts, halved, me_ref, qkv_ref, row_ref, lse_ref, w_ref, *refs):
    attend_backward_body(qkv_ref, row_ref, lse_ref, w_ref, parts, *refs)
    out_ref, back_refs, total = refs[parts], refs[parts + 2 : 2 * parts + 2], refs[-1]
    pair, pairs = pl.program_id(1), pl.num_programs(1)
    part = dot_nt(out_ref[...], w_ref[...])

    @pl.when(pair == 0)
    def _():
        total[...] = part

    @pl.when(pair != 0)
    def _():
        total[...] += part

    @pl.when(pair == pairs - 1)
    def _():
        span = back_refs[0].shape[0]
        for j, ref in enumerate(back_refs):
            ref[...] = total[j * span : (j + 1) * span, :].astype(ref.dtype)

    if halved:
        give_ref = refs[2 * parts + 2]

        @pl.when(pair // (pairs // 2) == 1 - me_ref[0] % 2)
        def _():
            give_ref[...] = out_ref[...]


def attend_backward(me, qkv, rows, lse, full_attn, grad_ctx):
    seqs, _, length = rows.shape
    pairs = qkv.shape[1] // 384
    half = pairs // 2
    parts = len(grad_ctx)
    span, width = length // parts, full_attn.shape[0]
    kernel = functools.partial(attend_backward_kernel, parts, half > 0)

    def give_place(s, p, m):
        return s, jnp.clip(p - half * (1 - m[0] % 2), 0, max(half - 1, 0))

    out = pl.pallas_call(
        kernel,
        grid_spec=pltpu.PrefetchScalarGridSpec(
            num_scalar_prefetch=1,
            grid=(seqs, pairs),
            in_specs=[
                pl.BlockSpec((length, 384), lambda s, p, m: (s, p)),
                pl.BlockSpec((1, 1, length), lambda s, p, m: (s, 0, 0)),
                pl.BlockSpec((1, 2, length), lambda s, p, m: (s * pairs + p, 0, 0)),
                pl.BlockSpec((width, 384), lambda s, p, m: (0, p)),
            ]
            + [
                pl.BlockSpec((length // len(grad_ctx), 128), lambda s, p, m: (s, p))
                for _ in grad_ctx
            ],
            out_specs=[
                pl.BlockSpec((length, 384), lambda s, p, m: (s, p)),
                pl.BlockSpec((1, 1, 384), lambda s, p, m: (s, 0, p)),
            ]
            + [pl.BlockSpec((span, width), lambda s, p, m: (s, 0))] * parts
            + ([pl.BlockSpec((length, 384), give_place)] if half else []),
            scratch_shapes=[pltpu.VMEM((length, width), F32)],
        ),
        out_shape=[
            jax.ShapeDtypeStruct(qkv.shape, BF),
            jax.ShapeDtypeStruct((seqs, 1, qkv.shape[1]), F32),
        ]
        + [jax.ShapeDtypeStruct((seqs * span, width), BF if j else F32) for j in range(parts)]
        + ([jax.ShapeDtypeStruct((qkv.shape[0], 384 * half), BF)] if half else []),
        compiler_params=PARAMS,
        cost_estimate=cost(seqs * pairs * 40 * 128 * length * length, 8 << 20),
    )(me, qkv, rows, lse, full_attn, *grad_ctx)
    bias = jnp.sum(out[1], axis=(0, 1))
    return out[0], bias, out[-1] if half else None, list(out[2 : 2 + parts])


def ring_chip(place, chips):
    return jnp.where(place < chips // 2, 2 * place, 2 * (chips - 1 - place) + 1)


def ring_place(chip, chips):
    return jnp.where(chip % 2 == 0, chip // 2, chips - 1 - chip // 2)


def chip_at(me, distance, chips):
    return ring_chip((ring_place(me // 2, chips) + distance + chips) % chips, chips)


def gathered_rows(me, plan, rows, chips):
    out = []
    for distance, other, row in plan:
        core = me % 2
        owner = 2 * chip_at(me, distance, chips) + (1 - core if other else core)
        out.append(pl.multiple_of(owner * rows + row, 16))
    return out


def place_pieces(me, plan, rows, chips, pieces, out, sem):
    copies = [
        pltpu.make_async_copy(piece, out.at[pl.ds(row, piece.shape[0]), :], sem.at[i])
        for i, (piece, row) in enumerate(
            zip(pieces, gathered_rows(me, plan, rows, chips))
        )
    ]
    for copy in copies:
        copy.start()
    for copy in copies:
        copy.wait()


def assemble_kernel(plan, rows, chips, me_ref, *refs):
    pieces, out, sem = refs[: len(plan)], refs[-2], refs[-1]
    place_pieces(me_ref[0], plan, rows, chips, pieces, out, sem)


def assemble(me, plan, pieces, rows, chips):
    cols = pieces[0].shape[1]
    return pl.pallas_call(
        functools.partial(assemble_kernel, plan, rows, chips),
        out_shape=jax.ShapeDtypeStruct((2 * chips * rows, cols), BF),
        in_specs=[SMEM] + [ANY] * len(plan),
        out_specs=VMEM,
        scratch_shapes=[pltpu.SemaphoreType.DMA((len(plan),))],
        compiler_params=PARAMS,
        cost_estimate=cost(0, 8 * chips * rows * cols),
    )(me, *pieces)


def project_kernel(plan, rows, chips, parts, me_ref, bias_ref, *refs):
    blocks, pieces = refs[:parts], refs[parts : parts + len(plan)]
    full_out, out, full, sem, out_sem = refs[parts + len(plan) :]
    place_pieces(me_ref[0], plan, rows, chips, pieces, full, sem)
    copy = pltpu.make_async_copy(full, full_out, out_sem)
    copy.start()
    cols = out.shape[1]
    count = blocks[0].shape[0]
    for i, block in enumerate(blocks):
        for start in range(0, cols, 384):
            out[i * count : (i + 1) * count, start : start + 384] = (
                dot(block[...], full[:, start : start + 384])
                + bias_ref[:, start : start + 384]
            ).astype(BF)
    copy.wait()


def project(me, plan, pieces, rows, chips, blocks, bias):
    cols, wide = pieces[0].shape[1], bias.shape[1]
    count, width = blocks[0].shape
    tokens = count * len(blocks)
    return pl.pallas_call(
        functools.partial(project_kernel, plan, rows, chips, len(blocks)),
        out_shape=[
            jax.ShapeDtypeStruct((width, cols), BF),
            jax.ShapeDtypeStruct((tokens, wide), BF),
        ],
        in_specs=[SMEM, VMEM] + [VMEM] * len(blocks) + [ANY] * len(plan),
        out_specs=[ANY, VMEM],
        scratch_shapes=[
            pltpu.VMEM((width, cols), BF),
            pltpu.SemaphoreType.DMA((len(plan),)),
            pltpu.SemaphoreType.DMA,
        ],
        compiler_params=PARAMS,
        cost_estimate=cost(2 * tokens * width * wide, 8 * width * cols),
    )(me, bias, *blocks, *pieces)


def grad_kernel(chips, sources, terms, me_ref, *refs):
    scratch, out = refs[-1], refs[-2]
    d = 2 * pl.program_id(0)
    rows = out.shape[1]
    k = 0
    for col, term in zip(terms, sources):
        total = None
        for _ in range(term):
            pair = jnp.concatenate([refs[k][...], refs[k + 1][...]], axis=1)
            product = dot_tn(pair, refs[k + 2][...])
            total = product if total is None else total + product
            k += 3
        cols = slice(col, col + total.shape[1])
        if total.shape[0] == 2 * rows:
            out[0, :, cols] = total[:rows].astype(BF)
            out[1, :, cols] = total[rows:].astype(BF)
        else:
            lanes = total.shape[0] // 2
            scratch[:, cols] = total
            for i in range(2):
                off = lanes * i + (chip_at(me_ref[0], d + i, chips) * rows) % lanes
                out[i, :, cols] = scratch[pl.ds(pl.multiple_of(off, 32), rows), cols].astype(BF)


def pair_grads(me, chips, terms):
    width = terms[0][0][0].shape[1]
    rows = width // chips
    lanes = max(rows, 128)
    specs, arrays, cols, sources, start, flops = [], [], [], [], 0, 0
    for term in terms:
        cols.append(start)
        sources.append(len(term))
        for wide, narrow, both, row in term:
            count, most = wide.shape[0], narrow.shape[1]
            half = most // 2 if both else most
            if both and half % 128:
                narrow = lax.dynamic_slice_in_dim(narrow, half * (me[0] % 2), half, 1)
                both = False
            specs += [
                pl.BlockSpec(
                    (count, lanes),
                    lambda d, m, i=i: (0, chip_at(m[0], 2 * d + i, chips) * rows // lanes),
                )
                for i in range(2)
            ] + [
                pl.BlockSpec(
                    (count, half),
                    lambda d, m, both=both, row=row: (row, m[0] % 2 if both else 0),
                ),
            ]
            arrays += [wide, wide, narrow]
            flops += 2 * count * width * half
        start += half
    return pl.pallas_call(
        functools.partial(grad_kernel, chips, sources, cols),
        grid_spec=pltpu.PrefetchScalarGridSpec(
            num_scalar_prefetch=1,
            grid=(chips // 2,),
            in_specs=specs,
            out_specs=pl.BlockSpec((2, rows, start), lambda d, m: (d, 0, 0)),
            scratch_shapes=[pltpu.VMEM((2 * lanes, start if lanes > rows else 128), F32)],
        ),
        out_shape=jax.ShapeDtypeStruct((chips, rows, start), BF),
        compiler_params=PARAMS,
        cost_estimate=cost(flops, 8 << 20),
    )(me, *arrays)


def start_all(pairs, sem):
    copies = [
        pltpu.make_async_copy(source, target, sem.at[i])
        for i, (source, target) in enumerate(pairs)
    ]
    for copy in copies:
        copy.start()
    return copies


def wait_all(copies):
    for copy in copies:
        copy.wait()


def start_weights(me, plan, rows, chips, sources, which, out, sem):
    wide = out.shape[1]
    if plan is None:
        half = wide // 2
        return [
            start_all(
                [(sources[which].at[:, k : k + half], out.at[:, k : k + half])],
                sem.at[pl.ds(k // half, 1)],
            )
            for k in (0, half)
        ]
    return [
        start_all(
            [
                (
                    piece.at[:, which * wide : (which + 1) * wide],
                    out.at[pl.ds(row, piece.shape[0]), :],
                )
                for piece, row in zip(sources, gathered_rows(me, plan, rows, chips))
            ],
            sem,
        )
    ]


def halves(me, kept, own, give):
    wide = own.shape[1]
    core = me % 2
    return [
        (kept.at[:, pl.ds(pl.multiple_of(wide * core, 128), wide)], own),
        (kept.at[:, pl.ds(pl.multiple_of(wide * (1 - core), 128), wide)], give),
    ]


def ffn_forward_kernel(plan, rows, chips, me_ref, bias_o, gain, shift, bias_e, *refs):
    count = 2 if plan is None else len(plan)
    ins, pieces, refs = refs[:3], refs[3 : 3 + count], refs[3 + count :]
    unit_out, low_out, own_out, give_out, slope_out = refs[:5]
    kept_out, refs = ((), refs) if plan is None else (refs[5:7], refs[2:])
    scale_out, part_out, refs = refs[5], refs[6], refs[7:]
    (
        tok, own, got, expand, reduce, unit_keep, low_keep, act_keep, slope_keep,
        sem, expand_sem, reduce_sem, out_sem,
    ) = refs
    me = me_ref[0]
    hidden = act_keep.shape[1]
    loads = start_all(zip(ins, (tok, own, got)), sem)
    expand_loads = start_weights(me, plan, rows, chips, pieces, 0, expand, expand_sem)
    reduce_loads = start_weights(me, plan, rows, chips, pieces, 1, reduce, reduce_sem)
    wait_all(loads)
    normed, unit, scale = ln_forward(
        tok[...].astype(F32) + (own[...].astype(F32) + got[...].astype(F32)) + bias_o[...],
        gain[...],
        shift[...],
    )
    scale_out[...] = scale
    unit_keep[...] = unit
    low_keep[...] = normed.astype(BF)
    copies = start_all([(unit_keep, unit_out), (low_keep, low_out)], out_sem)
    parts = len(expand_loads)
    step = min(512, hidden // parts)
    for start in range(0, hidden, step):
        if start % (hidden // parts) == 0:
            wait_all(expand_loads[start * parts // hidden])
        cols = slice(start, start + step)
        act, slope = gelu_pair(dot(low_keep[...], expand[:, cols]) + bias_e[:, cols])
        act_keep[:, cols] = act.astype(BF)
        slope_keep[:, cols] = slope.astype(BF)
    copies += start_all(
        halves(me, act_keep, own_out, give_out) + [(slope_keep, slope_out)],
        out_sem.at[pl.ds(2, 3)],
    )
    for load in reduce_loads:
        wait_all(load)
    if kept_out:
        copies += start_all(
            zip((expand, reduce), kept_out), out_sem.at[pl.ds(5, 2)]
        )
    part_out[...] = dot_nt(act_keep[...], reduce[...]).astype(BF)
    wait_all(copies)


def ffn_weights(ring, weights):
    if weights is None:
        return ring.plan, ring.pieces
    return None, weights


def ffn_scratch(sources, width, hidden):
    pieces = len(sources)
    return [pltpu.VMEM((width, hidden), BF)] * 2, [
        pltpu.SemaphoreType.DMA((pieces,)),
        pltpu.SemaphoreType.DMA((pieces,)),
    ]


def ffn_forward(me, ring, weights, chips, tok, own, got, bias_o, gain, shift, bias_e):
    count, width = tok.shape
    hidden = bias_e.shape[0]
    plan, sources = ffn_weights(ring, weights)
    scratch, sems = ffn_scratch(sources, width, hidden)
    kept = [] if weights else [jax.ShapeDtypeStruct((width, hidden), BF)] * 2
    out = pl.pallas_call(
        functools.partial(ffn_forward_kernel, plan, ring.rows, chips),
        out_shape=[
            jax.ShapeDtypeStruct((count, width), F32),
            jax.ShapeDtypeStruct((count, width), BF),
            jax.ShapeDtypeStruct((count, hidden // 2), BF),
            jax.ShapeDtypeStruct((count, hidden // 2), BF),
            jax.ShapeDtypeStruct((count, hidden), BF),
        ]
        + kept
        + [
            jax.ShapeDtypeStruct((count, 1), F32),
            jax.ShapeDtypeStruct((count, width), BF),
        ],
        in_specs=[SMEM] + [VMEM] * 4 + [ANY] * (3 + len(sources)),
        out_specs=[ANY] * (5 + len(kept)) + [VMEM] * 2,
        scratch_shapes=[pltpu.VMEM((count, width), BF)] * 3
        + scratch
        + [
            pltpu.VMEM((count, width), F32),
            pltpu.VMEM((count, width), BF),
            pltpu.VMEM((count, hidden), BF),
            pltpu.VMEM((count, hidden), BF),
            pltpu.SemaphoreType.DMA((3,)),
        ]
        + sems
        + [pltpu.SemaphoreType.DMA((5 + len(kept),))],
        compiler_params=PARAMS,
        cost_estimate=cost(8 * count * width * hidden, 16 << 20),
    )(me, bias_o[None], gain[None], shift[None], bias_e[None], tok, own, got, *sources)
    return weights or out[5:7], (*out[:5], *out[5 + len(kept) :])


def ffn_backward_kernel(plan, rows, chips, me_ref, vec_ref, *refs):
    count = 2 if plan is None else len(plan)
    ins, pieces = refs[:5], refs[5 : 5 + count]
    result_out, grad_out, low_out, own_out, give_out, part_out, sum_out, wide_out = refs[
        5 + count : 13 + count
    ]
    (
        unit_ref, own, got, cot_ref, slope, expand, reduce,
        result_keep, grad_keep, low_keep, wide_keep,
        sem, expand_sem, reduce_sem, out_sem,
    ) = refs[13 + count :]
    me = me_ref[0]
    hidden = wide_keep.shape[1]
    loads = start_all(zip(ins, (unit_ref, own, got, cot_ref, slope)), sem)
    reduce_loads = start_weights(me, plan, rows, chips, pieces, 1, reduce, reduce_sem)
    expand_loads = start_weights(me, plan, rows, chips, pieces, 0, expand, expand_sem)
    gain_first, shift_first, bias_r, gain, shift = (vec_ref[i : i + 1, :] for i in range(5))
    wait_all(loads)
    mixed = (
        unit_ref[...] * gain_first
        + shift_first
        + (own[...].astype(F32) + got[...].astype(F32))
        + bias_r
    )
    out, unit, scale = ln_forward(mixed, gain, shift)
    cot = cot_ref[...].astype(F32)
    grad = ln_backward(cot, unit, scale, gain)
    result_keep[...] = out.astype(BF)
    grad_keep[...] = grad
    low_keep[...] = grad.astype(BF)
    copies = start_all(
        [(result_keep, result_out), (grad_keep, grad_out), (low_keep, low_out)], out_sem
    )
    for i, value in enumerate((cot * unit, cot, grad)):
        sum_out[i : i + 1, :] = jnp.sum(value, axis=0, keepdims=True)
    parts = len(reduce_loads)
    step = min(512, hidden // parts)
    for start in range(0, hidden, step):
        if start % (hidden // parts) == 0:
            wait_all(reduce_loads[start * parts // hidden])
        cols = slice(start, start + step)
        low = (dot(low_keep[...], reduce[:, cols]) * slope[:, cols].astype(F32)).astype(BF)
        wide_keep[:, cols] = low
        wide_out[:, cols] = jnp.sum(low.astype(F32), axis=0, keepdims=True)
    copies += start_all(halves(me, wide_keep, own_out, give_out), out_sem.at[pl.ds(3, 2)])
    for load in expand_loads:
        wait_all(load)
    part_out[...] = dot_nt(wide_keep[...], expand[...]).astype(BF)
    wait_all(copies)


def ffn_backward(me, ring, weights, chips, unit, own, got, cot, slope, vectors):
    count, width = unit.shape
    hidden = slope.shape[1]
    plan, sources = ffn_weights(ring, weights)
    scratch, sems = ffn_scratch(sources, width, hidden)
    block = pltpu.VMEM((count, width), BF)
    wide = pltpu.VMEM((count, hidden), BF)
    return pl.pallas_call(
        functools.partial(ffn_backward_kernel, plan, ring.rows, chips),
        out_shape=[
            jax.ShapeDtypeStruct((count, width), BF),
            jax.ShapeDtypeStruct((count, width), F32),
            jax.ShapeDtypeStruct((count, width), BF),
            jax.ShapeDtypeStruct((count, hidden // 2), BF),
            jax.ShapeDtypeStruct((count, hidden // 2), BF),
            jax.ShapeDtypeStruct((count, width), BF),
            jax.ShapeDtypeStruct((3, width), F32),
            jax.ShapeDtypeStruct((1, hidden), F32),
        ],
        in_specs=[SMEM, VMEM] + [ANY] * (5 + len(sources)),
        out_specs=[ANY] * 5 + [VMEM] * 3,
        scratch_shapes=[pltpu.VMEM((count, width), F32), block, block, block, wide]
        + scratch
        + [
            block,
            pltpu.VMEM((count, width), F32),
            block,
            wide,
            pltpu.SemaphoreType.DMA((5,)),
        ]
        + sems
        + [pltpu.SemaphoreType.DMA((5,))],
        compiler_params=PARAMS,
        cost_estimate=cost(8 * count * width * hidden, 16 << 20),
    )(me, vectors, unit, own, got, cot, slope, *sources)


def first_backward_kernel(
    mixed_ref, own_ref, got_ref, unit_ref, scale_ref, gain_ref, out_w_ref, *refs
):
    grad_out, low_out, ctx_out, sum_out = refs
    grad_normed = mixed_ref[...] + (own_ref[...].astype(F32) + got_ref[...].astype(F32))
    unit = unit_ref[...]
    grad = ln_backward(grad_normed, unit, scale_ref[...], gain_ref[...])
    low = grad.astype(BF)
    grad_out[...] = grad
    low_out[...] = low
    ctx_out[...] = dot(low, out_w_ref[...]).astype(BF)
    for i, value in enumerate((grad_normed * unit, grad_normed, grad)):
        sum_out[i : i + 1, :] = jnp.sum(value, axis=0, keepdims=True)


def first_backward(mixed, own, got, unit, scale, gain, full_attn):
    count, width = unit.shape
    local = full_attn.shape[1] // 4

    def whole(*shape):
        return pl.BlockSpec(shape, lambda i: (0, 0))

    return pl.pallas_call(
        first_backward_kernel,
        grid=(1,),
        out_shape=[
            jax.ShapeDtypeStruct((count, width), F32),
            jax.ShapeDtypeStruct((count, width), BF),
            jax.ShapeDtypeStruct((count, local), BF),
            jax.ShapeDtypeStruct((3, width), F32),
        ],
        in_specs=[whole(count, width)] * 4
        + [whole(count, 1), whole(1, width), pl.BlockSpec((width, local), lambda i: (0, 3))],
        out_specs=[whole(count, width)] * 2 + [whole(count, local), whole(3, width)],
        compiler_params=PARAMS,
        cost_estimate=cost(2 * count * width * local, 6 << 20),
    )(mixed, own, got, unit, scale, gain[None], full_attn)


def unpack_kernel(me_ref, total_ref, got_ref, q_out, k_out, v_out, o_out):
    rows, half = got_ref.shape
    own = total_ref[pl.ds(pl.multiple_of(rows * (me_ref[0] % 2), rows), rows), :]
    wide = half * 3 // 4
    first = me_ref[0] % 2 == 0
    outs = (q_out, k_out, v_out)
    for part in range(2):
        mine, got = own, got_ref[...].astype(F32)
        block = jnp.where(first, mine, got) if part == 0 else jnp.where(first, got, mine)
        for col in range(0, wide, 128):
            pair, which = divmod(part * wide + col, 384)
            outs[which // 128][:, 128 * pair : 128 * (pair + 1)] = block[:, col : col + 128]
        o_out[:, part * (half - wide) : (part + 1) * (half - wide)] = block[:, wide:]


def unpack(me, total, got):
    rows, half = got.shape
    return pl.pallas_call(
        unpack_kernel,
        out_shape=[jax.ShapeDtypeStruct((rows, half // 2), F32)] * 4,
        in_specs=[SMEM, VMEM, VMEM],
        out_specs=[VMEM] * 4,
        compiler_params=PARAMS,
        cost_estimate=cost(0, 12 * rows * half),
    )(me, total, got)


def pack_kernel(q_ref, k_ref, v_ref, o_ref, out_ref):
    local = q_ref.shape[1]
    for pair in range(local // 128):
        for i, ref in enumerate((q_ref, k_ref, v_ref)):
            col = 384 * pair + 128 * i
            out_ref[:, col : col + 128] = ref[:, 128 * pair : 128 * (pair + 1)]
    out_ref[:, 3 * local :] = o_ref[...]


def pack(w_query, w_key, w_value, w_output):
    rows, local = w_query.shape
    return pl.pallas_call(
        pack_kernel,
        out_shape=jax.ShapeDtypeStruct((rows, 4 * local), BF),
        in_specs=[VMEM] * 4,
        out_specs=VMEM,
        compiler_params=PARAMS,
    )(w_query, w_key, w_value, w_output)


def pair_major(parts):
    lead = parts[0].shape[:-1]
    stacked = jnp.stack([p.reshape(*lead, -1, 128) for p in parts], axis=-2)
    return stacked.reshape(*lead, -1)


def from_pair_major(array):
    lead = array.shape[:-1]
    stacked = array.reshape(*lead, -1, 3, 128)
    return [stacked[..., i, :].reshape(*lead, -1) for i in range(3)]


def tie(*arrays):
    return lax.optimization_barrier(arrays)


def ln_forward(values, gain, shift):
    centre = values - jnp.mean(values, axis=-1, keepdims=True)
    scale = lax.rsqrt(jnp.mean(centre * centre, axis=-1, keepdims=True) + NORM_EPS)
    unit = centre * scale
    return unit * gain + shift, unit, scale


def ln_backward(grad, unit, scale, gain):
    grad_unit = grad * gain
    along = jnp.mean(grad_unit * unit, axis=-1, keepdims=True)
    return scale * (grad_unit - jnp.mean(grad_unit, axis=-1, keepdims=True) - unit * along)


def ring_add_kernel(ahead_ref, behind_ref, up_ref, down_ref, up_out, down_out):
    rows = up_ref.shape[0]
    start = ahead_ref.shape[1] - rows
    for own, got, out, first in (
        (ahead_ref, up_ref, up_out, 0),
        (behind_ref, down_ref, down_out, start),
    ):
        total = own[0, first : first + rows].astype(F32) + got[...].astype(F32)
        out[first : first + rows, :] = total.astype(BF)
        if start:
            rest = slice(rows, None) if first == 0 else slice(0, start)
            out[rest, :] = own[0, rest]


def ring_add(blocks, step, up, down):
    chips, rows, cols = blocks.shape

    def whole(shape):
        return pl.BlockSpec(shape, lambda i: (0, 0))

    return pl.pallas_call(
        ring_add_kernel,
        grid=(1,),
        in_specs=[
            pl.BlockSpec((1, rows, cols), lambda i: (step, 0, 0)),
            pl.BlockSpec((1, rows, cols), lambda i: (chips - step, 0, 0)),
            whole(up.shape),
            whole(down.shape),
        ],
        out_specs=[whole((rows, cols))] * 2,
        out_shape=[jax.ShapeDtypeStruct((rows, cols), BF)] * 2,
        compiler_params=PARAMS,
        cost_estimate=cost(0, 10 * rows * cols),
    )(blocks, blocks, up, down)


class Links:
    def __init__(self):
        self.dp = lax.axis_size("dp")
        self.tensor = lax.axis_size("tensor")
        self.chips = self.dp // 2
        self.half_way = self.chips // 2
        self.order = list(range(0, self.chips, 2)) + list(range(1, self.chips, 2))[::-1]
        self.place = lax.axis_index("dp").astype(jnp.int32)
        self.core = self.place % 2
        self.me = self.place.reshape(1)

    def swap_core(self, array):
        return self.swap_dp(array, 1)

    def swap_dp(self, array, bit):
        return lax.ppermute(array, "dp", [(i, i ^ bit) for i in range(self.dp)])

    def swap_tensor(self, array, bit):
        return lax.ppermute(array, "tensor", [(i, i ^ bit) for i in range(self.tensor)])

    def along_ring(self, array, step):
        pairs = [
            (2 * self.order[i] + c, 2 * self.order[(i + step) % self.chips] + c)
            for i in range(self.chips)
            for c in range(2)
        ]
        return lax.ppermute(array, "dp", pairs)

    def bits(self, size):
        return [1 << b for b in range((size - 1).bit_length())]

    def gather_blocks(self, block):
        blocks = [block]
        for bit in self.bits(self.tensor):
            blocks = blocks + [self.swap_tensor(b, bit) for b in blocks]
        return blocks

    def sum_blocks(self, blocks, order, tied=True):
        if self.tensor == 2:
            blocks, got = list(blocks), [None, None]
            first, second = order
            got[second] = self.swap_tensor(blocks[first], 1)
            if tied:
                blocks[second], got[second] = tie(blocks[second], got[second])
            got[first] = self.swap_tensor(blocks[second], 1)
            return list(zip(blocks, got))
        for bit in self.bits(self.tensor):
            low = [b.astype(BF) for b in blocks]
            got = [self.swap_tensor(low[j ^ bit], bit) for j in range(len(low))]
            blocks = [a.astype(F32) + b.astype(F32) for a, b in zip(low, got)]
        return list(zip(low, got))

    def scatter_blocks(self, blocks):
        for bit in self.bits(self.tensor)[::-1]:
            got = [self.swap_tensor(blocks[j + bit].astype(BF), bit) for j in range(bit)]
            blocks = [blocks[j].astype(F32) + got[j].astype(F32) for j in range(bit)]
        return blocks[0]

    def sum_small(self, vector, axis):
        rows = vector.reshape(-1, 128)
        swap, size = (
            (self.swap_tensor, self.tensor) if axis == "tensor" else (self.swap_dp, self.dp)
        )
        for bit in self.bits(size):
            rows = rows + swap(rows, bit)
        return rows.reshape(vector.shape)

    def sum_near(self, rows):
        for bit in self.bits(self.dp)[:2]:
            rows = rows + self.swap_dp(rows, bit)
        return rows

    def sum_far(self, rows):
        far = [rows] + [self.swap_dp(rows, bit) for bit in range(4, self.dp, 4)]
        while len(far) > 1:
            far = [a + b for a, b in zip(far[::2], far[1::2])]
        return far[0]

    def own_half(self, array):
        half = array.shape[1] // 2
        return lax.dynamic_slice_in_dim(array, half * self.core, half, 1)

    def give_half(self, array):
        half = array.shape[1] // 2
        return self.swap_core(
            lax.dynamic_slice_in_dim(array, half * (1 - self.core), half, 1)
        )

    def swap_halves(self, total):
        rows = total.shape[0] // 2
        mine = lax.dynamic_slice_in_dim(total, rows * self.core, rows, 0)
        return mine, self.get_rows(total).astype(F32)

    def get_rows(self, total):
        rows = total.shape[0] // 2
        other = lax.dynamic_slice_in_dim(total, rows * (1 - self.core), rows, 0)
        return self.swap_core(other.astype(BF))

    def in_order(self, mine, got):
        first = self.core == 0
        return jnp.concatenate(
            [jnp.where(first, mine, got), jnp.where(first, got, mine)], axis=1
        )


class Gather:
    def __init__(self, links, shard):
        self.links = links
        self.rows = shard.shape[0]
        self.up = self.down = shard
        self.plan, self.pieces, self.step = [], [], 0
        self.arrive(shard, 0, 0)

    def arrive(self, block, distance, row):
        self.plan += [(distance, 0, row), (distance, 1, row)]
        self.pieces += [block, self.links.swap_core(block)]

    def hops(self):
        for _ in range(max(1, self.links.half_way // 4)):
            self.hop()

    def finish(self):
        while self.step < self.links.half_way:
            self.hop()

    def hop(self):
        if self.step == self.links.half_way:
            return
        self.step += 1
        half, last = self.rows // 2, self.step == self.links.half_way
        up, down = (self.up[:half], self.down[half:]) if last else (self.up, self.down)
        self.up = self.links.along_ring(up, 1)
        self.down = self.links.along_ring(down, -1)
        self.arrive(self.up, -self.step, 0)
        self.arrive(self.down, self.step, half if last else 0)

    def land(self, *arrays):
        out = tie(self.up, self.down, *arrays)
        self.up, self.down = out[:2]
        if self.step:
            self.pieces[-2], self.pieces[-4] = self.down, self.up
        return out[2:] if len(arrays) > 1 else out[2]

    def full(self):
        return assemble(self.links.me, self.plan, self.pieces, self.rows, self.links.chips)


class Scatter:
    def __init__(self, links, blocks):
        self.links, self.blocks, self.step = links, blocks, links.half_way
        self.arrived = None
        self.rows = blocks.shape[1]
        far = blocks[self.step]
        self.up, self.down = far[: self.rows // 2], far[self.rows // 2 :]

    def hops(self):
        for _ in range(max(1, self.links.half_way // 4)):
            self.hop()

    def finish(self):
        while self.step:
            self.hop()

    def hop(self):
        if not self.step:
            return
        links = self.links
        self.ready()
        up, down = links.along_ring(self.up, 1), links.along_ring(self.down, -1)
        self.step -= 1
        if self.step:
            self.arrived, self.up, self.down = (up, down), None, None
        else:
            self.up, self.down = up, down

    def ready(self):
        if self.up is None:
            self.up, self.down = ring_add(self.blocks, self.step, *self.arrived)

    def land(self, *arrays):
        moving = self.arrived if self.up is None else (self.up, self.down)
        out = tie(*moving, *arrays)
        if self.up is None:
            self.arrived = out[:2]
        else:
            self.up, self.down = out[:2]
        return out[2:] if len(arrays) > 1 else out[2]

    def total(self):
        self.finish()
        return self.blocks[0].astype(F32) + self.up.astype(F32) + self.down.astype(F32)


def add(a, b):
    return (a.astype(F32) + b.astype(F32)).astype(BF)


def gelu_pair(u):
    cdf = 0.5 * (1.0 + lax.erf(u * (0.5**0.5)))
    slope = cdf + u * jnp.exp(-0.5 * u * u) * 0.3989422804014327
    return u * cdf, slope


def shards(
    inputs,
    segments,
    w_query,
    w_key,
    w_value,
    w_output,
    w_expand,
    w_reduce,
    query_bias_vector,
    b_value,
    b_output,
    b_expand,
    b_reduce,
    gain_first,
    shift_first,
    gain_second,
    shift_second,
    cotangent,
):
    links = Links()
    parts = links.tensor
    rank = lax.axis_index("tensor")
    seqs, span, width = inputs.shape
    local = w_query.shape[1]
    hidden = w_expand.shape[1]
    length = span * parts
    chips = links.chips

    def flat(block):
        return block.reshape(seqs * span, block.shape[-1])

    def joined(blocks):
        return jnp.concatenate(
            [b.reshape(seqs, span, b.shape[-1]) for b in blocks], axis=1
        ).reshape(seqs * length, -1)

    def split(array):
        array = array.reshape(seqs, length, -1)
        return [flat(array[:, j * span : (j + 1) * span]) for j in range(parts)]

    attn = Gather(links, pack(w_query, w_key, w_value, w_output.T))
    attn.hops()
    token_blocks = [flat(b) for b in links.gather_blocks(inputs)]
    labels = jnp.concatenate(
        [
            lax.dynamic_slice_in_dim(segments, span * (rank ^ j), span, 1)
            for j in range(parts)
        ],
        axis=1,
    )
    rows = labels[:, None, :]
    qkv_bias = pair_major([query_bias_vector, jnp.zeros_like(b_value), b_value])[None]
    token_blocks[-1], rows, qkv_bias = attn.land(token_blocks[-1], rows, qkv_bias)
    attn.hops()
    ffn_shard, cotangent, token_blocks[-1] = attn.land(
        jnp.concatenate([w_expand, w_reduce.T], axis=1), cotangent, token_blocks[-1]
    )
    attn.hops()
    cotangent_blocks = [flat(b) for b in links.gather_blocks(cotangent)]
    ffn_shard = attn.land(ffn_shard)
    attn.finish()
    ffn = Gather(links, ffn_shard)
    ffn.hops()

    tokens = token_blocks if seqs == 1 else [joined(token_blocks)]
    tokens_pair = [links.swap_core(t) for t in tokens]

    full_attn, qkv = project(
        links.me, attn.plan, attn.pieces, attn.rows, chips, tokens, qkv_bias
    )
    ffn.hops()
    context, lse, partial = attend_forward(qkv, rows, full_attn, parts)
    partial = list(partial)
    cotangent_blocks[-1], partial[-1] = tie(cotangent_blocks[-1], partial[-1])
    partial[0] = ffn.land(partial[0])
    sums = links.sum_blocks(partial, range(parts)[::-1], tied=False)
    ffn.hops()
    sums[0] = (sums[0][0], ffn.land(sums[0][1]))
    ffn.finish()

    weights = None
    units, scales, normed_low, activated, slopes, partial = [], [], [], [], [], []
    for tok, (own, got) in zip(token_blocks, sums):
        weights, (unit, low, act, act_give, slope, scale, part) = ffn_forward(
            links.me, ffn, weights, chips, tok, own, got, b_output, gain_first, shift_first, b_expand
        )
        units.append(unit)
        scales.append(scale)
        normed_low.append(low)
        activated.append((act, act_give))
        slopes.append(slope)
        partial.append(part)

    sums = links.sum_blocks(partial, range(parts), tied=False)
    context_pair = links.give_half(context)
    got, context_pair = tie(sums[-1][1], context_pair)
    sums[-1] = (sums[-1][0], got)
    vectors = jnp.stack([gain_first, shift_first, b_reduce, gain_second, shift_second])
    grad_mixed, reduce_in, expand_low, partial = ([None] * parts for _ in range(4))
    grad_b_expand, small = 0.0, {}
    for j in range(parts)[::-1]:
        own, got = sums[j]
        out, grad, low, wide, wide_give, part, sums_mixed, sums_wide = ffn_backward(
            links.me, ffn, weights, chips, units[j], own, got, cotangent_blocks[j], slopes[j], vectors
        )
        if j == 0:
            result = out.reshape(seqs, span, width)
            small["second"] = sums_mixed
        grad_b_expand = grad_b_expand + sums_wide[0]
        grad_mixed[j], reduce_in[j], expand_low[j], partial[j] = (
            grad, low, (wide, wide_give), part,
        )

    def cut_cores(wide, narrow):
        return [(w, n, False, 0) for w, (n, _) in zip(wide, narrow)] + [
            (links.swap_core(w), links.swap_core(n), False, 0)
            for w, (_, n) in zip(wide, narrow)
        ]

    def both_cores(wide, narrow):
        return [(w, n, True, 0) for w, n in zip(wide, narrow)] + [
            (links.swap_core(w), links.give_half(n), False, 0) for w, n in zip(wide, narrow)
        ]

    def rows_of(wide, narrow, pair):
        return [(w, narrow, True, j) for j, w in enumerate(wide)] + [
            (w, pair, False, j) for j, w in enumerate([links.swap_core(w) for w in wide])
        ]

    sums = links.sum_blocks(partial, range(parts)[::-1])
    grad_attended, attn_low, grad_context = [], [], []

    def first(j):
        grad, low, grad_ctx, sums_first = first_backward(
            grad_mixed[j], *sums[j], units[j], scales[j], gain_first, full_attn
        )
        if j == 0:
            small["first"] = sums_first
        grad_attended.append(grad)
        attn_low.append(low)
        grad_context.append(grad_ctx)

    first(0)
    early = links.sum_small(jnp.concatenate([small["second"], small["first"]]), "tensor")
    terms = [cut_cores(reduce_in, activated), cut_cores(normed_low, expand_low)]
    wide, grad_context[0] = tie(terms[0][0][0], grad_context[0])
    terms[0][0] = (wide, *terms[0][0][1:])
    blocks = pair_grads(links.me, chips, terms)
    last = sums[parts - 1]
    blocks, early, got = tie(blocks, early, last[1])
    sums[parts - 1] = (last[0], got)
    ffn_sum = Scatter(links, blocks)
    ffn_sum.hops()
    for j in range(1, parts):
        first(j)
    grad_context[-1] = ffn_sum.land(grad_context[-1])
    ffn_sum.hops()
    grad_qkv, bias_sums, give, back_low = attend_backward(
        links.me, qkv, rows, lse, full_attn, grad_context
    )
    grad_qkv, bias_sums = ffn_sum.land(grad_qkv, bias_sums)
    vector = jnp.concatenate([early.reshape(-1), grad_b_expand, bias_sums]).reshape(-1, 128)
    vector = links.sum_near(vector)
    ffn_sum.hops()
    pair = links.give_half(grad_qkv) if give is None else links.swap_core(give)
    if seqs == 1:
        context_terms = rows_of(attn_low, context, context_pair)
        qkv_terms = [(t, grad_qkv, True, j) for j, t in enumerate(tokens)] + [
            (t, pair, False, j) for j, t in enumerate(tokens_pair)
        ]
    else:
        context_terms = both_cores(attn_low, split(context))
        qkv_terms = [
            (tokens[0], grad_qkv, True, 0),
            (tokens_pair[0], pair, False, 0),
        ]
    blocks = pair_grads(links.me, chips, [qkv_terms, context_terms])
    blocks, vector = ffn_sum.land(blocks, vector)
    attn_sum = Scatter(links, blocks)
    attn_sum.hops()
    ffn_sum.finish()
    vector = links.sum_far(vector)
    back_low[-1] = attn_sum.land(back_low[-1])
    attn_sum.hops()
    grad_inputs = grad_attended[0] + links.scatter_blocks(back_low)
    vector = attn_sum.land(vector)
    attn_sum.hops()
    grad_inputs = attn_sum.land(grad_inputs)
    attn_sum.finish()
    vector = vector.reshape(-1)
    mine, got = links.swap_halves(ffn_sum.total())
    half_hidden, half_local = hidden // 2, local // 2
    grad_reduce = links.in_order(mine[:, :half_hidden], got[:, :half_hidden])
    grad_expand = links.in_order(mine[:, half_hidden:], got[:, half_hidden:])
    total = attn_sum.total()
    if local % 256 == 0:
        grad_wq, grad_wk, grad_wv, grad_output = unpack(
            links.me, total, links.get_rows(total)
        )
    else:
        mine, got = links.swap_halves(total)
        grad_wq, grad_wk, grad_wv = from_pair_major(
            links.in_order(mine[:, : 3 * half_local], got[:, : 3 * half_local])
        )
        grad_output = links.in_order(mine[:, 3 * half_local :], got[:, 3 * half_local :])

    early = vector[: 6 * width].reshape(6, width)
    middle = vector[6 * width : 6 * width + hidden]
    grad_bq, _, grad_bv = from_pair_major(vector[6 * width + hidden :])
    return (
        result,
        grad_inputs.reshape(seqs, span, width),
        grad_wq,
        grad_wk,
        grad_wv,
        grad_output.T,
        grad_expand,
        grad_reduce.T,
        grad_bq,
        grad_bv,
        early[5],
        middle,
        early[2],
        early[3],
        early[4],
        early[0],
        early[1],
    )


def solution(mesh):
    return jax.shard_map(
        shards,
        mesh=mesh,
        in_specs=(
            P("dp", "tensor", None),
            P("dp", None),
            P("dp", "tensor"),
            P("dp", "tensor"),
            P("dp", "tensor"),
            P("tensor", "dp"),
            P("dp", "tensor"),
            P("tensor", "dp"),
            P("tensor"),
            P("tensor"),
            P(),
            P("tensor"),
            P(),
            P(),
            P(),
            P(),
            P(),
            P("dp", "tensor", None),
        ),
        out_specs=(
            P("dp", "tensor", None),
            P("dp", "tensor", None),
            P("dp", "tensor"),
            P("dp", "tensor"),
            P("dp", "tensor"),
            P("tensor", "dp"),
            P("dp", "tensor"),
            P("tensor", "dp"),
            P("tensor"),
            P("tensor"),
            P(),
            P("tensor"),
            P(),
            P(),
            P(),
            P(),
            P(),
        ),
        check_vma=False,
    )
```

```python
import functools

import jax
import jax.numpy as jnp
from jax import lax
from jax.experimental import pallas as pl
from jax.experimental.pallas import tpu as pltpu
from jax.sharding import PartitionSpec as P

HD = 64
NORM_EPS = 1e-05
MASKED = -1e30
BF = jnp.bfloat16
F32 = jnp.float32
PARAMS = pltpu.CompilerParams(vmem_limit_bytes=60 << 20)
VMEM = pl.BlockSpec(memory_space=pltpu.VMEM)
SMEM = pl.BlockSpec(memory_space=pltpu.SMEM)
ANY = pl.BlockSpec(memory_space=pltpu.HBM)


def dot(a, b):
    return lax.dot_general(a, b, (((1,), (0,)), ((), ())), preferred_element_type=F32)


def dot_nt(a, b):
    return lax.dot_general(a, b, (((1,), (1,)), ((), ())), preferred_element_type=F32)


def dot_tn(a, b):
    return lax.dot_general(a, b, (((0,), (0,)), ((), ())), preferred_element_type=F32)


def cost(flops, nbytes):
    return pl.CostEstimate(flops=flops // 1024, bytes_accessed=nbytes // 1024, transcendentals=0)


def lane_half(array, head):
    lanes = lax.broadcasted_iota(jnp.int32, array.shape, 1)
    return jnp.where((lanes < HD) == (head == 0), array, jnp.zeros_like(array))


def column_of(row):
    return jnp.broadcast_to(row, (128, row.shape[1])).T[:, :1]


def attend_forward_kernel(parts, qkv_ref, row_ref, out_w_ref, *refs):
    ctx_ref, lse_ref, part_refs, scratch = refs[0], refs[1], refs[2 : 2 + parts], refs[-1]
    query, key, value = (qkv_ref[:, i * 128 : (i + 1) * 128] for i in range(3))
    same = column_of(row_ref[0]) == row_ref[0]
    query = query * jnp.asarray(HD**-0.5, BF)
    value_t = value.T
    out = []
    for head in range(2):
        scores = dot_nt(key, lane_half(query, head))
        scores = jnp.where(same, scores, MASKED)
        top = jnp.max(scores, axis=0, keepdims=True)
        weights = jnp.exp(scores - top)
        total = jnp.sum(weights, axis=0, keepdims=True)
        probs = (weights * (1.0 / total)).astype(BF)
        lse_ref[0, head : head + 1, :] = top + jnp.log(total)
        out.append(dot(value_t[head * HD : (head + 1) * HD], probs))
    context = jnp.concatenate(out, axis=0).T.astype(BF)
    ctx_ref[...] = context
    pair, pairs = pl.program_id(1), pl.num_programs(1)
    scratch[pair] = context

    @pl.when(pair == pairs - 1)
    def _():
        span = part_refs[0].shape[0]
        whole = jnp.concatenate([scratch[i] for i in range(scratch.shape[0])], axis=1)
        for j, part_ref in enumerate(part_refs):
            part_ref[...] = dot_nt(whole[j * span : (j + 1) * span], out_w_ref[...]).astype(BF)


def attend_forward(qkv, rows, full_attn, parts):
    seqs, _, length = rows.shape
    pairs = qkv.shape[1] // 384
    local, width, span = 128 * pairs, full_attn.shape[0], length // parts
    out = pl.pallas_call(
        functools.partial(attend_forward_kernel, parts),
        grid=(seqs, pairs),
        in_specs=[
            pl.BlockSpec((length, 384), lambda s, p: (s, p)),
            pl.BlockSpec((1, 1, length), lambda s, p: (s, 0, 0)),
            pl.BlockSpec((width, local), lambda s, p: (0, 3)),
        ],
        out_specs=[
            pl.BlockSpec((length, 128), lambda s, p: (s, p)),
            pl.BlockSpec((1, 2, length), lambda s, p: (s * pairs + p, 0, 0)),
        ]
        + [pl.BlockSpec((span, width), lambda s, p: (s, 0))] * parts,
        out_shape=[
            jax.ShapeDtypeStruct((seqs * length, local), BF),
            jax.ShapeDtypeStruct((seqs * pairs, 2, length), F32),
        ]
        + [jax.ShapeDtypeStruct((seqs * span, width), BF)] * parts,
        scratch_shapes=[pltpu.VMEM((pairs, length, 128), BF)],
        compiler_params=PARAMS,
        cost_estimate=cost(seqs * pairs * 24 * 128 * length * length, 8 << 20),
    )(qkv, rows, full_attn)
    return out[0], out[1], out[2:]


def attend_backward_body(qkv_ref, row_ref, lse_ref, w_ref, parts, *refs):
    out_ref, sum_ref = refs[parts : parts + 2]
    query, key, value = (qkv_ref[:, i * 128 : (i + 1) * 128] for i in range(3))
    grad_ctx = jnp.concatenate([ref[...] for ref in refs[:parts]], axis=0)
    same = column_of(row_ref[0]) == row_ref[0]
    small_query = query * jnp.asarray(HD**-0.5, BF)
    key_t = key.T
    grad_q, grad_k, grad_v = [], [], []
    for head in range(2):
        scores = dot_nt(key, lane_half(small_query, head))
        probs = jnp.exp(jnp.where(same, scores, MASKED) - lse_ref[0, head : head + 1, :])
        grad_probs = dot_nt(value, lane_half(grad_ctx, head))
        inner = jnp.sum(probs * grad_probs, axis=0, keepdims=True)
        grad_scores = (probs * (grad_probs - inner)).astype(BF)
        grad_q.append(dot(key_t[head * HD : (head + 1) * HD], grad_scores))
        grad_k.append(dot(grad_scores, query))
        grad_v.append(dot(probs.astype(BF), grad_ctx))
    lanes = lax.broadcasted_iota(jnp.int32, grad_k[0].shape, 1) < HD
    factor = HD**-0.5
    outs = (
        jnp.concatenate(grad_q, axis=0).T * factor,
        jnp.where(lanes, grad_k[0], grad_k[1]) * factor,
        jnp.where(lanes, grad_v[0], grad_v[1]),
    )
    for i, value in enumerate(outs):
        low = value.astype(BF)
        out_ref[:, i * 128 : (i + 1) * 128] = low
        sum_ref[0, :, i * 128 : (i + 1) * 128] = jnp.sum(
            low.astype(F32), axis=0, keepdims=True
        )


def attend_backward_kernel(parts, halved, me_ref, qkv_ref, row_ref, lse_ref, w_ref, *refs):
    attend_backward_body(qkv_ref, row_ref, lse_ref, w_ref, parts, *refs)
    out_ref, back_refs, total = refs[parts], refs[parts + 2 : 2 * parts + 2], refs[-1]
    pair, pairs = pl.program_id(1), pl.num_programs(1)
    part = dot_nt(out_ref[...], w_ref[...])

    @pl.when(pair == 0)
    def _():
        total[...] = part

    @pl.when(pair != 0)
    def _():
        total[...] += part

    @pl.when(pair == pairs - 1)
    def _():
        span = back_refs[0].shape[0]
        for j, ref in enumerate(back_refs):
            ref[...] = total[j * span : (j + 1) * span, :].astype(ref.dtype)

    if halved:
        give_ref = refs[2 * parts + 2]

        @pl.when(pair // (pairs // 2) == 1 - me_ref[0] % 2)
        def _():
            give_ref[...] = out_ref[...]


def attend_backward(me, qkv, rows, lse, full_attn, grad_ctx):
    seqs, _, length = rows.shape
    pairs = qkv.shape[1] // 384
    half = pairs // 2
    parts = len(grad_ctx)
    span, width = length // parts, full_attn.shape[0]
    kernel = functools.partial(attend_backward_kernel, parts, half > 0)

    def give_place(s, p, m):
        return s, jnp.clip(p - half * (1 - m[0] % 2), 0, max(half - 1, 0))

    out = pl.pallas_call(
        kernel,
        grid_spec=pltpu.PrefetchScalarGridSpec(
            num_scalar_prefetch=1,
            grid=(seqs, pairs),
            in_specs=[
                pl.BlockSpec((length, 384), lambda s, p, m: (s, p)),
                pl.BlockSpec((1, 1, length), lambda s, p, m: (s, 0, 0)),
                pl.BlockSpec((1, 2, length), lambda s, p, m: (s * pairs + p, 0, 0)),
                pl.BlockSpec((width, 384), lambda s, p, m: (0, p)),
            ]
            + [
                pl.BlockSpec((length // len(grad_ctx), 128), lambda s, p, m: (s, p))
                for _ in grad_ctx
            ],
            out_specs=[
                pl.BlockSpec((length, 384), lambda s, p, m: (s, p)),
                pl.BlockSpec((1, 1, 384), lambda s, p, m: (s, 0, p)),
            ]
            + [pl.BlockSpec((span, width), lambda s, p, m: (s, 0))] * parts
            + ([pl.BlockSpec((length, 384), give_place)] if half else []),
            scratch_shapes=[pltpu.VMEM((length, width), F32)],
        ),
        out_shape=[
            jax.ShapeDtypeStruct(qkv.shape, BF),
            jax.ShapeDtypeStruct((seqs, 1, qkv.shape[1]), F32),
        ]
        + [jax.ShapeDtypeStruct((seqs * span, width), BF if j else F32) for j in range(parts)]
        + ([jax.ShapeDtypeStruct((qkv.shape[0], 384 * half), BF)] if half else []),
        compiler_params=PARAMS,
        cost_estimate=cost(seqs * pairs * 40 * 128 * length * length, 8 << 20),
    )(me, qkv, rows, lse, full_attn, *grad_ctx)
    bias = jnp.sum(out[1], axis=(0, 1))
    return out[0], bias, out[-1] if half else None, list(out[2 : 2 + parts])


def ring_chip(place, chips):
    return jnp.where(place < chips // 2, 2 * place, 2 * (chips - 1 - place) + 1)


def ring_place(chip, chips):
    return jnp.where(chip % 2 == 0, chip // 2, chips - 1 - chip // 2)


def chip_at(me, distance, chips):
    return ring_chip((ring_place(me // 2, chips) + distance + chips) % chips, chips)


def gathered_rows(me, plan, rows, chips):
    out = []
    for distance, other, row in plan:
        core = me % 2
        owner = 2 * chip_at(me, distance, chips) + (1 - core if other else core)
        out.append(pl.multiple_of(owner * rows + row, 16))
    return out


def place_pieces(me, plan, rows, chips, pieces, out, sem):
    copies = [
        pltpu.make_async_copy(piece, out.at[pl.ds(row, piece.shape[0]), :], sem.at[i])
        for i, (piece, row) in enumerate(
            zip(pieces, gathered_rows(me, plan, rows, chips))
        )
    ]
    for copy in copies:
        copy.start()
    for copy in copies:
        copy.wait()


def assemble_kernel(plan, rows, chips, me_ref, *refs):
    pieces, out, sem = refs[: len(plan)], refs[-2], refs[-1]
    place_pieces(me_ref[0], plan, rows, chips, pieces, out, sem)


def assemble(me, plan, pieces, rows, chips):
    cols = pieces[0].shape[1]
    return pl.pallas_call(
        functools.partial(assemble_kernel, plan, rows, chips),
        out_shape=jax.ShapeDtypeStruct((2 * chips * rows, cols), BF),
        in_specs=[SMEM] + [ANY] * len(plan),
        out_specs=VMEM,
        scratch_shapes=[pltpu.SemaphoreType.DMA((len(plan),))],
        compiler_params=PARAMS,
        cost_estimate=cost(0, 8 * chips * rows * cols),
    )(me, *pieces)


def project_kernel(plan, rows, chips, parts, me_ref, bias_ref, *refs):
    blocks, pieces = refs[:parts], refs[parts : parts + len(plan)]
    full_out, out, full, sem, out_sem = refs[parts + len(plan) :]
    place_pieces(me_ref[0], plan, rows, chips, pieces, full, sem)
    copy = pltpu.make_async_copy(full, full_out, out_sem)
    copy.start()
    cols = out.shape[1]
    count = blocks[0].shape[0]
    for i, block in enumerate(blocks):
        for start in range(0, cols, 384):
            out[i * count : (i + 1) * count, start : start + 384] = (
                dot(block[...], full[:, start : start + 384])
                + bias_ref[:, start : start + 384]
            ).astype(BF)
    copy.wait()


def project(me, plan, pieces, rows, chips, blocks, bias):
    cols, wide = pieces[0].shape[1], bias.shape[1]
    count, width = blocks[0].shape
    tokens = count * len(blocks)
    return pl.pallas_call(
        functools.partial(project_kernel, plan, rows, chips, len(blocks)),
        out_shape=[
            jax.ShapeDtypeStruct((width, cols), BF),
            jax.ShapeDtypeStruct((tokens, wide), BF),
        ],
        in_specs=[SMEM, VMEM] + [VMEM] * len(blocks) + [ANY] * len(plan),
        out_specs=[ANY, VMEM],
        scratch_shapes=[
            pltpu.VMEM((width, cols), BF),
            pltpu.SemaphoreType.DMA((len(plan),)),
            pltpu.SemaphoreType.DMA,
        ],
        compiler_params=PARAMS,
        cost_estimate=cost(2 * tokens * width * wide, 8 * width * cols),
    )(me, bias, *blocks, *pieces)


def grad_kernel(chips, sources, terms, me_ref, *refs):
    out, far_up, far_down, scratch = refs[-4:]
    d = 2 * pl.program_id(0)
    rows = out.shape[1]
    k = 0
    for col, term in zip(terms, sources):
        total = None
        for _ in range(term):
            pair = jnp.concatenate([refs[k][...], refs[k + 1][...]], axis=1)
            product = dot_tn(pair, refs[k + 2][...])
            total = product if total is None else total + product
            k += 3
        cols = slice(col, col + total.shape[1])
        if total.shape[0] == 2 * rows:
            out[0, :, cols] = total[:rows].astype(BF)
            out[1, :, cols] = total[rows:].astype(BF)
        else:
            lanes = total.shape[0] // 2
            scratch[:, cols] = total
            for i in range(2):
                off = lanes * i + (chip_at(me_ref[0], d + i, chips) * rows) % lanes
                out[i, :, cols] = scratch[pl.ds(pl.multiple_of(off, 32), rows), cols].astype(BF)

    @pl.when(d == chips // 4 * 2)
    def _():
        block = out[chips // 2 % 2]
        far_up[...] = block[: rows // 2]
        far_down[...] = block[rows // 2 :]


def pair_grads(me, chips, terms):
    width = terms[0][0][0].shape[1]
    rows = width // chips
    lanes = max(rows, 128)
    specs, arrays, cols, sources, start, flops = [], [], [], [], 0, 0
    for term in terms:
        cols.append(start)
        sources.append(len(term))
        for wide, narrow, both, row in term:
            count, most = wide.shape[0], narrow.shape[1]
            half = most // 2 if both else most
            if both and half % 128:
                narrow = lax.dynamic_slice_in_dim(narrow, half * (me[0] % 2), half, 1)
                both = False
            specs += [
                pl.BlockSpec(
                    (count, lanes),
                    lambda d, m, i=i: (0, chip_at(m[0], 2 * d + i, chips) * rows // lanes),
                )
                for i in range(2)
            ] + [
                pl.BlockSpec(
                    (count, half),
                    lambda d, m, both=both, row=row: (row, m[0] % 2 if both else 0),
                ),
            ]
            arrays += [wide, wide, narrow]
            flops += 2 * count * width * half
        start += half
    return pl.pallas_call(
        functools.partial(grad_kernel, chips, sources, cols),
        grid_spec=pltpu.PrefetchScalarGridSpec(
            num_scalar_prefetch=1,
            grid=(chips // 2,),
            in_specs=specs,
            out_specs=[pl.BlockSpec((2, rows, start), lambda d, m: (d, 0, 0))]
            + [pl.BlockSpec((rows // 2, start), lambda d, m: (0, 0))] * 2,
            scratch_shapes=[pltpu.VMEM((2 * lanes, start if lanes > rows else 128), F32)],
        ),
        out_shape=[jax.ShapeDtypeStruct((chips, rows, start), BF)]
        + [jax.ShapeDtypeStruct((rows // 2, start), BF)] * 2,
        compiler_params=PARAMS,
        cost_estimate=cost(flops, 8 << 20),
    )(me, *arrays)


def start_all(pairs, sem):
    copies = [
        pltpu.make_async_copy(source, target, sem.at[i])
        for i, (source, target) in enumerate(pairs)
    ]
    for copy in copies:
        copy.start()
    return copies


def wait_all(copies):
    for copy in copies:
        copy.wait()


def start_weights(me, plan, rows, chips, sources, which, out, sem):
    wide = out.shape[1]
    if plan is None:
        half = wide // 2
        return [
            start_all(
                [(sources[which].at[:, k : k + half], out.at[:, k : k + half])],
                sem.at[pl.ds(k // half, 1)],
            )
            for k in (0, half)
        ]
    return [
        start_all(
            [
                (
                    piece.at[:, which * wide : (which + 1) * wide],
                    out.at[pl.ds(row, piece.shape[0]), :],
                )
                for piece, row in zip(sources, gathered_rows(me, plan, rows, chips))
            ],
            sem,
        )
    ]


def halves(me, kept, own, give):
    wide = own.shape[1]
    core = me % 2
    return [
        (kept.at[:, pl.ds(pl.multiple_of(wide * core, 128), wide)], own),
        (kept.at[:, pl.ds(pl.multiple_of(wide * (1 - core), 128), wide)], give),
    ]


def ffn_forward_kernel(plan, rows, chips, me_ref, bias_o, gain, shift, bias_e, *refs):
    count = 2 if plan is None else len(plan)
    ins, pieces, refs = refs[:3], refs[3 : 3 + count], refs[3 + count :]
    unit_out, low_out, own_out, give_out, slope_out = refs[:5]
    kept_out, refs = ((), refs) if plan is None else (refs[5:7], refs[2:])
    scale_out, part_out, refs = refs[5], refs[6], refs[7:]
    (
        tok, own, got, expand, reduce, unit_keep, low_keep, act_keep, slope_keep,
        sem, expand_sem, reduce_sem, out_sem,
    ) = refs
    me = me_ref[0]
    hidden = act_keep.shape[1]
    loads = start_all(zip(ins, (tok, own, got)), sem)
    expand_loads = start_weights(me, plan, rows, chips, pieces, 0, expand, expand_sem)
    reduce_loads = start_weights(me, plan, rows, chips, pieces, 1, reduce, reduce_sem)
    wait_all(loads)
    normed, unit, scale = ln_forward(
        tok[...].astype(F32) + (own[...].astype(F32) + got[...].astype(F32)) + bias_o[...],
        gain[...],
        shift[...],
    )
    scale_out[...] = scale
    unit_keep[...] = unit
    low_keep[...] = normed.astype(BF)
    copies = start_all([(unit_keep, unit_out), (low_keep, low_out)], out_sem)
    parts = len(expand_loads)
    step = min(512, hidden // parts)
    for start in range(0, hidden, step):
        if start % (hidden // parts) == 0:
            wait_all(expand_loads[start * parts // hidden])
        cols = slice(start, start + step)
        act, slope = gelu_pair(dot(low_keep[...], expand[:, cols]) + bias_e[:, cols])
        act_keep[:, cols] = act.astype(BF)
        slope_keep[:, cols] = slope.astype(BF)
    copies += start_all(
        halves(me, act_keep, own_out, give_out) + [(slope_keep, slope_out)],
        out_sem.at[pl.ds(2, 3)],
    )
    for load in reduce_loads:
        wait_all(load)
    if kept_out:
        copies += start_all(
            zip((expand, reduce), kept_out), out_sem.at[pl.ds(5, 2)]
        )
    part_out[...] = dot_nt(act_keep[...], reduce[...]).astype(BF)
    wait_all(copies)


def ffn_weights(ring, weights):
    if weights is None:
        return ring.plan, ring.pieces
    return None, weights


def ffn_scratch(sources, width, hidden):
    pieces = len(sources)
    return [pltpu.VMEM((width, hidden), BF)] * 2, [
        pltpu.SemaphoreType.DMA((pieces,)),
        pltpu.SemaphoreType.DMA((pieces,)),
    ]


def ffn_forward(me, ring, weights, chips, tok, own, got, bias_o, gain, shift, bias_e):
    count, width = tok.shape
    hidden = bias_e.shape[0]
    plan, sources = ffn_weights(ring, weights)
    scratch, sems = ffn_scratch(sources, width, hidden)
    kept = [] if weights else [jax.ShapeDtypeStruct((width, hidden), BF)] * 2
    out = pl.pallas_call(
        functools.partial(ffn_forward_kernel, plan, ring.rows, chips),
        out_shape=[
            jax.ShapeDtypeStruct((count, width), F32),
            jax.ShapeDtypeStruct((count, width), BF),
            jax.ShapeDtypeStruct((count, hidden // 2), BF),
            jax.ShapeDtypeStruct((count, hidden // 2), BF),
            jax.ShapeDtypeStruct((count, hidden), BF),
        ]
        + kept
        + [
            jax.ShapeDtypeStruct((count, 1), F32),
            jax.ShapeDtypeStruct((count, width), BF),
        ],
        in_specs=[SMEM] + [VMEM] * 4 + [ANY] * (3 + len(sources)),
        out_specs=[ANY] * (5 + len(kept)) + [VMEM] * 2,
        scratch_shapes=[pltpu.VMEM((count, width), BF)] * 3
        + scratch
        + [
            pltpu.VMEM((count, width), F32),
            pltpu.VMEM((count, width), BF),
            pltpu.VMEM((count, hidden), BF),
            pltpu.VMEM((count, hidden), BF),
            pltpu.SemaphoreType.DMA((3,)),
        ]
        + sems
        + [pltpu.SemaphoreType.DMA((5 + len(kept),))],
        compiler_params=PARAMS,
        cost_estimate=cost(8 * count * width * hidden, 16 << 20),
    )(me, bias_o[None], gain[None], shift[None], bias_e[None], tok, own, got, *sources)
    return weights or out[5:7], (*out[:5], *out[5 + len(kept) :])


def ffn_backward_kernel(plan, rows, chips, me_ref, vec_ref, *refs):
    count = 2 if plan is None else len(plan)
    ins, pieces = refs[:5], refs[5 : 5 + count]
    result_out, grad_out, low_out, own_out, give_out, part_out, sum_out, wide_out = refs[
        5 + count : 13 + count
    ]
    (
        unit_ref, own, got, cot_ref, slope, expand, reduce,
        result_keep, grad_keep, low_keep, wide_keep,
        sem, expand_sem, reduce_sem, out_sem,
    ) = refs[13 + count :]
    me = me_ref[0]
    hidden = wide_keep.shape[1]
    loads = start_all(zip(ins, (unit_ref, own, got, cot_ref, slope)), sem)
    reduce_loads = start_weights(me, plan, rows, chips, pieces, 1, reduce, reduce_sem)
    expand_loads = start_weights(me, plan, rows, chips, pieces, 0, expand, expand_sem)
    gain_first, shift_first, bias_r, gain, shift = (vec_ref[i : i + 1, :] for i in range(5))
    wait_all(loads)
    mixed = (
        unit_ref[...] * gain_first
        + shift_first
        + (own[...].astype(F32) + got[...].astype(F32))
        + bias_r
    )
    out, unit, scale = ln_forward(mixed, gain, shift)
    cot = cot_ref[...].astype(F32)
    grad = ln_backward(cot, unit, scale, gain)
    result_keep[...] = out.astype(BF)
    grad_keep[...] = grad
    low_keep[...] = grad.astype(BF)
    copies = start_all(
        [(result_keep, result_out), (grad_keep, grad_out), (low_keep, low_out)], out_sem
    )
    for i, value in enumerate((cot * unit, cot, grad)):
        sum_out[i : i + 1, :] = jnp.sum(value, axis=0, keepdims=True)
    parts = len(reduce_loads)
    step = min(512, hidden // parts)
    for start in range(0, hidden, step):
        if start % (hidden // parts) == 0:
            wait_all(reduce_loads[start * parts // hidden])
        cols = slice(start, start + step)
        low = (dot(low_keep[...], reduce[:, cols]) * slope[:, cols].astype(F32)).astype(BF)
        wide_keep[:, cols] = low
        wide_out[:, cols] = jnp.sum(low.astype(F32), axis=0, keepdims=True)
    copies += start_all(halves(me, wide_keep, own_out, give_out), out_sem.at[pl.ds(3, 2)])
    for load in expand_loads:
        wait_all(load)
    part_out[...] = dot_nt(wide_keep[...], expand[...]).astype(BF)
    wait_all(copies)


def ffn_backward(me, ring, weights, chips, unit, own, got, cot, slope, vectors):
    count, width = unit.shape
    hidden = slope.shape[1]
    plan, sources = ffn_weights(ring, weights)
    scratch, sems = ffn_scratch(sources, width, hidden)
    block = pltpu.VMEM((count, width), BF)
    wide = pltpu.VMEM((count, hidden), BF)
    return pl.pallas_call(
        functools.partial(ffn_backward_kernel, plan, ring.rows, chips),
        out_shape=[
            jax.ShapeDtypeStruct((count, width), BF),
            jax.ShapeDtypeStruct((count, width), F32),
            jax.ShapeDtypeStruct((count, width), BF),
            jax.ShapeDtypeStruct((count, hidden // 2), BF),
            jax.ShapeDtypeStruct((count, hidden // 2), BF),
            jax.ShapeDtypeStruct((count, width), BF),
            jax.ShapeDtypeStruct((3, width), F32),
            jax.ShapeDtypeStruct((1, hidden), F32),
        ],
        in_specs=[SMEM, VMEM] + [ANY] * (5 + len(sources)),
        out_specs=[ANY] * 5 + [VMEM] * 3,
        scratch_shapes=[pltpu.VMEM((count, width), F32), block, block, block, wide]
        + scratch
        + [
            block,
            pltpu.VMEM((count, width), F32),
            block,
            wide,
            pltpu.SemaphoreType.DMA((5,)),
        ]
        + sems
        + [pltpu.SemaphoreType.DMA((5,))],
        compiler_params=PARAMS,
        cost_estimate=cost(8 * count * width * hidden, 16 << 20),
    )(me, vectors, unit, own, got, cot, slope, *sources)


def first_backward_kernel(
    mixed_ref, own_ref, got_ref, unit_ref, scale_ref, gain_ref, out_w_ref, *refs
):
    grad_out, low_out, ctx_out, sum_out = refs
    grad_normed = mixed_ref[...] + (own_ref[...].astype(F32) + got_ref[...].astype(F32))
    unit = unit_ref[...]
    grad = ln_backward(grad_normed, unit, scale_ref[...], gain_ref[...])
    low = grad.astype(BF)
    grad_out[...] = grad
    low_out[...] = low
    ctx_out[...] = dot(low, out_w_ref[...]).astype(BF)
    for i, value in enumerate((grad_normed * unit, grad_normed, grad)):
        sum_out[i : i + 1, :] = jnp.sum(value, axis=0, keepdims=True)


def first_backward(mixed, own, got, unit, scale, gain, full_attn):
    count, width = unit.shape
    local = full_attn.shape[1] // 4

    def whole(*shape):
        return pl.BlockSpec(shape, lambda i: (0, 0))

    return pl.pallas_call(
        first_backward_kernel,
        grid=(1,),
        out_shape=[
            jax.ShapeDtypeStruct((count, width), F32),
            jax.ShapeDtypeStruct((count, width), BF),
            jax.ShapeDtypeStruct((count, local), BF),
            jax.ShapeDtypeStruct((3, width), F32),
        ],
        in_specs=[whole(count, width)] * 4
        + [whole(count, 1), whole(1, width), pl.BlockSpec((width, local), lambda i: (0, 3))],
        out_specs=[whole(count, width)] * 2 + [whole(count, local), whole(3, width)],
        compiler_params=PARAMS,
        cost_estimate=cost(2 * count * width * local, 6 << 20),
    )(mixed, own, got, unit, scale, gain[None], full_attn)


def unpack_kernel(me_ref, total_ref, got_ref, q_out, k_out, v_out, o_out):
    rows, half = got_ref.shape
    own = total_ref[pl.ds(pl.multiple_of(rows * (me_ref[0] % 2), rows), rows), :]
    wide = half * 3 // 4
    first = me_ref[0] % 2 == 0
    outs = (q_out, k_out, v_out)
    for part in range(2):
        mine, got = own, got_ref[...].astype(F32)
        block = jnp.where(first, mine, got) if part == 0 else jnp.where(first, got, mine)
        for col in range(0, wide, 128):
            pair, which = divmod(part * wide + col, 384)
            outs[which // 128][:, 128 * pair : 128 * (pair + 1)] = block[:, col : col + 128]
        o_out[:, part * (half - wide) : (part + 1) * (half - wide)] = block[:, wide:]


def unpack(me, total, got):
    rows, half = got.shape
    return pl.pallas_call(
        unpack_kernel,
        out_shape=[jax.ShapeDtypeStruct((rows, half // 2), F32)] * 4,
        in_specs=[SMEM, VMEM, VMEM],
        out_specs=[VMEM] * 4,
        compiler_params=PARAMS,
        cost_estimate=cost(0, 12 * rows * half),
    )(me, total, got)


def pack_kernel(q_ref, k_ref, v_ref, o_ref, out_ref):
    local = q_ref.shape[1]
    for pair in range(local // 128):
        for i, ref in enumerate((q_ref, k_ref, v_ref)):
            col = 384 * pair + 128 * i
            out_ref[:, col : col + 128] = ref[:, 128 * pair : 128 * (pair + 1)]
    out_ref[:, 3 * local :] = o_ref[...]


def pack(w_query, w_key, w_value, w_output):
    rows, local = w_query.shape
    return pl.pallas_call(
        pack_kernel,
        out_shape=jax.ShapeDtypeStruct((rows, 4 * local), BF),
        in_specs=[VMEM] * 4,
        out_specs=VMEM,
        compiler_params=PARAMS,
    )(w_query, w_key, w_value, w_output)


def pair_major(parts):
    lead = parts[0].shape[:-1]
    stacked = jnp.stack([p.reshape(*lead, -1, 128) for p in parts], axis=-2)
    return stacked.reshape(*lead, -1)


def from_pair_major(array):
    lead = array.shape[:-1]
    stacked = array.reshape(*lead, -1, 3, 128)
    return [stacked[..., i, :].reshape(*lead, -1) for i in range(3)]


def tie(*arrays):
    return lax.optimization_barrier(arrays)


def ln_forward(values, gain, shift):
    centre = values - jnp.mean(values, axis=-1, keepdims=True)
    scale = lax.rsqrt(jnp.mean(centre * centre, axis=-1, keepdims=True) + NORM_EPS)
    unit = centre * scale
    return unit * gain + shift, unit, scale


def ln_backward(grad, unit, scale, gain):
    grad_unit = grad * gain
    along = jnp.mean(grad_unit * unit, axis=-1, keepdims=True)
    return scale * (grad_unit - jnp.mean(grad_unit, axis=-1, keepdims=True) - unit * along)


def ring_add_kernel(ahead_ref, behind_ref, up_ref, down_ref, up_out, down_out):
    rows = up_ref.shape[0]
    start = ahead_ref.shape[1] - rows
    for own, got, out, first in (
        (ahead_ref, up_ref, up_out, 0),
        (behind_ref, down_ref, down_out, start),
    ):
        total = own[0, first : first + rows].astype(F32) + got[...].astype(F32)
        out[first : first + rows, :] = total.astype(BF)
        if start:
            rest = slice(rows, None) if first == 0 else slice(0, start)
            out[rest, :] = own[0, rest]


def ring_add(blocks, step, up, down):
    chips, rows, cols = blocks.shape

    def whole(shape):
        return pl.BlockSpec(shape, lambda i: (0, 0))

    return pl.pallas_call(
        ring_add_kernel,
        grid=(1,),
        in_specs=[
            pl.BlockSpec((1, rows, cols), lambda i: (step, 0, 0)),
            pl.BlockSpec((1, rows, cols), lambda i: (chips - step, 0, 0)),
            whole(up.shape),
            whole(down.shape),
        ],
        out_specs=[whole((rows, cols))] * 2,
        out_shape=[jax.ShapeDtypeStruct((rows, cols), BF)] * 2,
        compiler_params=PARAMS,
        cost_estimate=cost(0, 10 * rows * cols),
    )(blocks, blocks, up, down)


class Links:
    def __init__(self):
        self.dp = lax.axis_size("dp")
        self.tensor = lax.axis_size("tensor")
        self.chips = self.dp // 2
        self.half_way = self.chips // 2
        self.order = list(range(0, self.chips, 2)) + list(range(1, self.chips, 2))[::-1]
        self.place = lax.axis_index("dp").astype(jnp.int32)
        self.core = self.place % 2
        self.me = self.place.reshape(1)

    def swap_core(self, array):
        return self.swap_dp(array, 1)

    def swap_dp(self, array, bit):
        return lax.ppermute(array, "dp", [(i, i ^ bit) for i in range(self.dp)])

    def swap_tensor(self, array, bit):
        return lax.ppermute(array, "tensor", [(i, i ^ bit) for i in range(self.tensor)])

    def along_ring(self, array, step):
        pairs = [
            (2 * self.order[i] + c, 2 * self.order[(i + step) % self.chips] + c)
            for i in range(self.chips)
            for c in range(2)
        ]
        return lax.ppermute(array, "dp", pairs)

    def bits(self, size):
        return [1 << b for b in range((size - 1).bit_length())]

    def gather_blocks(self, block):
        blocks = [block]
        for bit in self.bits(self.tensor):
            blocks = blocks + [self.swap_tensor(b, bit) for b in blocks]
        return blocks

    def sum_blocks(self, blocks, order, tied=True):
        if self.tensor == 2:
            blocks, got = list(blocks), [None, None]
            first, second = order
            got[second] = self.swap_tensor(blocks[first], 1)
            if tied:
                blocks[second], got[second] = tie(blocks[second], got[second])
            got[first] = self.swap_tensor(blocks[second], 1)
            return list(zip(blocks, got))
        for bit in self.bits(self.tensor):
            low = [b.astype(BF) for b in blocks]
            got = [self.swap_tensor(low[j ^ bit], bit) for j in range(len(low))]
            blocks = [a.astype(F32) + b.astype(F32) for a, b in zip(low, got)]
        return list(zip(low, got))

    def scatter_blocks(self, blocks):
        for bit in self.bits(self.tensor)[::-1]:
            got = [self.swap_tensor(blocks[j + bit].astype(BF), bit) for j in range(bit)]
            blocks = [blocks[j].astype(F32) + got[j].astype(F32) for j in range(bit)]
        return blocks[0]

    def sum_small(self, vector, axis):
        rows = vector.reshape(-1, 128)
        swap, size = (
            (self.swap_tensor, self.tensor) if axis == "tensor" else (self.swap_dp, self.dp)
        )
        for bit in self.bits(size):
            rows = rows + swap(rows, bit)
        return rows.reshape(vector.shape)

    def sum_near(self, rows):
        for bit in self.bits(self.dp)[:2]:
            rows = rows + self.swap_dp(rows, bit)
        return rows

    def sum_far(self, rows):
        far = [rows] + [self.swap_dp(rows, bit) for bit in range(4, self.dp, 4)]
        while len(far) > 1:
            far = [a + b for a, b in zip(far[::2], far[1::2])]
        return far[0]

    def own_half(self, array):
        half = array.shape[1] // 2
        return lax.dynamic_slice_in_dim(array, half * self.core, half, 1)

    def give_half(self, array):
        half = array.shape[1] // 2
        return self.swap_core(
            lax.dynamic_slice_in_dim(array, half * (1 - self.core), half, 1)
        )

    def swap_halves(self, total):
        rows = total.shape[0] // 2
        mine = lax.dynamic_slice_in_dim(total, rows * self.core, rows, 0)
        return mine, self.get_rows(total).astype(F32)

    def get_rows(self, total):
        rows = total.shape[0] // 2
        other = lax.dynamic_slice_in_dim(total, rows * (1 - self.core), rows, 0)
        return self.swap_core(other.astype(BF))

    def in_order(self, mine, got):
        first = self.core == 0
        return jnp.concatenate(
            [jnp.where(first, mine, got), jnp.where(first, got, mine)], axis=1
        )


class Gather:
    def __init__(self, links, shard):
        self.links = links
        self.rows = shard.shape[0]
        self.up = self.down = shard
        self.plan, self.pieces, self.step = [], [], 0
        self.arrive(shard, 0, 0)

    def arrive(self, block, distance, row):
        self.plan += [(distance, 0, row), (distance, 1, row)]
        self.pieces += [block, self.links.swap_core(block)]

    def hops(self):
        for _ in range(max(1, self.links.half_way // 4)):
            self.hop()

    def finish(self):
        while self.step < self.links.half_way:
            self.hop()

    def hop(self):
        if self.step == self.links.half_way:
            return
        self.step += 1
        half, last = self.rows // 2, self.step == self.links.half_way
        up, down = (self.up[:half], self.down[half:]) if last else (self.up, self.down)
        self.up = self.links.along_ring(up, 1)
        self.down = self.links.along_ring(down, -1)
        self.arrive(self.up, -self.step, 0)
        self.arrive(self.down, self.step, half if last else 0)

    def land(self, *arrays):
        out = tie(self.up, self.down, *arrays)
        self.up, self.down = out[:2]
        if self.step:
            self.pieces[-2], self.pieces[-4] = self.down, self.up
        return out[2:] if len(arrays) > 1 else out[2]

    def full(self):
        return assemble(self.links.me, self.plan, self.pieces, self.rows, self.links.chips)


class Scatter:
    def __init__(self, links, blocks, up, down):
        self.links, self.blocks, self.step = links, blocks, links.half_way
        self.arrived = None
        self.rows = blocks.shape[1]
        self.up, self.down = up, down

    def hops(self):
        for _ in range(max(1, self.links.half_way // 4)):
            self.hop()

    def finish(self):
        while self.step:
            self.hop()

    def hop(self):
        if not self.step:
            return
        links = self.links
        self.ready()
        up, down = links.along_ring(self.up, 1), links.along_ring(self.down, -1)
        self.step -= 1
        if self.step:
            self.arrived, self.up, self.down = (up, down), None, None
        else:
            self.up, self.down = up, down

    def ready(self):
        if self.up is None:
            self.up, self.down = ring_add(self.blocks, self.step, *self.arrived)

    def land(self, *arrays):
        moving = self.arrived if self.up is None else (self.up, self.down)
        out = tie(*moving, *arrays)
        if self.up is None:
            self.arrived = out[:2]
        else:
            self.up, self.down = out[:2]
        return out[2:] if len(arrays) > 1 else out[2]

    def total(self):
        self.finish()
        return self.blocks[0].astype(F32) + self.up.astype(F32) + self.down.astype(F32)


def add(a, b):
    return (a.astype(F32) + b.astype(F32)).astype(BF)


def gelu_pair(u):
    cdf = 0.5 * (1.0 + lax.erf(u * (0.5**0.5)))
    slope = cdf + u * jnp.exp(-0.5 * u * u) * 0.3989422804014327
    return u * cdf, slope


def shards(
    inputs,
    segments,
    w_query,
    w_key,
    w_value,
    w_output,
    w_expand,
    w_reduce,
    query_bias_vector,
    b_value,
    b_output,
    b_expand,
    b_reduce,
    gain_first,
    shift_first,
    gain_second,
    shift_second,
    cotangent,
):
    links = Links()
    parts = links.tensor
    rank = lax.axis_index("tensor")
    seqs, span, width = inputs.shape
    local = w_query.shape[1]
    hidden = w_expand.shape[1]
    length = span * parts
    chips = links.chips

    def flat(block):
        return block.reshape(seqs * span, block.shape[-1])

    def joined(blocks):
        return jnp.concatenate(
            [b.reshape(seqs, span, b.shape[-1]) for b in blocks], axis=1
        ).reshape(seqs * length, -1)

    def split(array):
        array = array.reshape(seqs, length, -1)
        return [flat(array[:, j * span : (j + 1) * span]) for j in range(parts)]

    attn = Gather(links, pack(w_query, w_key, w_value, w_output.T))
    attn.hops()
    token_blocks = [flat(b) for b in links.gather_blocks(inputs)]
    labels = jnp.concatenate(
        [
            lax.dynamic_slice_in_dim(segments, span * (rank ^ j), span, 1)
            for j in range(parts)
        ],
        axis=1,
    )
    rows = labels[:, None, :]
    qkv_bias = pair_major([query_bias_vector, jnp.zeros_like(b_value), b_value])[None]
    token_blocks[-1], rows, qkv_bias = attn.land(token_blocks[-1], rows, qkv_bias)
    attn.hops()
    ffn_shard, cotangent, token_blocks[-1] = attn.land(
        jnp.concatenate([w_expand, w_reduce.T], axis=1), cotangent, token_blocks[-1]
    )
    attn.hops()
    cotangent_blocks = [flat(b) for b in links.gather_blocks(cotangent)]
    ffn_shard = attn.land(ffn_shard)
    attn.finish()
    ffn = Gather(links, ffn_shard)
    ffn.hops()

    tokens = token_blocks if seqs == 1 else [joined(token_blocks)]
    tokens_pair = [links.swap_core(t) for t in tokens]

    full_attn, qkv = project(
        links.me, attn.plan, attn.pieces, attn.rows, chips, tokens, qkv_bias
    )
    ffn.hops()
    context, lse, partial = attend_forward(qkv, rows, full_attn, parts)
    partial = list(partial)
    cotangent_blocks[-1], partial[-1] = tie(cotangent_blocks[-1], partial[-1])
    partial[0] = ffn.land(partial[0])
    sums = links.sum_blocks(partial, range(parts)[::-1], tied=False)
    ffn.hops()
    sums[0] = (sums[0][0], ffn.land(sums[0][1]))
    ffn.finish()

    weights = None
    units, scales, normed_low, activated, slopes, partial = [], [], [], [], [], []
    for tok, (own, got) in zip(token_blocks, sums):
        weights, (unit, low, act, act_give, slope, scale, part) = ffn_forward(
            links.me, ffn, weights, chips, tok, own, got, b_output, gain_first, shift_first, b_expand
        )
        units.append(unit)
        scales.append(scale)
        normed_low.append(low)
        activated.append((act, act_give))
        slopes.append(slope)
        partial.append(part)

    sums = links.sum_blocks(partial, range(parts), tied=False)
    context_pair = links.give_half(context)
    got, context_pair = tie(sums[-1][1], context_pair)
    sums[-1] = (sums[-1][0], got)
    vectors = jnp.stack([gain_first, shift_first, b_reduce, gain_second, shift_second])
    grad_mixed, reduce_in, expand_low, partial = ([None] * parts for _ in range(4))
    grad_b_expand, small = 0.0, {}
    for j in range(parts)[::-1]:
        own, got = sums[j]
        out, grad, low, wide, wide_give, part, sums_mixed, sums_wide = ffn_backward(
            links.me, ffn, weights, chips, units[j], own, got, cotangent_blocks[j], slopes[j], vectors
        )
        if j == 0:
            result = out.reshape(seqs, span, width)
            small["second"] = sums_mixed
        grad_b_expand = grad_b_expand + sums_wide[0]
        grad_mixed[j], reduce_in[j], expand_low[j], partial[j] = (
            grad, low, (wide, wide_give), part,
        )

    def cut_cores(wide, narrow):
        return [(w, n, False, 0) for w, (n, _) in zip(wide, narrow)] + [
            (links.swap_core(w), links.swap_core(n), False, 0)
            for w, (_, n) in zip(wide, narrow)
        ]

    def both_cores(wide, narrow):
        return [(w, n, True, 0) for w, n in zip(wide, narrow)] + [
            (links.swap_core(w), links.give_half(n), False, 0) for w, n in zip(wide, narrow)
        ]

    def rows_of(wide, narrow, pair):
        return [(w, narrow, True, j) for j, w in enumerate(wide)] + [
            (w, pair, False, j) for j, w in enumerate([links.swap_core(w) for w in wide])
        ]

    sums = links.sum_blocks(partial, range(parts)[::-1])
    grad_attended, attn_low, grad_context = [], [], []

    def first(j):
        grad, low, grad_ctx, sums_first = first_backward(
            grad_mixed[j], *sums[j], units[j], scales[j], gain_first, full_attn
        )
        if j == 0:
            small["first"] = sums_first
        grad_attended.append(grad)
        attn_low.append(low)
        grad_context.append(grad_ctx)

    first(0)
    early = links.sum_small(jnp.concatenate([small["second"], small["first"]]), "tensor")
    terms = [cut_cores(reduce_in, activated), cut_cores(normed_low, expand_low)]
    wide, grad_context[0] = tie(terms[0][0][0], grad_context[0])
    terms[0][0] = (wide, *terms[0][0][1:])
    blocks = pair_grads(links.me, chips, terms)
    last = sums[parts - 1]
    *blocks, early, got = tie(*blocks, early, last[1])
    sums[parts - 1] = (last[0], got)
    ffn_sum = Scatter(links, *blocks)
    ffn_sum.hops()
    for j in range(1, parts):
        first(j)
    grad_context[-1] = ffn_sum.land(grad_context[-1])
    ffn_sum.hops()
    grad_qkv, bias_sums, give, back_low = attend_backward(
        links.me, qkv, rows, lse, full_attn, grad_context
    )
    grad_qkv, bias_sums = ffn_sum.land(grad_qkv, bias_sums)
    vector = jnp.concatenate([early.reshape(-1), grad_b_expand, bias_sums]).reshape(-1, 128)
    vector = links.sum_near(vector)
    ffn_sum.hops()
    pair = links.give_half(grad_qkv) if give is None else links.swap_core(give)
    if seqs == 1:
        context_terms = rows_of(attn_low, context, context_pair)
        qkv_terms = [(t, grad_qkv, True, j) for j, t in enumerate(tokens)] + [
            (t, pair, False, j) for j, t in enumerate(tokens_pair)
        ]
    else:
        context_terms = both_cores(attn_low, split(context))
        qkv_terms = [
            (tokens[0], grad_qkv, True, 0),
            (tokens_pair[0], pair, False, 0),
        ]
    blocks = pair_grads(links.me, chips, [qkv_terms, context_terms])
    *blocks, vector = ffn_sum.land(*blocks, vector)
    attn_sum = Scatter(links, *blocks)
    attn_sum.hops()
    ffn_sum.finish()
    vector = links.sum_far(vector)
    back_low[-1] = attn_sum.land(back_low[-1])
    attn_sum.hops()
    grad_inputs = grad_attended[0] + links.scatter_blocks(back_low)
    vector = attn_sum.land(vector)
    attn_sum.hops()
    grad_inputs = attn_sum.land(grad_inputs)
    attn_sum.finish()
    vector = vector.reshape(-1)
    mine, got = links.swap_halves(ffn_sum.total())
    half_hidden, half_local = hidden // 2, local // 2
    grad_reduce = links.in_order(mine[:, :half_hidden], got[:, :half_hidden])
    grad_expand = links.in_order(mine[:, half_hidden:], got[:, half_hidden:])
    total = attn_sum.total()
    if local % 256 == 0:
        grad_wq, grad_wk, grad_wv, grad_output = unpack(
            links.me, total, links.get_rows(total)
        )
    else:
        mine, got = links.swap_halves(total)
        grad_wq, grad_wk, grad_wv = from_pair_major(
            links.in_order(mine[:, : 3 * half_local], got[:, : 3 * half_local])
        )
        grad_output = links.in_order(mine[:, 3 * half_local :], got[:, 3 * half_local :])

    early = vector[: 6 * width].reshape(6, width)
    middle = vector[6 * width : 6 * width + hidden]
    grad_bq, _, grad_bv = from_pair_major(vector[6 * width + hidden :])
    return (
        result,
        grad_inputs.reshape(seqs, span, width),
        grad_wq,
        grad_wk,
        grad_wv,
        grad_output.T,
        grad_expand,
        grad_reduce.T,
        grad_bq,
        grad_bv,
        early[5],
        middle,
        early[2],
        early[3],
        early[4],
        early[0],
        early[1],
    )


def solution(mesh):
    return jax.shard_map(
        shards,
        mesh=mesh,
        in_specs=(
            P("dp", "tensor", None),
            P("dp", None),
            P("dp", "tensor"),
            P("dp", "tensor"),
            P("dp", "tensor"),
            P("tensor", "dp"),
            P("dp", "tensor"),
            P("tensor", "dp"),
            P("tensor"),
            P("tensor"),
            P(),
            P("tensor"),
            P(),
            P(),
            P(),
            P(),
            P(),
            P("dp", "tensor", None),
        ),
        out_specs=(
            P("dp", "tensor", None),
            P("dp", "tensor", None),
            P("dp", "tensor"),
            P("dp", "tensor"),
            P("dp", "tensor"),
            P("tensor", "dp"),
            P("dp", "tensor"),
            P("tensor", "dp"),
            P("tensor"),
            P("tensor"),
            P(),
            P("tensor"),
            P(),
            P(),
            P(),
            P(),
            P(),
        ),
        check_vma=False,
    )
```
